128 devices in a mesh: row: 16 (over y, x), col: 8 (over z, core).
Axes of the slice: x: 4, y: 4, z: 4, core: 2. Of those that a mesh axis runs over, the one named last changes fastest.
Arguments:
- phase_space: float32 [6, 131072], P(None, 'col'), may hold values from -6 to 6
- derivs: float32 [6, 131072], P(None, 'col'), may hold values from -6 to 6
- star_time: float32 [131072], P('col'), may hold values from -0.5 to 0
- masses: float32 [131072], P('col'), may hold values from 0.5 to 2
- active_index: int32 [2, 16, 1024], P(None, 'row'), may hold values from 0 to 131071, as said below
- active_count: int32 [2, 16], P(None, 'row'), may hold values from 1 to 1024, 8192 in all within a row
Outputs:
- new_phase: float32 [6, 131072], P(None, 'col')
- new_derivs: float32 [6, 131072], P(None, 'col')
- new_time: float32 [131072], P('col')
The draws below stay inside these ranges and needn't reach their ends.
Inputs may be any that keep to these rules, and one draw needn't show every extreme that they name: `active_index`: within each step all 16384 entries are different star numbers; entries past a row's count are valid numbers but not active. `active_count`: in each step the counts sum to 8192, and some row index of each step has exactly 1024.
All inputs are finite; a program needn't handle non-finite values. No bound on the sum of `active_count` on one device may be relied on, other than what follows from the above.
Results may differ from the reference program's by a relative error of at most 0.0001.
Values sent between devices are 32-bit elements; how exact they have to be, the bound alone decides.
A program may use at most 192 MiB of HBM per device.

```python
import math
import jax
import jax.numpy as jnp
import numpy as np
from jax import lax

CAP = 1024
ACTIVE = 8192
N_STARS = 131072
N_ROW = 16


def draw_active_index(key, part):
    key = jax.random.fold_in(key, 11)
    keys = jax.random.split(key, 2)
    lists = []
    for number in range(2):
        order = jax.random.permutation(keys[number], N_STARS)
        lists.append(order[:N_ROW * CAP].reshape(N_ROW, CAP))
    return jnp.stack(lists).astype(jnp.int32)


def block_levels(stream_key, shape, cuts, least, largest):
    factor_of = 1.0
    for dim, parts in cuts:
        steps = jax.random.uniform(jax.random.fold_in(jax.random.fold_in(stream_key, 6), dim), (parts,), jnp.float32, least / len(cuts), largest / len(cuts))
        factor_of = factor_of * jnp.repeat(jnp.exp(steps), shape[dim] // parts).reshape((-1,) + (1,) * (len(shape) - 1 - dim))
    return factor_of


def profile(amount, total, most, lean):
    weights = [(1 << 20) // math.isqrt(standing ** lean) + 1 for standing in range(2, amount + 1)]
    rest, holding = total - most - (amount - 1), [1] * (amount - 1)
    while rest > 0:
        free = [i for i in range(amount - 1) if holding[i] < most]
        pool, remaining = sum([weights[i] for i in free]), rest
        for i in free:
            extra = min(most - holding[i], max(1, remaining * weights[i] // pool), rest)
            holding[i] = holding[i] + extra
            rest = rest - extra
    return np.array([most] + holding)


def ragged_sizes(stream_key, number_of, total, reach, skew):
    if number_of == 2:
        one = jax.random.randint(stream_key, (), max(1, total - reach), min(reach, total - 1) + 1)
        return jnp.stack([one, total - one])
    tallies = jnp.asarray(profile(number_of, total, reach, skew), jnp.int32)
    pairs = (number_of - 1) // 2
    source_of, taker = tallies[1:1 + 2 * pairs:2], tallies[2:2 + 2 * pairs:2]
    margin = jnp.minimum(source_of - 1, reach - taker)
    moved = jax.random.randint(jax.random.fold_in(stream_key, 1), (pairs,), 0, 1 << 20) % (margin + 1)
    tallies = tallies.at[1:1 + 2 * pairs:2].set(source_of - moved).at[2:2 + 2 * pairs:2].set(taker + moved)
    return tallies[jax.random.permutation(jax.random.fold_in(stream_key, 2), number_of)]


def noise(own_key, shape, width, most, cuts=(), kind=jnp.bfloat16):
    values = jax.random.normal(own_key, shape, jnp.float32) * width
    if len(cuts) > 0:
        values = block_levels(own_key, shape, cuts, -0.22, 0.18) * values
    return jnp.clip(values, min=-most, max=most).astype(kind)


def setup_inputs(seed: int = 0) -> dict:
    key_list = jax.random.split(jax.random.key(seed), 7)
    return {
        "phase_space": noise(key_list[0], (6, N_STARS), 1.0, 6.0, ((1, 8),), jnp.float32),
        "derivs": noise(key_list[1], (6, N_STARS), 1.0, 6.0, ((1, 8),), jnp.float32),
        "star_time": jnp.clip(-0.5 + 0.5 * jax.random.uniform(key_list[2], (N_STARS,), jnp.float32) ** block_levels(key_list[2], (N_STARS,), ((0, 8),), -0.2, 0.2), -0.5, 0.0),
        "masses": jnp.clip(jnp.exp(math.log(2.0) - 1.3862944 * jax.random.uniform(key_list[3], (N_STARS,), jnp.float32) ** block_levels(key_list[3], (N_STARS,), ((0, 8),), -0.2, 0.2)), 0.5, 2.0),
        "active_index": draw_active_index(jax.random.fold_in(key_list[6], 71), 0),
        "active_count": jax.vmap(lambda own: ragged_sizes(own, N_ROW, ACTIVE, CAP, 2))(jax.random.split(key_list[5], 2)).reshape((2, N_ROW)).astype(jnp.int32),
    }


softening = 0.01
block_times = (0.125, 0.25)

def predict(state, time, now):
    delta = (now - time)[None, :]
    pos = state[0:3]
    vel = state[3:6]
    accel = state[6:9]
    jerks = state[9:12]
    pred_pos = pos + delta * (vel + delta * (accel / 2.0 + delta * jerks / 6.0))
    pred_vel = vel + delta * (accel + delta * jerks / 2.0)
    return jnp.concatenate([pred_pos, pred_vel], axis=0)

def pair_terms(i_pred, j_pred, j_mass):
    delta_x = j_pred[0:3, None, :] - i_pred[0:3, :, None]
    delta_v = j_pred[3:6, None, :] - i_pred[3:6, :, None]
    dist_sq = softening + lax.optimization_barrier(jnp.sum(delta_x * delta_x, axis=0))
    inverse = lax.rsqrt(dist_sq)
    inverse_sq = inverse * inverse
    weight = j_mass[None, :] * inverse * inverse_sq
    radial = 3.0 * lax.optimization_barrier(jnp.sum(delta_x * delta_v, axis=0)) * inverse_sq
    accel = lax.optimization_barrier(jnp.sum(weight[None] * delta_x, axis=-1))
    jerks = lax.optimization_barrier(jnp.sum(weight[None] * (delta_v - radial[None] * delta_x), axis=-1))
    return jnp.concatenate([accel, jerks], axis=0)

def correct(fetched, forces, now):
    pred_pos = fetched[0:3]
    pred_vel = fetched[3:6]
    old_acc = fetched[6:9]
    old_jerk = fetched[9:12]
    step_len = (now - fetched[12])[None, :]
    new_acc = forces[0:3]
    new_jerk = forces[3:6]
    change = old_acc - new_acc
    second = (-6.0 * change - step_len * (4.0 * old_jerk + 2.0 * new_jerk)) / (step_len * step_len)
    third = (12.0 * change + 6.0 * step_len * (old_jerk + new_jerk)) / (step_len * step_len * step_len)
    h_two = step_len * step_len
    h_three = h_two * step_len
    h_four = h_three * step_len
    h_five = h_four * step_len
    new_pos = pred_pos + h_four / 24.0 * second + h_five / 120.0 * third
    new_vel = pred_vel + h_three / 6.0 * second + h_four / 24.0 * third
    return jnp.concatenate([new_pos, new_vel, new_acc, new_jerk], axis=0)

def spread_list(all_lists, counts, first, length):
    ends = jnp.cumsum(counts)
    starts = ends - counts
    position = first + jnp.arange(length, dtype=jnp.int32)
    which = lax.optimization_barrier(jnp.sum((position[:, None] >= ends[None, :]).astype(jnp.int32), axis=1))
    picker = (which[:, None] == jnp.arange(counts.shape[0], dtype=jnp.int32)[None, :]).astype(jnp.int32)
    slot = position - lax.optimization_barrier(jnp.sum(picker * starts[None, :], axis=1))
    return all_lists[which, slot].astype(jnp.int32)

def reference(phase_space, derivs, star_time, masses, active_index, active_count):
    state = jnp.concatenate([phase_space, derivs], axis=0)
    time = star_time
    share = masses / N_STARS
    tile = min(64, ACTIVE)
    for step in range(2):
        now = block_times[step]
        pred = predict(state, time, now)
        chosen = spread_list(active_index[step], active_count[step], 0, ACTIVE)
        fetched = jnp.concatenate([pred[:, chosen], state[6:12][:, chosen], time[chosen][None, :]], axis=0)
        tiles = fetched[0:6].reshape(6, ACTIVE // tile, tile).transpose(1, 0, 2)
        forces = lax.map(lambda piece: pair_terms(piece, pred, share), tiles)
        forces = forces.transpose(1, 0, 2).reshape(6, ACTIVE)
        corrected = correct(fetched, forces, now)
        state = state.at[:, chosen].set(corrected)
        time = time.at[chosen].set(jnp.float32(now))
    return (state[0:6], state[6:12], time)
```

```python
import functools

import jax
import jax.numpy as jnp
from jax import lax
from jax.experimental import pallas as pl
from jax.experimental.pallas import tpu as pltpu
from jax.sharding import PartitionSpec as P

F32 = jnp.float32
BF16 = jnp.bfloat16
I32 = jnp.int32
softening = 0.01
block_times = (0.125, 0.25)
ROWS = 16
COLS = 8
CAP = 1024
PART = 512
LOCAL = 16384
BLOCKS = LOCAL // 128
N_STARS = ROWS * PART * 16
MESH = pl.DeviceIdType.MESH
ADDED = (((1,), (1,)), ((), ()))


def rows_of(first, last, width):
    return jnp.zeros((last - first, width), F32)


def in_vmem(n):
    return [pl.BlockSpec(memory_space=pltpu.VMEM)] * n


def params(**more):
    return pltpu.CompilerParams(vmem_limit_bytes=56 * 2**20, **more)


def greet(partners):
    barrier = pltpu.get_barrier_semaphore()
    for partner in partners:
        pl.semaphore_signal(barrier, inc=1, device_id=partner, device_id_type=MESH)
    pl.semaphore_wait(barrier, len(partners))


def partners_of(axis, size, place):
    return [(k, {axis: lax.rem(place + k, size)}) for k in range(1, size)]


def exchange(axis, size, place, source, landing, send_sem, recv_sem):
    copies = []
    for k, partner in partners_of(axis, size, place):
        copy = pltpu.make_async_remote_copy(
            src_ref=source,
            dst_ref=landing.at[place],
            send_sem=send_sem.at[k],
            recv_sem=recv_sem.at[place],
            device_id=partner,
            device_id_type=MESH,
        )
        copy.start()
        copies.append(copy)
    return copies


def arrived(axis, size, place, source, landing, send_sem, recv_sem):
    for k, partner in partners_of(axis, size, place):
        slot = lax.rem(place + k, size)
        pltpu.make_async_remote_copy(
            src_ref=source,
            dst_ref=landing.at[slot],
            send_sem=send_sem.at[k],
            recv_sem=recv_sem.at[slot],
            device_id=partner,
            device_id_type=MESH,
        ).wait_recv()


def lists_kernel(own_ref, all_ref, send_sem, recv_sem):
    place = lax.axis_index("row")
    greet([p for _, p in partners_of("row", ROWS, place)])
    copies = exchange("row", ROWS, place, own_ref, all_ref, send_sem, recv_sem)
    all_ref[pl.ds(place, 1)] = own_ref[...][None]
    arrived("row", ROWS, place, own_ref, all_ref, send_sem, recv_sem)
    for copy in copies:
        copy.wait_send()


def gather_lists(own):
    return pl.pallas_call(
        lists_kernel,
        out_shape=jax.ShapeDtypeStruct((ROWS,) + own.shape, own.dtype),
        in_specs=in_vmem(1),
        out_specs=in_vmem(1)[0],
        scratch_shapes=[pltpu.SemaphoreType.DMA((ROWS,)), pltpu.SemaphoreType.DMA((ROWS,))],
        compiler_params=params(collective_id=0, has_side_effects=True),
        name="gather_lists",
    )(own)


def lane_pick(table, lanes):
    return jnp.take_along_axis(table, lanes, axis=1, mode="promise_in_bounds")


def spread_hot(index_rows, count):
    kinds = lax.broadcasted_iota(I32, (count, 128), 0).astype(F32).astype(BF16)
    return jnp.broadcast_to(index_rows, (count, 128)).astype(BF16) == kinds


def scattered(high, low, first, second, high_count):
    left, right = [], []
    one, zero = jnp.ones((), BF16), jnp.zeros((), BF16)
    for k in range(8):
        at_high = spread_hot(high[k : k + 1], high_count)
        at_low = spread_hot(low[k : k + 1], 128)
        left.append(jnp.where(at_high, one, zero))
        a = jnp.broadcast_to(first[k : k + 1], (128, 128)).astype(BF16)
        b = jnp.broadcast_to(second[k : k + 1], (128, 128)).astype(BF16)
        right.append(jnp.concatenate([jnp.where(at_low, a, zero), jnp.where(at_low, b, zero)], axis=0))
    return lax.dot_general(
        jnp.concatenate(left, axis=1), jnp.concatenate(right, axis=1), ADDED, preferred_element_type=F32
    )


def maps_kernel(
    place_ref, lists_ref, phase_ref, derivs_ref, time_ref,
    picks_ref, near_ref, base_ref, order_ref, table, hot,
):
    place = place_ref[0]
    offset = place_ref[1] * LOCAL
    lane8 = lax.broadcasted_iota(I32, (8, 128), 1)
    sub8 = lax.broadcasted_iota(I32, (8, 128), 0)
    upper = sub8 < 4

    position = place * PART + lax.rem(sub8, 4) * 128 + lane8
    before = jnp.zeros((8, 128), I32)
    which = jnp.zeros((8, 128), I32)
    start = jnp.zeros((8, 128), I32)
    for r in range(ROWS):
        count = jnp.where(
            upper,
            jnp.broadcast_to(lists_ref[r, 16:17, :], (8, 128)),
            jnp.broadcast_to(lists_ref[r, 17:18, :], (8, 128)),
        )
        end = before + count
        passed = position >= end
        which = which + passed.astype(I32)
        start = jnp.where(passed, end, start)
        before = end
    flat = which * CAP + position - start
    flat_high, flat_low = flat >> 7, flat & 127

    def look(r, stars):
        for k in range(8):
            row = jnp.where(
                upper,
                jnp.broadcast_to(lists_ref[r, k : k + 1, :], (8, 128)),
                jnp.broadcast_to(lists_ref[r, 8 + k : 9 + k, :], (8, 128)),
            )
            stars = jnp.where(flat_high == r * 8 + k, lane_pick(row, flat_low), stars)
        return stars

    stars = lax.fori_loop(0, ROWS, look, jnp.zeros((8, 128), I32))

    tri_row = lax.broadcasted_iota(I32, (128, 128), 0)
    tri_lane = lax.broadcasted_iota(I32, (128, 128), 1)
    up_to = (tri_row <= tri_lane).astype(F32).astype(BF16)
    below = (tri_lane < tri_row).astype(F32).astype(BF16)
    slot = sub8 * 128 + lane8
    for step in range(2):
        hot[...] = jnp.zeros((128, 256), F32)

        def place_list(r, begin, step=step):
            count = jnp.broadcast_to(lists_ref[r, 16 + step : 17 + step, :], (8, 128))
            star = lists_ref[r, 8 * step : 8 * step + 8, :] - offset
            live = (slot < count) & (star >= 0) & (star < LOCAL)
            at = begin + slot
            high = jnp.where(live, star >> 7, 255).astype(F32)
            low = (star & 127).astype(F32)
            hot[...] += scattered(
                high, low, ((at >> 7) + 1).astype(F32), (at & 127).astype(F32), 128
            )
            return begin + count

        lax.fori_loop(0, ROWS, place_list, jnp.zeros((8, 128), I32))
        at_high, at_low = hot[:, 0:128], hot[:, 128:256]
        if step == 0:
            for b in range(BLOCKS):
                table[13:14, b * 128 : b * 128 + 128] = at_high[b : b + 1]
                table[14:15, b * 128 : b * 128 + 128] = at_low[b : b + 1]
        active = (at_high > 0.0).astype(F32)
        so_far = jnp.dot(active.astype(BF16), up_to, preferred_element_type=F32)
        total = jnp.broadcast_to(so_far[:, 127:128], (128, 128))
        first = jnp.dot(below, total.astype(BF16), preferred_element_type=F32)
        rank = (first + so_far - active).astype(I32)
        base = first.astype(I32) >> 7
        near_ref[step] = jnp.where(active > 0.0, rank - base * 128 + 1, 0)
        base_ref[step, 0:128, :] = base
        base_ref[step, 128:129, :] = (first + total).astype(I32)[127:128]
        rank_high = jnp.where(active > 0.0, rank >> 7, 255).astype(F32)
        rank_low = (rank & 127).astype(F32)
        near_ref[2 + step] = rank_high.astype(I32)
        near_ref[4 + step] = rank_low.astype(I32)

        def place_rank(g, found, step=step):
            rows = pl.ds(pl.multiple_of(g * 8, 8), 8)
            return found + scattered(
                near_ref[2 + step, rows, :].astype(F32),
                near_ref[4 + step, rows, :].astype(F32),
                hot[rows, 0:128],
                hot[rows, 128:256],
                64,
            )

        found = lax.fori_loop(0, 16, place_rank, jnp.zeros((64, 256), F32))
        order_ref[step, 0] = found[:, 0:128]
        order_ref[step, 1] = found[:, 128:256]

    table[0:6, :] = phase_ref[...]
    table[6:12, :] = derivs_ref[...]
    table[12:13, :] = time_ref[...]
    table[15:16, :] = jnp.zeros((1, LOCAL), F32)
    local = stars - offset
    highs = [jnp.broadcast_to((local >> 7)[s : s + 1], (8, 128)) for s in range(8)]
    lows = [jnp.broadcast_to((local & 127)[s : s + 1], (8, 128)) for s in range(8)]

    def fetch(b, found):
        block = pl.ds(pl.multiple_of(b * 128, 128), 128)
        upper_half, lower_half = table[0:8, block], table[8:16, block]
        result = []
        for s in range(8):
            here = highs[s] == b
            result.append(jnp.where(here, lane_pick(upper_half, lows[s]), found[2 * s]))
            result.append(jnp.where(here, lane_pick(lower_half, lows[s]), found[2 * s + 1]))
        return tuple(result)

    found = lax.fori_loop(0, BLOCKS, fetch, tuple(jnp.zeros((8, 128), F32) for _ in range(16)))
    for s in range(8):
        picks_ref[0:8, s * 128 : s * 128 + 128] = found[2 * s]
        picks_ref[8:16, s * 128 : s * 128 + 128] = found[2 * s + 1]


def make_maps(place, lists, phase, derivs, time):
    return pl.pallas_call(
        maps_kernel,
        out_shape=[
            jax.ShapeDtypeStruct((16, 2 * PART), F32),
            jax.ShapeDtypeStruct((6, 128, 128), I32),
            jax.ShapeDtypeStruct((2, 136, 128), I32),
            jax.ShapeDtypeStruct((2, 2, 64, 128), F32),
        ],
        in_specs=[pl.BlockSpec(memory_space=pltpu.SMEM)] + in_vmem(4),
        out_specs=in_vmem(4),
        scratch_shapes=[pltpu.VMEM((16, LOCAL), F32), pltpu.VMEM((128, 256), F32)],
        compiler_params=params(),
        name="make_maps",
    )(place, lists, phase, derivs, time)


def picks_kernel(own_ref, sum_ref, landing, send_sem, recv_sem):
    place = lax.axis_index("col")
    greet([p for _, p in partners_of("col", COLS, place)])
    copies = exchange("col", COLS, place, own_ref, landing, send_sem, recv_sem)
    landing[pl.ds(place, 1)] = own_ref[...][None]
    arrived("col", COLS, place, own_ref, landing, send_sem, recv_sem)
    total = landing[0]
    for c in range(1, COLS):
        total = total + landing[c]
    sum_ref[...] = total
    for copy in copies:
        copy.wait_send()


def sum_picks(picks):
    return pl.pallas_call(
        picks_kernel,
        out_shape=jax.ShapeDtypeStruct(picks.shape, F32),
        in_specs=in_vmem(1),
        out_specs=in_vmem(1)[0],
        scratch_shapes=[
            pltpu.VMEM((COLS,) + picks.shape, F32),
            pltpu.SemaphoreType.DMA((COLS,)),
            pltpu.SemaphoreType.DMA((COLS,)),
        ],
        compiler_params=params(collective_id=1, has_side_effects=True),
        name="sum_picks",
    )(picks)


def predict(phase, derivs, time, now):
    d = now - time
    x, v, a, j = phase[0:3], phase[3:6], derivs[0:3], derivs[3:6]
    return x + d * (v + d * (a / 2.0 + d * j / 6.0)), v + d * (a + d * j / 2.0)


def correct(old, forces, now):
    x, v = predict(old[0:6], old[6:12], old[12:13], now)
    old_acc, old_jerk = old[6:9], old[9:12]
    h = now - old[12:13]
    new_acc, new_jerk = forces[0:3], forces[3:6]
    change = old_acc - new_acc
    second = (-6.0 * change - h * (4.0 * old_jerk + 2.0 * new_jerk)) / (h * h)
    third = (12.0 * change + 6.0 * h * (old_jerk + new_jerk)) / (h * h * h)
    h2 = h * h
    h3 = h2 * h
    h4 = h3 * h
    h5 = h4 * h
    x = x + h4 / 24.0 * second + h5 / 120.0 * third
    v = v + h3 / 6.0 * second + h4 / 24.0 * third
    return x, v, new_acc, new_jerk


def correct_kernel(now, own_ref, old_ref, all_ref, landing, mine, send_sem, recv_sem, send_row, recv_row):
    col, row = lax.axis_index("col"), lax.axis_index("row")
    greet(
        [p for _, p in partners_of("col", COLS, col)] + [p for _, p in partners_of("row", ROWS, row)]
    )
    copies = exchange("col", COLS, col, own_ref, landing, send_sem, recv_sem)
    landing[pl.ds(col, 1)] = own_ref[...][None]
    arrived("col", COLS, col, own_ref, landing, send_sem, recv_sem)
    total = landing[0]
    for c in range(1, COLS):
        total = total + landing[c]
    x, v, a, j = correct(old_ref[...], total, now)
    blank = jnp.zeros((2, PART), F32)
    mine[...] = jnp.concatenate([x, v, blank, a, j, blank], axis=0)
    copies += exchange("row", ROWS, row, mine, all_ref, send_row, recv_row)
    all_ref[pl.ds(row, 1)] = mine[...][None]
    arrived("row", ROWS, row, mine, all_ref, send_row, recv_row)
    for copy in copies:
        copy.wait_send()


def correct_all(partial_forces, old, step):
    return pl.pallas_call(
        functools.partial(correct_kernel, block_times[step]),
        out_shape=jax.ShapeDtypeStruct((ROWS, 16, PART), F32),
        in_specs=in_vmem(2),
        out_specs=in_vmem(1)[0],
        scratch_shapes=[
            pltpu.VMEM((COLS, 8, PART), F32),
            pltpu.VMEM((16, PART), F32),
            pltpu.SemaphoreType.DMA((COLS,)),
            pltpu.SemaphoreType.DMA((COLS,)),
            pltpu.SemaphoreType.DMA((ROWS,)),
            pltpu.SemaphoreType.DMA((ROWS,)),
        ],
        compiler_params=params(collective_id=2 + step, has_side_effects=True),
        name=f"correct_all_{step}",
    )(partial_forces, old)


PAIRS = ((0, 0), (0, 1), (0, 2), (1, 0), (1, 1), (2, 0))


def split3(x):
    high = x.astype(BF16).astype(F32)
    rest = x - high
    middle = rest.astype(BF16).astype(F32)
    return high, middle, rest - middle


def split2(x):
    high = x.astype(BF16)
    return high, (x - high.astype(F32)).astype(BF16)


def squares(x, v):
    xx = x * x
    xv = x * v
    return xx[0:1] + xx[1:2] + xx[2:3], xv[0:1] + xv[1:2] + xv[2:3]


def star_features(x, v):
    width = x.shape[1]
    parts = split3(jnp.concatenate([x, v, jnp.zeros((2, width), F32)], axis=0))
    xx, xv = squares(x, v)
    one = jnp.ones((3, width), F32)
    extra = jnp.concatenate(list(split3(xx)) + list(split3(xv)) + [one, one, rows_of(12, 16, width)], axis=0)
    return jnp.concatenate([parts[a] for a, _ in PAIRS] + [extra], axis=0)


def active_features(x, v):
    width = x.shape[1]
    xp, vp = split3(x), split3(v)
    xx, xv = squares(x, v)
    one, none3, none5 = jnp.ones((3, width), F32), rows_of(0, 3, width), rows_of(0, 5, width)
    dist, both = [], []
    for _, b in PAIRS:
        dist += [-2.0 * xp[b], none5]
        both += [-vp[b], -xp[b], rows_of(0, 2, width)]
    dist += [one, none3] + list(split3(xx + softening)) + [none3, rows_of(12, 16, width)]
    both += [none3, one, none3] + list(split3(xv)) + [rows_of(12, 16, width)]
    return jnp.concatenate(dist, axis=0).astype(BF16), jnp.concatenate(both, axis=0).astype(BF16)


def force_sums(x_own, v_own, pred_of, mass_ref, out_ref, weights, features):
    chunk = 2048

    def prepare(n, _):
        lanes = pl.ds(pl.multiple_of(n * chunk, chunk), chunk)
        x, v = pred_of(lanes)
        share = mass_ref[0:1, lanes] / N_STARS
        one = jnp.ones((1, chunk), F32)
        scaled = split3(jnp.concatenate([x, v, one, jnp.zeros((1, chunk), F32)], axis=0) * share)
        weights[:, lanes] = jnp.concatenate(list(scaled) + [rows_of(24, 32, chunk)], axis=0).astype(BF16)
        features[lanes, :] = star_features(x, v).T.astype(BF16)
        return 0

    lax.fori_loop(0, LOCAL // chunk, prepare, 0)
    dist_own, both_own = active_features(x_own, v_own)
    wide, deep = 256, 4096
    for half in range(PART // wide):
        cut = slice(half * wide, half * wide + wide)

        def sums(n, total, cut=cut):
            lanes = pl.ds(pl.multiple_of(n * deep, deep), deep)
            factor = features[lanes, :]
            dist = jnp.dot(factor, dist_own[:, cut], preferred_element_type=F32)
            both = jnp.dot(factor, both_own[:, cut], preferred_element_type=F32)
            inverse = lax.rsqrt(jnp.maximum(dist, softening))
            inverse_sq = inverse * inverse
            weight = inverse * inverse_sq
            radial = (weight * inverse_sq) * both
            w_high, w_low = split2(weight)
            u_high, u_low = split2(radial)
            factor = weights[:, lanes]
            dot = functools.partial(jnp.dot, factor, preferred_element_type=F32)
            return (total[0] + (dot(w_high) + dot(w_low)), total[1] + (dot(u_high) + dot(u_low)))

        nothing = jnp.zeros((32, wide), F32)
        w_sum, u_sum = lax.fori_loop(0, LOCAL // deep, sums, (nothing, nothing))
        w_sum = w_sum[0:8] + w_sum[8:16] + w_sum[16:24]
        u_sum = u_sum[0:8] + u_sum[8:16] + u_sum[16:24]
        x, v = x_own[:, cut], v_own[:, cut]
        acc = w_sum[0:3] - x * w_sum[6:7]
        jerk = w_sum[3:6] - v * w_sum[6:7] - 3.0 * (u_sum[0:3] - x * u_sum[6:7])
        out_ref[:, cut] = jnp.concatenate([acc, jerk, jnp.zeros((2, wide), F32)], axis=0)


def first_kernel(phase_ref, derivs_ref, time_ref, mass_ref, picks_ref, out_ref, weights, features):
    now = block_times[0]
    x_own, v_own = predict(picks_ref[0:6], picks_ref[6:12], picks_ref[12:13], now)

    def pred_of(lanes):
        return predict(phase_ref[:, lanes], derivs_ref[:, lanes], time_ref[:, lanes], now)

    force_sums(x_own, v_own, pred_of, mass_ref, out_ref, weights, features)


FORCE_SCRATCH = [pltpu.VMEM((32, LOCAL), BF16), pltpu.VMEM((LOCAL, 64), BF16)]


def first_forces(phase, derivs, time, masses, picks):
    return pl.pallas_call(
        first_kernel,
        out_shape=jax.ShapeDtypeStruct((8, PART), F32),
        in_specs=in_vmem(5),
        out_specs=in_vmem(1)[0],
        scratch_shapes=FORCE_SCRATCH,
        compiler_params=params(),
        name="first_forces",
    )(phase, derivs, time, masses, picks)


def update(step, now, base_ref, near_ref, order_ref, all_ref, state, sorted_ref):
    phase_in, derivs_in, time_in, phase_out, derivs_out, time_out = state
    count = base_ref[step, 128]

    def collect(n, _):
        high = jnp.broadcast_to(order_ref[step, 0, pl.ds(n, 1), :], (8, 128)).astype(I32) - 1
        low = jnp.broadcast_to(order_ref[step, 1, pl.ds(n, 1), :], (8, 128)).astype(I32)
        upper = jnp.zeros((8, 128), F32)
        lower = jnp.zeros((8, 128), F32)
        for b in range(64):
            here = high == b
            lanes = slice((b % 4) * 128, (b % 4) * 128 + 128)
            upper = jnp.where(here, lane_pick(all_ref[b // 4, 0:8, lanes], low), upper)
            lower = jnp.where(here, lane_pick(all_ref[b // 4, 8:16, lanes], low), lower)
        sorted_ref[n, 0:8, :] = upper
        sorted_ref[n, 8:16, :] = lower
        return 0

    lax.fori_loop(0, (count + 127) // 128, collect, 0)

    def put(b, _):
        lanes = pl.ds(pl.multiple_of(b * 128, 128), 128)
        n = jnp.minimum(base_ref[step, b], 63)
        m = jnp.minimum(n + 1, 63)
        at = jnp.broadcast_to(near_ref[step, pl.ds(b, 1), :], (8, 128)) - 1
        low = at & 127
        is_first = (at >= 0) & (at < 128)
        is_next = at >= 128

        def chosen(rows, old):
            new = jnp.where(is_first, lane_pick(sorted_ref[n, rows, :], low), old)
            return jnp.where(is_next, lane_pick(sorted_ref[m, rows, :], low), new)

        blank = jnp.zeros((2, 128), F32)
        phase_out[:, lanes] = chosen(slice(0, 8), jnp.concatenate([phase_in[:, lanes], blank], axis=0))[0:6]
        derivs_out[:, lanes] = chosen(slice(8, 16), jnp.concatenate([derivs_in[:, lanes], blank], axis=0))[0:6]
        time_out[:, lanes] = jnp.where(at[0:1] >= 0, now, time_in[:, lanes])
        return 0

    lax.fori_loop(0, BLOCKS, put, 0)


def second_kernel(
    base_ref, near_ref, order_ref, all_ref, phase_ref, derivs_ref, time_ref, mass_ref, picks_ref,
    out_ref, phase_out, derivs_out, time_out, fixed_ref, sorted_ref, weights, features,
):
    state = (phase_ref, derivs_ref, time_ref, phase_out, derivs_out, time_out)
    update(0, block_times[0], base_ref, near_ref, order_ref, all_ref, state, sorted_ref)
    for s in range(PART // 128):
        lanes = slice(s * 128, s * 128 + 128)
        high = jnp.broadcast_to(picks_ref[13:14, lanes], (8, 128)).astype(I32) - 1
        low = jnp.broadcast_to(picks_ref[14:15, lanes], (8, 128)).astype(I32)

        def look(r, found, high=high, low=low):
            upper, lower = found
            for k in range(4):
                here = high == r * 4 + k
                cut = slice(k * 128, k * 128 + 128)
                upper = jnp.where(here, lane_pick(all_ref[r, 0:8, cut], low), upper)
                lower = jnp.where(here, lane_pick(all_ref[r, 8:16, cut], low), lower)
            return upper, lower

        old = picks_ref[:, lanes]
        blank = jnp.zeros((2, 128), F32)
        upper, lower = lax.fori_loop(
            0,
            ROWS,
            look,
            (jnp.concatenate([old[0:6], blank], axis=0), jnp.concatenate([old[6:12], blank], axis=0)),
        )
        when = jnp.where(high[0:1] >= 0, block_times[0], old[12:13])
        fixed_ref[:, lanes] = jnp.concatenate([upper[0:6], lower[0:6], when, jnp.zeros((3, 128), F32)], axis=0)
    now = block_times[1]
    x_own, v_own = predict(fixed_ref[0:6], fixed_ref[6:12], fixed_ref[12:13], now)

    def pred_of(lanes):
        return predict(phase_out[:, lanes], derivs_out[:, lanes], time_out[:, lanes], now)

    force_sums(x_own, v_own, pred_of, mass_ref, out_ref, weights, features)


STATE_SHAPES = [
    jax.ShapeDtypeStruct((6, LOCAL), F32),
    jax.ShapeDtypeStruct((6, LOCAL), F32),
    jax.ShapeDtypeStruct((1, LOCAL), F32),
]


def second_forces(base, near, order, everyone, phase, derivs, time, masses, picks):
    return pl.pallas_call(
        second_kernel,
        out_shape=[jax.ShapeDtypeStruct((8, PART), F32)]
        + STATE_SHAPES
        + [jax.ShapeDtypeStruct((16, PART), F32)],
        in_specs=[pl.BlockSpec(memory_space=pltpu.SMEM)] + in_vmem(8),
        out_specs=in_vmem(5),
        scratch_shapes=[pltpu.VMEM((64, 16, 128), F32)] + FORCE_SCRATCH,
        compiler_params=params(),
        name="second_forces",
    )(base, near, order, everyone, phase, derivs, time, masses, picks)


def last_kernel(
    base_ref, near_ref, order_ref, all_ref, phase_ref, derivs_ref, time_ref,
    phase_out, derivs_out, time_out, sorted_ref,
):
    state = (phase_ref, derivs_ref, time_ref, phase_out, derivs_out, time_out)
    update(1, block_times[1], base_ref, near_ref, order_ref, all_ref, state, sorted_ref)


def last_update(base, near, order, everyone, phase, derivs, time):
    return pl.pallas_call(
        last_kernel,
        out_shape=STATE_SHAPES,
        in_specs=[pl.BlockSpec(memory_space=pltpu.SMEM)] + in_vmem(6),
        out_specs=in_vmem(3),
        scratch_shapes=[pltpu.VMEM((64, 16, 128), F32)],
        compiler_params=params(),
        name="last_update",
    )(base, near, order, everyone, phase, derivs, time)


def body(phase_space, derivs, star_time, masses, active_index, active_count):
    time = star_time.reshape(1, LOCAL)
    masses = masses.reshape(1, LOCAL)
    place = jnp.stack([lax.axis_index("row"), lax.axis_index("col")]).astype(I32)
    own = jnp.concatenate(
        [
            active_index.reshape(16, 128),
            jnp.broadcast_to(active_count.reshape(2, 1), (2, 128)),
            jnp.zeros((6, 128), I32),
        ],
        axis=0,
    )
    lists = gather_lists(own)
    picks, near, base, order = make_maps(place, lists, phase_space, derivs, time)
    picks = sum_picks(picks)
    base = base[:, :, 0]
    first, second = picks[:, 0:PART], picks[:, PART:]
    forces = first_forces(phase_space, derivs, time, masses, first)
    everyone = correct_all(forces, first, 0)
    forces, phase_space, derivs, time, old = second_forces(
        base, near, order, everyone, phase_space, derivs, time, masses, second
    )
    everyone = correct_all(forces, old, 1)
    phase_space, derivs, time = last_update(base, near, order, everyone, phase_space, derivs, time)
    return phase_space, derivs, time.reshape(LOCAL)


def solution(mesh):
    return jax.shard_map(
        body,
        mesh=mesh,
        in_specs=(
            P(None, "col"),
            P(None, "col"),
            P("col"),
            P("col"),
            P(None, "row", None),
            P(None, "row"),
        ),
        out_specs=(P(None, "col"), P(None, "col"), P("col")),
        check_vma=False,
    )
```

```python
import functools

import jax
import jax.numpy as jnp
from jax import lax
from jax.experimental import pallas as pl
from jax.experimental.pallas import tpu as pltpu
from jax.sharding import PartitionSpec as P

F32 = jnp.float32
BF16 = jnp.bfloat16
I32 = jnp.int32
softening = 0.01
block_times = (0.125, 0.25)
ROWS = 16
COLS = 8
CAP = 1024
PART = 512
LOCAL = 16384
BLOCKS = LOCAL // 128
N_STARS = ROWS * PART * 16
MESH = pl.DeviceIdType.MESH
ADDED = (((1,), (1,)), ((), ()))


def rows_of(first, last, width):
    return jnp.zeros((last - first, width), F32)


def in_vmem(n):
    return [pl.BlockSpec(memory_space=pltpu.VMEM)] * n


def params(**more):
    return pltpu.CompilerParams(vmem_limit_bytes=56 * 2**20, **more)


def greet(partners):
    barrier = pltpu.get_barrier_semaphore()
    for partner in partners:
        pl.semaphore_signal(barrier, inc=1, device_id=partner, device_id_type=MESH)
    pl.semaphore_wait(barrier, len(partners))


def partners_of(axis, size, place):
    return [(k, {axis: lax.rem(place + k, size)}) for k in range(1, size)]


def exchange(axis, size, place, source, landing, send_sem, recv_sem):
    copies = []
    for k, partner in partners_of(axis, size, place):
        copy = pltpu.make_async_remote_copy(
            src_ref=source,
            dst_ref=landing.at[place],
            send_sem=send_sem.at[k],
            recv_sem=recv_sem.at[place],
            device_id=partner,
            device_id_type=MESH,
        )
        copy.start()
        copies.append(copy)
    return copies


def arrived(axis, size, place, source, landing, send_sem, recv_sem):
    for k, partner in partners_of(axis, size, place):
        slot = lax.rem(place + k, size)
        pltpu.make_async_remote_copy(
            src_ref=source,
            dst_ref=landing.at[slot],
            send_sem=send_sem.at[k],
            recv_sem=recv_sem.at[slot],
            device_id=partner,
            device_id_type=MESH,
        ).wait_recv()


def lane_pick(table, lanes):
    return jnp.take_along_axis(table, lanes, axis=1, mode="promise_in_bounds")


def spread(row):
    return jnp.broadcast_to(row, (8, 128))


def hot(index_row, count):
    kinds = lax.broadcasted_iota(I32, (count, 128), 0).astype(F32).astype(BF16)
    return jnp.broadcast_to(index_row, (count, 128)).astype(BF16) == kinds


def scattered(entries, high_count):
    one, zero = jnp.ones((), BF16), jnp.zeros((), BF16)
    left, right = [], []
    for high, low, first, second in entries:
        left.append(jnp.where(hot(high, high_count), one, zero))
        at_low = hot(low, 128)
        a = jnp.broadcast_to(first, (128, 128)).astype(BF16)
        b = jnp.broadcast_to(second, (128, 128)).astype(BF16)
        right.append(jnp.concatenate([jnp.where(at_low, a, zero), jnp.where(at_low, b, zero)], axis=0))
    return lax.dot_general(
        jnp.concatenate(left, axis=1), jnp.concatenate(right, axis=1), ADDED, preferred_element_type=F32
    )


def place_map(lists_ref, step, offset):
    slot = lax.broadcasted_iota(I32, (8, 128), 0) * 128 + lax.broadcasted_iota(I32, (8, 128), 1)
    begin = jnp.zeros((8, 128), I32)
    entries = []
    for r in range(ROWS):
        count = spread(lists_ref[r, 16 + step : 17 + step, :])
        star = lists_ref[r, 8 * step : 8 * step + 8, :] - offset
        live = (slot < count) & (star >= 0) & (star < LOCAL)
        at = begin + slot
        high = jnp.where(live, star >> 7, 255).astype(F32)
        low = (star & 127).astype(F32)
        first, second = ((at >> 7) + 1).astype(F32), (at & 127).astype(F32)
        for k in range(8):
            cut = slice(k, k + 1)
            entries.append((high[cut], low[cut], first[cut], second[cut]))
        begin = begin + count
    return scattered(entries, 128)


def rank_map(places, near_ref, base_ref, order_ref, step):
    at_high, at_low = places[0], places[1]
    row = lax.broadcasted_iota(I32, (128, 128), 0)
    lane = lax.broadcasted_iota(I32, (128, 128), 1)
    up_to = (row <= lane).astype(F32).astype(BF16)
    before = (row < lane).astype(F32).astype(BF16)
    below = (lane < row).astype(F32).astype(BF16)
    active = (at_high > 0.0).astype(F32)
    active16 = active.astype(BF16)
    so_far = jnp.dot(active16, up_to, preferred_element_type=F32)
    total = jnp.broadcast_to(so_far[:, 127:128], (128, 128))
    first = jnp.dot(below, total.astype(BF16), preferred_element_type=F32)
    rank = (first + so_far - active).astype(I32)
    near_ref[step] = jnp.where(active > 0.0, rank - (first.astype(I32) >> 7) * 128 + 1, 0)
    ones = jnp.ones((8, 128), F32).astype(BF16)
    totals = lax.dot_general(ones, active16, ADDED, preferred_element_type=F32)
    firsts = jnp.dot(totals.astype(BF16), before, preferred_element_type=F32).astype(I32)
    base_ref[step, 0] = firsts >> 7
    base_ref[step, 1] = firsts + totals.astype(I32)
    rank_high = jnp.where(active > 0.0, rank >> 7, 255).astype(F32)
    rank_low = (rank & 127).astype(F32)
    entries = []
    for b in range(BLOCKS):
        cut = slice(b, b + 1)
        entries.append((rank_high[cut], rank_low[cut], at_high[cut], at_low[cut]))
    order_ref[step] = scattered(entries, 64)


def own_stars(lists_ref, place):
    lane = lax.broadcasted_iota(I32, (8, 128), 1)
    sub = lax.broadcasted_iota(I32, (8, 128), 0)
    position = place * PART + (sub & 3) * 128 + lane
    before = jnp.zeros((8, 128), I32)
    which = jnp.zeros((8, 128), I32)
    start = jnp.zeros((8, 128), I32)
    for r in range(ROWS):
        count = jnp.where(sub < 4, spread(lists_ref[r, 16:17, :]), spread(lists_ref[r, 17:18, :]))
        end = before + count
        passed = position >= end
        which = which + passed.astype(I32)
        start = jnp.where(passed, end, start)
        before = end
    flat = which * CAP + position - start
    high, low = flat >> 7, flat & 127
    stars = jnp.zeros((8, 128), I32)
    for r in range(ROWS):
        for k in range(8):
            row = jnp.where(
                sub < 4, spread(lists_ref[r, k : k + 1, :]), spread(lists_ref[r, 8 + k : 9 + k, :])
            )
            stars = jnp.where(high == r * 8 + k, lane_pick(row, low), stars)
    return stars


def both_halves(x, step):
    part = x[4 * step : 4 * step + 4]
    return jnp.concatenate([part, part], axis=0)


def fetch(stars, pairs):
    high, low = stars >> 7, stars & 127

    def look(g, found):
        for u in range(8):
            b = g * 8 + u
            here = high == b
            found = tuple(
                jnp.where(here, lane_pick(pair(b), low), old) for pair, old in zip(pairs, found)
            )
        return found

    return lax.fori_loop(0, BLOCKS // 8, look, tuple(jnp.zeros((8, 128), F32) for _ in pairs))


def two_rows(sub, a, b):
    return jnp.where(sub < 4, spread(a), spread(b))


def unpack(pairs, out_ref):
    for p, pair in enumerate(pairs):
        for half in range(2):
            for s in range(4):
                out_ref[2 * p + half : 2 * p + half + 1, s * 128 : s * 128 + 128] = pair[
                    4 * half + s : 4 * half + s + 1
                ]


def predict(phase, derivs, time, now):
    d = now - time
    x, v, a, j = phase[0:3], phase[3:6], derivs[0:3], derivs[3:6]
    return x + d * (v + d * (a / 2.0 + d * j / 6.0)), v + d * (a + d * j / 2.0)


def correct(old, forces, now):
    x, v = predict(old[0:6], old[6:12], old[12:13], now)
    old_acc, old_jerk = old[6:9], old[9:12]
    h = now - old[12:13]
    new_acc, new_jerk = forces[0:3], forces[3:6]
    change = old_acc - new_acc
    second = (-6.0 * change - h * (4.0 * old_jerk + 2.0 * new_jerk)) / (h * h)
    third = (12.0 * change + 6.0 * h * (old_jerk + new_jerk)) / (h * h * h)
    h2 = h * h
    h3 = h2 * h
    h4 = h3 * h
    h5 = h4 * h
    x = x + h4 / 24.0 * second + h5 / 120.0 * third
    v = v + h3 / 6.0 * second + h4 / 24.0 * third
    return x, v, new_acc, new_jerk


PAIRS = ((0, 0), (0, 1), (0, 2), (1, 0), (1, 1), (2, 0))


def split3(x):
    high = x.astype(BF16).astype(F32)
    rest = x - high
    middle = rest.astype(BF16).astype(F32)
    return high, middle, rest - middle


def split2(x):
    high = x.astype(BF16)
    return high, (x - high.astype(F32)).astype(BF16)


def squares(x, v):
    xx = x * x
    xv = x * v
    return xx[0:1] + xx[1:2] + xx[2:3], xv[0:1] + xv[1:2] + xv[2:3]


def star_features(x, v):
    width = x.shape[1]
    parts = split3(jnp.concatenate([x, v, jnp.zeros((2, width), F32)], axis=0))
    xx, xv = squares(x, v)
    one = jnp.ones((3, width), F32)
    extra = jnp.concatenate(list(split3(xx)) + list(split3(xv)) + [one, one, rows_of(12, 16, width)], axis=0)
    return jnp.concatenate([parts[a] for a, _ in PAIRS] + [extra], axis=0)


def active_features(x, v):
    width = x.shape[1]
    xp, vp = split3(x), split3(v)
    xx, xv = squares(x, v)
    one, none3, none5 = jnp.ones((3, width), F32), rows_of(0, 3, width), rows_of(0, 5, width)
    dist, both = [], []
    for _, b in PAIRS:
        dist += [-2.0 * xp[b], none5]
        both += [-vp[b], -xp[b], rows_of(0, 2, width)]
    dist += [one, none3] + list(split3(xx + softening)) + [none3, rows_of(12, 16, width)]
    both += [none3, one, none3] + list(split3(xv)) + [rows_of(12, 16, width)]
    return jnp.concatenate(dist, axis=0).astype(BF16), jnp.concatenate(both, axis=0).astype(BF16)


def prepare(first, chunk, count, pred_of, weights, features):
    def one_chunk(n, _):
        x, v, mass = pred_of(n)
        at = pl.ds(pl.multiple_of(first + n * chunk, chunk), chunk)
        ones, none = jnp.ones((1, chunk), F32), jnp.zeros((1, chunk), F32)
        scaled = split3(jnp.concatenate([x, v, ones, none], axis=0) * (mass / N_STARS))
        weights[:, at] = jnp.concatenate(list(scaled) + [rows_of(24, 32, chunk)], axis=0).astype(BF16)
        features[at, :] = star_features(x, v).T.astype(BF16)
        return 0

    lax.fori_loop(0, count, one_chunk, 0)


def force_sums(x_own, v_own, deep, out_ref, weights, features, dist_own, both_own, own):
    dist_own[...], both_own[...] = active_features(x_own, v_own)
    own[...] = jnp.concatenate([x_own, v_own, jnp.zeros((2, PART), F32)], axis=0)
    wide = 256

    def half(h, _):
        cut = pl.ds(pl.multiple_of(h * wide, wide), wide)

        def sums(n, total):
            lanes = pl.ds(pl.multiple_of(n * deep, deep), deep)
            factor = features[lanes, :]
            dist = jnp.dot(factor, dist_own[:, cut], preferred_element_type=F32)
            both = jnp.dot(factor, both_own[:, cut], preferred_element_type=F32)
            inverse = lax.rsqrt(jnp.maximum(dist, softening))
            inverse_sq = inverse * inverse
            weight = inverse * inverse_sq
            radial = (weight * inverse_sq) * both
            w_high, w_low = split2(weight)
            u_high, u_low = split2(radial)
            dot = functools.partial(jnp.dot, weights[:, lanes], preferred_element_type=F32)
            return (total[0] + (dot(w_high) + dot(w_low)), total[1] + (dot(u_high) + dot(u_low)))

        nothing = jnp.zeros((32, wide), F32)
        w_sum, u_sum = lax.fori_loop(0, 4, sums, (nothing, nothing))
        w_sum = w_sum[0:8] + w_sum[8:16] + w_sum[16:24]
        u_sum = u_sum[0:8] + u_sum[8:16] + u_sum[16:24]
        mine = own[:, cut]
        x, v = mine[0:3], mine[3:6]
        acc = w_sum[0:3] - x * w_sum[6:7]
        jerk = w_sum[3:6] - v * w_sum[6:7] - 3.0 * (u_sum[0:3] - x * u_sum[6:7])
        out_ref[:, cut] = jnp.concatenate([acc, jerk, jnp.zeros((2, wide), F32)], axis=0)
        return 0

    lax.fori_loop(0, PART // wide, half, 0)


def sum_of(landing):
    total = landing[0]
    for c in range(1, COLS):
        total = total + landing[c]
    return total


def steps_kernel(
    lists_own, phase_ref, derivs_ref, time_ref, mass_ref,
    all0_ref, all1_ref, near_ref, base_ref, order_ref,
    lists_ref, places, picks0, picks1, land0, land1, part0, part1, landf0, landf1, mine0, mine1,
    old, own, weights, features, dist_own, both_own,
    s_list, r_list, s_pick0, r_pick0, s_pick1, r_pick1, s_for0, r_for0, s_for1, r_for1,
    s_all0, r_all0, s_all1, r_all1,
):
    row, col = lax.axis_index("row"), lax.axis_index("col")
    offset = col * LOCAL
    chunk = 2048
    sub = lax.broadcasted_iota(I32, (8, 128), 0)
    greet([p for _, p in partners_of("row", ROWS, row)] + [p for _, p in partners_of("col", COLS, col)])
    lists = ("row", ROWS, row, lists_own, lists_ref, s_list, r_list)
    copies = exchange(*lists)
    lists_ref[pl.ds(row, 1)] = lists_own[...][None]

    def first_stars(n):
        lanes = pl.ds(pl.multiple_of(n * chunk, chunk), chunk)
        x, v = predict(phase_ref[:, lanes], derivs_ref[:, lanes], time_ref[:, lanes], block_times[0])
        return x, v, mass_ref[:, lanes]

    prepare(0, chunk, LOCAL // chunk, first_stars, weights, features)
    arrived(*lists)

    def block(b):
        return pl.ds(pl.multiple_of(b * 128, 128), 128)

    pairs = [
        lambda b, ref=ref, c=c: two_rows(sub, ref[c : c + 1, block(b)], ref[c + 1 : c + 2, block(b)])
        for ref in (phase_ref, derivs_ref)
        for c in (0, 2, 4)
    ]
    pairs.append(lambda b: two_rows(sub, time_ref[:, block(b)], mass_ref[:, block(b)]))
    local = own_stars(lists_ref, row) - offset
    for p, value in enumerate(fetch(both_halves(local, 0), pairs)):
        picks0[p] = value
    first_picks = ("col", COLS, col, picks0, land0, s_pick0, r_pick0)
    copies += exchange(*first_picks)
    land0[pl.ds(col, 1)] = picks0[...][None]

    found = place_map(lists_ref, 0, offset)
    places[0, 0], places[0, 1] = found[:, 0:128], found[:, 128:256]
    pairs.append(
        lambda b: two_rows(sub, places[0, 0, pl.ds(b, 1), :], places[0, 1, pl.ds(b, 1), :])
    )
    for p, value in enumerate(fetch(both_halves(local, 1), pairs)):
        picks1[p] = value
    second_picks = ("col", COLS, col, picks1, land1, s_pick1, r_pick1)
    copies += exchange(*second_picks)
    land1[pl.ds(col, 1)] = picks1[...][None]

    arrived(*first_picks)
    total = sum_of(land0)
    unpack([total[p] for p in range(7)], old)
    x_own, v_own = predict(old[0:6], old[6:12], old[12:13], block_times[0])
    force_sums(x_own, v_own, 4096, part0, weights, features, dist_own, both_own, own)
    forces = ("col", COLS, col, part0, landf0, s_for0, r_for0)
    copies += exchange(*forces)
    landf0[pl.ds(col, 1)] = part0[...][None]
    found = place_map(lists_ref, 1, offset)
    places[1, 0], places[1, 1] = found[:, 0:128], found[:, 128:256]
    arrived(*forces)

    def corrected(landing, mine, now):
        x, v, a, j = correct(old[...], sum_of(landing), now)
        blank = jnp.zeros((1, PART), F32)
        mine[...] = jnp.concatenate([x, v, old[13:14], blank, a, j, blank, blank], axis=0)

    corrected(landf0, mine0, block_times[0])
    gather = ("row", ROWS, row, mine0, all0_ref, s_all0, r_all0)
    copies += exchange(*gather)
    all0_ref[pl.ds(row, 1)] = mine0[...][None]

    def second_stars(n):
        lanes = pl.ds(pl.multiple_of(n * chunk, chunk), chunk)
        x, v = predict(phase_ref[:, lanes], derivs_ref[:, lanes], time_ref[:, lanes], block_times[1])
        moved = jnp.concatenate([places[0, 0, pl.ds(n * 16 + k, 1), :] for k in range(16)], axis=1)
        return x, v, jnp.where(moved > 0.0, 0.0, mass_ref[:, lanes])

    prepare(0, chunk, LOCAL // chunk, second_stars, weights, features)
    rank_map(places[0], near_ref, base_ref, order_ref, 0)
    arrived(*second_picks)
    total = sum_of(land1)
    arrived(*gather)

    def moved_stars(n):
        state = all0_ref[pl.ds(2 * col + n, 1)][0]
        x, v = predict(state[0:6], state[8:14], block_times[0], block_times[1])
        return x, v, state[6:7]

    prepare(LOCAL, PART, 2, moved_stars, weights, features)
    high = both_halves(total[7], 0).astype(I32) - 1
    low = both_halves(total[7], 1).astype(I32)

    def look(r, found):
        for k in range(4):
            here = high == r * 4 + k
            cut = slice(k * 128, k * 128 + 128)
            found = tuple(
                jnp.where(
                    here,
                    lane_pick(two_rows(sub, all0_ref[r, c : c + 1, cut], all0_ref[r, c + 1 : c + 2, cut]), low),
                    was,
                )
                for c, was in zip((0, 2, 4, 8, 10, 12), found)
            )
        return found

    state = lax.fori_loop(0, ROWS, look, tuple(total[p] for p in range(6)))
    when = jnp.where((high >= 0) & (sub < 4), block_times[0], total[6])
    unpack(list(state) + [when], old)
    x_own, v_own = predict(old[0:6], old[6:12], old[12:13], block_times[1])
    force_sums(x_own, v_own, (LOCAL + 2 * PART) // 4, part1, weights, features, dist_own, both_own, own)
    forces = ("col", COLS, col, part1, landf1, s_for1, r_for1)
    copies += exchange(*forces)
    landf1[pl.ds(col, 1)] = part1[...][None]
    arrived(*forces)
    corrected(landf1, mine1, block_times[1])
    gather = ("row", ROWS, row, mine1, all1_ref, s_all1, r_all1)
    copies += exchange(*gather)
    all1_ref[pl.ds(row, 1)] = mine1[...][None]
    rank_map(places[1], near_ref, base_ref, order_ref, 1)
    arrived(*gather)
    for copy in copies:
        copy.wait_send()


def both_steps(lists, phase, derivs, time, masses):
    stars = LOCAL + 2 * PART
    vmem = [
        ((ROWS,) + lists.shape, I32),
        ((2, 2, 128, 128), F32),
        ((8, 8, 128), F32),
        ((8, 8, 128), F32),
        ((COLS, 8, 8, 128), F32),
        ((COLS, 8, 8, 128), F32),
        ((8, PART), F32),
        ((8, PART), F32),
        ((COLS, 8, PART), F32),
        ((COLS, 8, PART), F32),
        ((16, PART), F32),
        ((16, PART), F32),
        ((16, PART), F32),
        ((8, PART), F32),
        ((32, stars), BF16),
        ((stars, 64), BF16),
        ((64, PART), BF16),
        ((64, PART), BF16),
    ]
    sems = [ROWS] * 2 + [COLS] * 8 + [ROWS] * 4
    return pl.pallas_call(
        steps_kernel,
        out_shape=[
            jax.ShapeDtypeStruct((ROWS, 16, PART), F32),
            jax.ShapeDtypeStruct((ROWS, 16, PART), F32),
            jax.ShapeDtypeStruct((2, 128, 128), I32),
            jax.ShapeDtypeStruct((2, 2, 8, 128), I32),
            jax.ShapeDtypeStruct((2, 64, 256), F32),
        ],
        in_specs=in_vmem(5),
        out_specs=in_vmem(5),
        scratch_shapes=[pltpu.VMEM(shape, kind) for shape, kind in vmem]
        + [pltpu.SemaphoreType.DMA((n,)) for n in sems],
        compiler_params=params(collective_id=0, has_side_effects=True),
        name="both_steps",
    )(lists, phase, derivs, time, masses)


def collect(step, count, order_ref, all_ref, sorted_ref):
    def one_block(n, _):
        group = order_ref[step, pl.ds(pl.multiple_of((n >> 3) * 8, 8), 8), :]
        mask = lax.broadcasted_iota(I32, (8, 256), 0) == (n & 7)
        digits = jnp.sum(jnp.where(mask, group, 0.0), axis=0, keepdims=True)
        high = spread(digits[:, 0:128]).astype(I32) - 1
        low = spread(digits[:, 128:256]).astype(I32)
        upper = jnp.zeros((8, 128), F32)
        lower = jnp.zeros((8, 128), F32)
        for b in range(64):
            here = high == b
            lanes = slice((b % 4) * 128, (b % 4) * 128 + 128)
            upper = jnp.where(here, lane_pick(all_ref[b // 4, 0:8, lanes], low), upper)
            lower = jnp.where(here, lane_pick(all_ref[b // 4, 8:16, lanes], low), lower)
        sorted_ref[step, n, 0:8, :] = upper
        sorted_ref[step, n, 8:16, :] = lower
        return 0

    lax.fori_loop(0, (count + 127) // 128, one_block, 0)


def last_kernel(
    base_ref, near_ref, order_ref, all0_ref, all1_ref, phase_ref, derivs_ref, time_ref,
    phase_out, derivs_out, time_out, sorted_ref,
):
    collect(0, base_ref[0, 1, 0, 127], order_ref, all0_ref, sorted_ref)
    collect(1, base_ref[1, 1, 0, 127], order_ref, all1_ref, sorted_ref)

    def put(g, _):
        for u in range(8):
            b = g * 8 + u
            lanes = pl.ds(pl.multiple_of(b * 128, 128), 128)
            blank = jnp.zeros((2, 128), F32)
            phase = jnp.concatenate([phase_ref[:, lanes], blank], axis=0)
            derivs = jnp.concatenate([derivs_ref[:, lanes], blank], axis=0)
            time = time_ref[:, lanes]
            for step in range(2):
                n = jnp.minimum(base_ref[step, 0, 0, b], 63)
                m = jnp.minimum(n + 1, 63)
                at = spread(near_ref[step, pl.ds(b, 1), :]) - 1
                low = at & 127
                is_first = (at >= 0) & (at < 128)
                is_next = at >= 128

                def chosen(rows, was):
                    new = jnp.where(is_first, lane_pick(sorted_ref[step, n, rows, :], low), was)
                    return jnp.where(is_next, lane_pick(sorted_ref[step, m, rows, :], low), new)

                phase = chosen(slice(0, 8), phase)
                derivs = chosen(slice(8, 16), derivs)
                time = jnp.where(at[0:1] >= 0, block_times[step], time)
            phase_out[:, lanes] = phase[0:6]
            derivs_out[:, lanes] = derivs[0:6]
            time_out[:, lanes] = time
        return 0

    lax.fori_loop(0, BLOCKS // 8, put, 0)


def last_update(base, near, order, all0, all1, phase, derivs, time):
    return pl.pallas_call(
        last_kernel,
        out_shape=[
            jax.ShapeDtypeStruct((6, LOCAL), F32),
            jax.ShapeDtypeStruct((6, LOCAL), F32),
            jax.ShapeDtypeStruct((1, LOCAL), F32),
        ],
        in_specs=[pl.BlockSpec(memory_space=pltpu.SMEM)] + in_vmem(7),
        out_specs=in_vmem(3),
        scratch_shapes=[pltpu.VMEM((2, 64, 16, 128), F32)],
        compiler_params=params(),
        name="last_update",
    )(base, near, order, all0, all1, phase, derivs, time)


def body(phase_space, derivs, star_time, masses, active_index, active_count):
    time = star_time.reshape(1, LOCAL)
    masses = masses.reshape(1, LOCAL)
    own = jnp.concatenate(
        [
            active_index.reshape(16, 128),
            jnp.broadcast_to(active_count.reshape(2, 1), (2, 128)),
            jnp.zeros((6, 128), I32),
        ],
        axis=0,
    )
    all0, all1, near, base, order = both_steps(own, phase_space, derivs, time, masses)
    phase_space, derivs, time = last_update(base, near, order, all0, all1, phase_space, derivs, time)
    return phase_space, derivs, time.reshape(LOCAL)


def solution(mesh):
    return jax.shard_map(
        body,
        mesh=mesh,
        in_specs=(
            P(None, "col"),
            P(None, "col"),
            P("col"),
            P("col"),
            P(None, "row", None),
            P(None, "row"),
        ),
        out_specs=(P(None, "col"), P(None, "col"), P("col")),
        check_vma=False,
    )
```

```python
import functools

import jax
import jax.numpy as jnp
from jax import lax
from jax.experimental import pallas as pl
from jax.experimental.pallas import tpu as pltpu
from jax.sharding import PartitionSpec as P

F32 = jnp.float32
BF16 = jnp.bfloat16
I32 = jnp.int32
softening = 0.01
block_times = (0.125, 0.25)
ROWS = 16
COLS = 8
CAP = 1024
PART = 512
LOCAL = 16384
BLOCKS = LOCAL // 128
N_STARS = ROWS * PART * 16
MESH = pl.DeviceIdType.MESH
ADDED = (((1,), (1,)), ((), ()))


def rows_of(first, last, width):
    return jnp.zeros((last - first, width), F32)


def in_vmem(n):
    return [pl.BlockSpec(memory_space=pltpu.VMEM)] * n


def params(**more):
    return pltpu.CompilerParams(vmem_limit_bytes=40 * 2**20, **more)


def partners_of(axis, size, place):
    return [(k, {axis: lax.rem(place + k, size)}) for k in range(1, size)]


def exchange(axis, size, place, source, landing, send_sem, recv_sem):
    copies = []
    for k, partner in partners_of(axis, size, place):
        copy = pltpu.make_async_remote_copy(
            src_ref=source,
            dst_ref=landing.at[place],
            send_sem=send_sem.at[k],
            recv_sem=recv_sem.at[place],
            device_id=partner,
            device_id_type=MESH,
        )
        copy.start()
        copies.append(copy)
    return copies


def arrived(axis, size, place, source, landing, send_sem, recv_sem):
    for k, partner in partners_of(axis, size, place):
        slot = lax.rem(place + k, size)
        pltpu.make_async_remote_copy(
            src_ref=source,
            dst_ref=landing.at[slot],
            send_sem=send_sem.at[k],
            recv_sem=recv_sem.at[slot],
            device_id=partner,
            device_id_type=MESH,
        ).wait_recv()


def lane_pick(table, lanes):
    return jnp.take_along_axis(table, lanes, axis=1, mode="promise_in_bounds")


def spread(row):
    return jnp.broadcast_to(row, (8, 128))


def hot(index_row, count):
    kinds = lax.broadcasted_iota(I32, (count, 128), 0).astype(F32).astype(BF16)
    return jnp.broadcast_to(index_row, (count, 128)).astype(BF16) == kinds


def scattered(entries, high_count):
    one, zero = jnp.ones((), BF16), jnp.zeros((), BF16)
    left, right = [], []
    for high, low, first, second in entries:
        left.append(jnp.where(hot(high, high_count), one, zero))
        at_low = hot(low, 128)
        a = jnp.broadcast_to(first, (128, 128)).astype(BF16)
        b = jnp.broadcast_to(second, (128, 128)).astype(BF16)
        right.append(jnp.concatenate([jnp.where(at_low, a, zero), jnp.where(at_low, b, zero)], axis=0))
    return lax.dot_general(
        jnp.concatenate(left, axis=1), jnp.concatenate(right, axis=1), ADDED, preferred_element_type=F32
    )


def place_map(lists_ref, step, offset):
    slot = lax.broadcasted_iota(I32, (8, 128), 0) * 128 + lax.broadcasted_iota(I32, (8, 128), 1)
    begin = jnp.zeros((8, 128), I32)
    entries = []
    for r in range(ROWS):
        count = spread(lists_ref[r, 16 + step : 17 + step, :])
        star = lists_ref[r, 8 * step : 8 * step + 8, :] - offset
        live = (slot < count) & (star >= 0) & (star < LOCAL)
        at = begin + slot
        high = jnp.where(live, star >> 7, 255).astype(F32)
        low = (star & 127).astype(F32)
        first, second = ((at >> 7) + 1).astype(F32), (at & 127).astype(F32)
        for k in range(8):
            cut = slice(k, k + 1)
            entries.append((high[cut], low[cut], first[cut], second[cut]))
        begin = begin + count
    return scattered(entries, 128)


def rank_map(places, near_ref, base_ref, order_ref, step):
    at_high, at_low = places[0], places[1]
    row = lax.broadcasted_iota(I32, (128, 128), 0)
    lane = lax.broadcasted_iota(I32, (128, 128), 1)
    up_to = (row <= lane).astype(F32).astype(BF16)
    before = (row < lane).astype(F32).astype(BF16)
    below = (lane < row).astype(F32).astype(BF16)
    active = (at_high > 0.0).astype(F32)
    active16 = active.astype(BF16)
    so_far = jnp.dot(active16, up_to, preferred_element_type=F32)
    total = jnp.broadcast_to(so_far[:, 127:128], (128, 128))
    first = jnp.dot(below, total.astype(BF16), preferred_element_type=F32)
    rank = (first + so_far - active).astype(I32)
    near_ref[step] = jnp.where(active > 0.0, rank - (first.astype(I32) >> 7) * 128 + 1, 0)
    ones = jnp.ones((8, 128), F32).astype(BF16)
    totals = lax.dot_general(ones, active16, ADDED, preferred_element_type=F32)
    firsts = jnp.dot(totals.astype(BF16), before, preferred_element_type=F32).astype(I32)
    base_ref[step, 0] = firsts >> 7
    base_ref[step, 1] = firsts + totals.astype(I32)
    rank_high = jnp.where(active > 0.0, rank >> 7, 255).astype(F32)
    rank_low = (rank & 127).astype(F32)
    entries = []
    for b in range(BLOCKS):
        cut = slice(b, b + 1)
        entries.append((rank_high[cut], rank_low[cut], at_high[cut], at_low[cut]))
    order_ref[step] = scattered(entries, 64)


def own_stars(lists_ref, place):
    lane = lax.broadcasted_iota(I32, (8, 128), 1)
    sub = lax.broadcasted_iota(I32, (8, 128), 0)
    position = place * PART + (sub & 3) * 128 + lane
    before = jnp.zeros((8, 128), I32)
    which = jnp.zeros((8, 128), I32)
    start = jnp.zeros((8, 128), I32)
    for r in range(ROWS):
        count = jnp.where(sub < 4, spread(lists_ref[r, 16:17, :]), spread(lists_ref[r, 17:18, :]))
        end = before + count
        passed = position >= end
        which = which + passed.astype(I32)
        start = jnp.where(passed, end, start)
        before = end
    flat = which * CAP + position - start
    high, low = flat >> 7, flat & 127
    stars = jnp.zeros((8, 128), I32)
    for r in range(ROWS):
        for k in range(8):
            row = jnp.where(
                sub < 4, spread(lists_ref[r, k : k + 1, :]), spread(lists_ref[r, 8 + k : 9 + k, :])
            )
            stars = jnp.where(high == r * 8 + k, lane_pick(row, low), stars)
    return stars


def both_halves(x, step):
    part = x[4 * step : 4 * step + 4]
    return jnp.concatenate([part, part], axis=0)


def fetch(stars, pairs):
    high, low = stars >> 7, stars & 127

    def look(g, found):
        for u in range(8):
            b = g * 8 + u
            here = high == b
            found = tuple(
                jnp.where(here, lane_pick(pair(b), low), old) for pair, old in zip(pairs, found)
            )
        return found

    return lax.fori_loop(0, BLOCKS // 8, look, tuple(jnp.zeros((8, 128), F32) for _ in pairs))


def two_rows(sub, a, b):
    return jnp.where(sub < 4, spread(a), spread(b))


def unpack(pairs, out_ref):
    for p, pair in enumerate(pairs):
        for half in range(2):
            for s in range(4):
                out_ref[2 * p + half : 2 * p + half + 1, s * 128 : s * 128 + 128] = pair[
                    4 * half + s : 4 * half + s + 1
                ]


def predict(phase, derivs, time, now):
    d = now - time
    x, v, a, j = phase[0:3], phase[3:6], derivs[0:3], derivs[3:6]
    return x + d * (v + d * (a / 2.0 + d * j / 6.0)), v + d * (a + d * j / 2.0)


def correct(x, v, old_acc, old_jerk, h, forces):
    new_acc, new_jerk = forces[0:3], forces[3:6]
    change = old_acc - new_acc
    second = (-6.0 * change - h * (4.0 * old_jerk + 2.0 * new_jerk)) / (h * h)
    third = (12.0 * change + 6.0 * h * (old_jerk + new_jerk)) / (h * h * h)
    h2 = h * h
    h3 = h2 * h
    h4 = h3 * h
    h5 = h4 * h
    x = x + h4 / 24.0 * second + h5 / 120.0 * third
    v = v + h3 / 6.0 * second + h4 / 24.0 * third
    return x, v, new_acc, new_jerk


PAIRS = ((0, 0), (0, 1), (0, 2), (1, 0), (1, 1), (2, 0))


def split3(x):
    high = x.astype(BF16).astype(F32)
    rest = x - high
    middle = rest.astype(BF16).astype(F32)
    return high, middle, rest - middle


def split2(x):
    high = x.astype(BF16)
    return high, (x - high.astype(F32)).astype(BF16)


def squares(x, v):
    xx = x * x
    xv = x * v
    return xx[0:1] + xx[1:2] + xx[2:3], xv[0:1] + xv[1:2] + xv[2:3]


def star_features(x, v):
    width = x.shape[1]
    parts = split3(jnp.concatenate([x, v, jnp.zeros((2, width), F32)], axis=0))
    xx, xv = squares(x, v)
    one = jnp.ones((3, width), F32)
    extra = jnp.concatenate(list(split3(xx)) + list(split3(xv)) + [one, one, rows_of(12, 16, width)], axis=0)
    return jnp.concatenate([parts[a] for a, _ in PAIRS] + [extra], axis=0)


def active_features(x, v):
    width = x.shape[1]
    xp, vp = split3(x), split3(v)
    xx, xv = squares(x, v)
    one, none3, none5 = jnp.ones((3, width), F32), rows_of(0, 3, width), rows_of(0, 5, width)
    dist, both = [], []
    for _, b in PAIRS:
        dist += [-2.0 * xp[b], none5]
        both += [-vp[b], -xp[b], rows_of(0, 2, width)]
    dist += [one, none3] + list(split3(xx + softening)) + [none3, rows_of(12, 16, width)]
    both += [none3, one, none3] + list(split3(xv)) + [rows_of(12, 16, width)]
    return jnp.concatenate(dist, axis=0).astype(BF16), jnp.concatenate(both, axis=0).astype(BF16)


def prepare(first, chunk, count, pred_of, weights, features):
    def one_chunk(n, _):
        x, v, mass = pred_of(n)
        at = pl.ds(pl.multiple_of(first + n * chunk, chunk), chunk)
        ones, none = jnp.ones((1, chunk), F32), jnp.zeros((1, chunk), F32)
        scaled = split3(jnp.concatenate([x, v, ones, none], axis=0) * (mass / N_STARS))
        weights[:, at] = jnp.concatenate(list(scaled) + [rows_of(24, 32, chunk)], axis=0).astype(BF16)
        features[at, :] = star_features(x, v).T.astype(BF16)
        return 0

    lax.fori_loop(0, count, one_chunk, 0)


def force_sums(x_own, v_own, deep, out_ref, weights, features, dist_own, both_own, own):
    dist_own[...], both_own[...] = active_features(x_own, v_own)
    own[...] = jnp.concatenate([x_own, v_own, jnp.zeros((2, PART), F32)], axis=0)
    wide = 256

    def half(h, _):
        cut = pl.ds(pl.multiple_of(h * wide, wide), wide)

        def sums(n, total):
            lanes = pl.ds(pl.multiple_of(n * deep, deep), deep)
            factor = features[lanes, :]
            dist = jnp.dot(factor, dist_own[:, cut], preferred_element_type=F32)
            both = jnp.dot(factor, both_own[:, cut], preferred_element_type=F32)
            inverse = lax.rsqrt(jnp.maximum(dist, softening))
            inverse_sq = inverse * inverse
            weight = inverse * inverse_sq
            radial = (weight * inverse_sq) * both
            w_high, w_low = split2(weight)
            u_high, u_low = split2(radial)
            dot = functools.partial(jnp.dot, weights[:, lanes], preferred_element_type=F32)
            return (total[0] + (dot(w_high) + dot(w_low)), total[1] + (dot(u_high) + dot(u_low)))

        nothing = jnp.zeros((32, wide), F32)
        w_sum, u_sum = lax.fori_loop(0, 4, sums, (nothing, nothing))
        w_sum = w_sum[0:8] + w_sum[8:16] + w_sum[16:24]
        u_sum = u_sum[0:8] + u_sum[8:16] + u_sum[16:24]
        mine = own[:, cut]
        x, v = mine[0:3], mine[3:6]
        acc = w_sum[0:3] - x * w_sum[6:7]
        jerk = w_sum[3:6] - v * w_sum[6:7] - 3.0 * (u_sum[0:3] - x * u_sum[6:7])
        out_ref[:, cut] = jnp.concatenate([acc, jerk, jnp.zeros((2, wide), F32)], axis=0)
        return 0

    lax.fori_loop(0, PART // wide, half, 0)


def sum_of(landing):
    total = landing[0]
    for c in range(1, COLS):
        total = total + landing[c]
    return total


def packed(x, v, a, j):
    rest = jnp.concatenate([a[2:3], j], axis=0)
    right = jnp.concatenate([rest[:, 0:256], rest[:, 256:512]], axis=0)
    return jnp.concatenate([jnp.concatenate([x, v, a[0:2]], axis=0), right], axis=1)


def take_moved(high, low, sub, rows_at):
    def look(r, found):
        for k in range(4):
            here = high == r * 4 + k
            found = tuple(
                jnp.where(here, lane_pick(two_rows(sub, *pair), low), was)
                for pair, was in zip(rows_at(r, k), found)
            )
        return found

    return lax.fori_loop(0, ROWS, look, tuple(jnp.zeros((8, 128), F32) for _ in range(3)))


def steps_kernel(
    index_ref, count_ref, phase_far, derivs_far, time_far, mass_far,
    all0_ref, all1_ref, near_ref, base_ref, order_ref,
    phase_ref, derivs_ref, time_ref, mass_ref, lists_own, lists_ref, places,
    picks0, picks1, land0, land1, part0, part1, landf0, landf1, lead, lead_all, mine0, mine1,
    old, fix, own, weights, features, dist_own, both_own,
    s_in, s_list, r_list, s_pick0, r_pick0, s_pick1, r_pick1, s_for0, r_for0, s_for1, r_for1,
    s_lead, r_lead, s_all0, r_all0, s_all1, r_all1,
):
    row, col = lax.axis_index("row"), lax.axis_index("col")
    barrier = pltpu.get_barrier_semaphore()
    everyone = partners_of("row", ROWS, row) + partners_of("col", COLS, col)
    for _, partner in everyone:
        pl.semaphore_signal(barrier, inc=1, device_id=partner, device_id_type=MESH)
    inputs = [
        pltpu.make_async_copy(far, near, s_in.at[n])
        for n, (far, near) in enumerate(
            [(phase_far, phase_ref), (derivs_far, derivs_ref), (time_far, time_ref), (mass_far, mass_ref)]
        )
    ]
    for copy in inputs:
        copy.start()
    offset = col * LOCAL
    chunk = 2048
    sub = lax.broadcasted_iota(I32, (8, 128), 0)
    for step in range(2):
        for k in range(8):
            lists_own[8 * step + k : 8 * step + k + 1, :] = index_ref[step, 0:1, k * 128 : k * 128 + 128]
        lists_own[16 + step : 17 + step, :] = jnp.broadcast_to(count_ref[0:1, step : step + 1], (1, 128))
    lists_own[18:24, :] = jnp.zeros((6, 128), I32)
    pl.semaphore_wait(barrier, len(everyone))
    lists = ("row", ROWS, row, lists_own, lists_ref, s_list, r_list)
    copies = exchange(*lists)
    lists_ref[pl.ds(row, 1)] = lists_own[...][None]
    for copy in inputs:
        copy.wait()

    def first_stars(n):
        lanes = pl.ds(pl.multiple_of(n * chunk, chunk), chunk)
        x, v = predict(phase_ref[:, lanes], derivs_ref[:, lanes], time_ref[:, lanes], block_times[0])
        return x, v, mass_ref[:, lanes]

    prepare(0, chunk, LOCAL // chunk, first_stars, weights, features)
    arrived(*lists)

    def block(b):
        return pl.ds(pl.multiple_of(b * 128, 128), 128)

    pairs = [
        lambda b, ref=ref, c=c: two_rows(sub, ref[c : c + 1, block(b)], ref[c + 1 : c + 2, block(b)])
        for ref in (phase_ref, derivs_ref)
        for c in (0, 2, 4)
    ]
    pairs.append(lambda b: two_rows(sub, time_ref[:, block(b)], mass_ref[:, block(b)]))
    local = own_stars(lists_ref, row) - offset
    for p, value in enumerate(fetch(both_halves(local, 0), pairs)):
        picks0[p] = value
    first_picks = ("col", COLS, col, picks0, land0, s_pick0, r_pick0)
    copies += exchange(*first_picks)
    land0[pl.ds(col, 1)] = picks0[...][None]

    found = place_map(lists_ref, 0, offset)
    places[0, 0], places[0, 1] = found[:, 0:128], found[:, 128:256]
    pairs.append(lambda b: two_rows(sub, places[0, 0, pl.ds(b, 1), :], places[0, 1, pl.ds(b, 1), :]))
    for p, value in enumerate(fetch(both_halves(local, 1), pairs)):
        picks1[p] = value
    second_picks = ("col", COLS, col, picks1, land1, s_pick1, r_pick1)
    copies += exchange(*second_picks)
    land1[pl.ds(col, 1)] = picks1[...][None]

    arrived(*first_picks)
    total = sum_of(land0)
    unpack([total[p] for p in range(7)], old)
    x_own, v_own = predict(old[0:6], old[6:12], old[12:13], block_times[0])
    force_sums(x_own, v_own, 4096, part0, weights, features, dist_own, both_own, own)
    forces = ("col", COLS, col, part0, landf0, s_for0, r_for0)
    copies += exchange(*forces)
    landf0[pl.ds(col, 1)] = part0[...][None]
    found = place_map(lists_ref, 1, offset)
    places[1, 0], places[1, 1] = found[:, 0:128], found[:, 128:256]
    arrived(*forces)
    x, v, a, j = correct(
        own[0:3], own[3:6], old[6:9], old[9:12], block_times[0] - old[12:13], sum_of(landf0)
    )
    x_next, v_next = predict(
        jnp.concatenate([x, v], axis=0), jnp.concatenate([a, j], axis=0), block_times[0], block_times[1]
    )
    lead[...] = jnp.concatenate([x_next, v_next, old[13:14], jnp.zeros((1, PART), F32)], axis=0)
    first_lead = ("row", ROWS, row, lead, lead_all, s_lead, r_lead)
    copies += exchange(*first_lead)
    mine0[...] = packed(x, v, a, j)
    gather0 = ("row", ROWS, row, mine0, all0_ref, s_all0, r_all0)
    copies += exchange(*gather0)
    lead_all[pl.ds(row, 1)] = lead[...][None]
    all0_ref[pl.ds(row, 1)] = mine0[...][None]

    def second_stars(n):
        lanes = pl.ds(pl.multiple_of(n * chunk, chunk), chunk)
        x, v = predict(phase_ref[:, lanes], derivs_ref[:, lanes], time_ref[:, lanes], block_times[1])
        moved = jnp.concatenate([places[0, 0, pl.ds(n * 16 + k, 1), :] for k in range(16)], axis=1)
        return x, v, jnp.where(moved > 0.0, 0.0, mass_ref[:, lanes])

    prepare(0, chunk, LOCAL // chunk, second_stars, weights, features)
    rank_map(places[0], near_ref, base_ref, order_ref, 0)
    arrived(*second_picks)
    total = sum_of(land1)
    unpack([total[p] for p in range(8)], old)
    high = both_halves(total[7], 0).astype(I32) - 1
    low = both_halves(total[7], 1).astype(I32)
    arrived(*first_lead)

    def moved_stars(n):
        state = lead_all[pl.ds(2 * col + n, 1)][0]
        return state[0:3], state[3:6], state[6:7]

    prepare(LOCAL, PART, 2, moved_stars, weights, features)

    def lead_rows(r, k):
        cut = slice(k * 128, k * 128 + 128)
        return [(lead_all[r, c : c + 1, cut], lead_all[r, c + 1 : c + 2, cut]) for c in (0, 2, 4)]

    unpack(take_moved(high, low, sub, lead_rows), fix)
    moved = old[14:15] > 0.0
    x_own, v_own = predict(old[0:6], old[6:12], old[12:13], block_times[1])
    x_own = jnp.where(moved, fix[0:3], x_own)
    v_own = jnp.where(moved, fix[3:6], v_own)
    force_sums(x_own, v_own, (LOCAL + 2 * PART) // 4, part1, weights, features, dist_own, both_own, own)
    forces = ("col", COLS, col, part1, landf1, s_for1, r_for1)
    copies += exchange(*forces)
    landf1[pl.ds(col, 1)] = part1[...][None]
    arrived(*gather0)

    def rest_rows(r, k):
        cut, at = slice(k * 128, k * 128 + 128), 4 * (k // 2)
        tail = slice(512 + (k % 2) * 128, 640 + (k % 2) * 128)
        return [
            (all0_ref[r, 6:7, cut], all0_ref[r, 7:8, cut]),
            (all0_ref[r, at : at + 1, tail], all0_ref[r, at + 1 : at + 2, tail]),
            (all0_ref[r, at + 2 : at + 3, tail], all0_ref[r, at + 3 : at + 4, tail]),
        ]

    unpack(take_moved(high, low, sub, rest_rows), fix)
    moved = old[14:15] > 0.0
    acc = jnp.where(moved, fix[0:3], old[6:9])
    jerk = jnp.where(moved, fix[3:6], old[9:12])
    h = block_times[1] - jnp.where(moved, block_times[0], old[12:13])
    arrived(*forces)
    mine1[...] = packed(*correct(own[0:3], own[3:6], acc, jerk, h, sum_of(landf1)))
    gather1 = ("row", ROWS, row, mine1, all1_ref, s_all1, r_all1)
    copies += exchange(*gather1)
    all1_ref[pl.ds(row, 1)] = mine1[...][None]
    rank_map(places[1], near_ref, base_ref, order_ref, 1)
    arrived(*gather1)
    for copy in copies:
        copy.wait_send()


def both_steps(index, count, phase, derivs, time, masses):
    stars = LOCAL + 2 * PART
    vmem = [
        ((6, LOCAL), F32),
        ((6, LOCAL), F32),
        ((1, LOCAL), F32),
        ((1, LOCAL), F32),
        ((24, 128), I32),
        ((ROWS, 24, 128), I32),
        ((2, 2, 128, 128), F32),
        ((7, 8, 128), F32),
        ((8, 8, 128), F32),
        ((COLS, 7, 8, 128), F32),
        ((COLS, 8, 8, 128), F32),
        ((8, PART), F32),
        ((8, PART), F32),
        ((COLS, 8, PART), F32),
        ((COLS, 8, PART), F32),
        ((8, PART), F32),
        ((ROWS, 8, PART), F32),
        ((8, 768), F32),
        ((8, 768), F32),
        ((16, PART), F32),
        ((8, PART), F32),
        ((8, PART), F32),
        ((32, stars), BF16),
        ((stars, 64), BF16),
        ((64, PART), BF16),
        ((64, PART), BF16),
    ]
    sems = [4] + [ROWS] * 2 + [COLS] * 8 + [ROWS] * 6
    return pl.pallas_call(
        steps_kernel,
        out_shape=[
            jax.ShapeDtypeStruct((ROWS, 8, 768), F32),
            jax.ShapeDtypeStruct((ROWS, 8, 768), F32),
            jax.ShapeDtypeStruct((2, 128, 128), I32),
            jax.ShapeDtypeStruct((2, 2, 8, 128), I32),
            jax.ShapeDtypeStruct((2, 64, 256), F32),
        ],
        in_specs=in_vmem(2) + [pl.BlockSpec(memory_space=pltpu.HBM)] * 4,
        out_specs=in_vmem(5),
        scratch_shapes=[pltpu.VMEM(shape, kind) for shape, kind in vmem]
        + [pltpu.SemaphoreType.DMA((n,)) for n in sems],
        compiler_params=params(collective_id=0, has_side_effects=True),
        name="both_steps",
    )(index, count, phase, derivs, time, masses)


def collect(step, count, order_ref, all_ref, sorted_ref):
    def one_block(n, _):
        group = order_ref[step, pl.ds(pl.multiple_of((n >> 3) * 8, 8), 8), :]
        mask = lax.broadcasted_iota(I32, (8, 256), 0) == (n & 7)
        digits = jnp.sum(jnp.where(mask, group, 0.0), axis=0, keepdims=True)
        high = spread(digits[:, 0:128]).astype(I32) - 1
        low = spread(digits[:, 128:256]).astype(I32)
        upper = jnp.zeros((8, 128), F32)
        lower = jnp.zeros((8, 128), F32)
        shifted = high - 2 * (lax.broadcasted_iota(I32, (8, 128), 0) >> 2)
        for b in range(64):
            r, k = b // 4, b % 4
            upper = jnp.where(high == b, lane_pick(all_ref[r, :, k * 128 : k * 128 + 128], low), upper)
            if k < 2:
                tail = slice(512 + k * 128, 640 + k * 128)
                lower = jnp.where(shifted == b, lane_pick(all_ref[r, :, tail], low), lower)
        blank = jnp.zeros((2, 128), F32)
        rest = lower[0:4] + lower[4:8]
        sorted_ref[step, n, 0:8, :] = upper
        sorted_ref[step, n, 8:16, :] = jnp.concatenate([upper[6:8], rest, blank], axis=0)
        return 0

    lax.fori_loop(0, (count + 127) // 128, one_block, 0)


def last_kernel(
    base_ref, near_ref, order_ref, all0_ref, all1_ref, phase_ref, derivs_ref, time_ref,
    phase_out, derivs_out, time_out, sorted_ref,
):
    collect(0, base_ref[0, 1, 0, 127], order_ref, all0_ref, sorted_ref)
    collect(1, base_ref[1, 1, 0, 127], order_ref, all1_ref, sorted_ref)

    def put(g, _):
        for u in range(8):
            b = g * 8 + u
            lanes = pl.ds(pl.multiple_of(b * 128, 128), 128)
            blank = jnp.zeros((2, 128), F32)
            phase = jnp.concatenate([phase_ref[:, lanes], blank], axis=0)
            derivs = jnp.concatenate([derivs_ref[:, lanes], blank], axis=0)
            time = time_ref[:, lanes]
            for step in range(2):
                n = jnp.minimum(base_ref[step, 0, 0, b], 63)
                m = jnp.minimum(n + 1, 63)
                at = spread(near_ref[step, pl.ds(b, 1), :]) - 1
                low = at & 127
                is_first = (at >= 0) & (at < 128)
                is_next = at >= 128

                def chosen(rows, was):
                    new = jnp.where(is_first, lane_pick(sorted_ref[step, n, rows, :], low), was)
                    return jnp.where(is_next, lane_pick(sorted_ref[step, m, rows, :], low), new)

                phase = chosen(slice(0, 8), phase)
                derivs = chosen(slice(8, 16), derivs)
                time = jnp.where(at[0:1] >= 0, block_times[step], time)
            phase_out[:, lanes] = phase[0:6]
            derivs_out[:, lanes] = derivs[0:6]
            time_out[:, lanes] = time
        return 0

    lax.fori_loop(0, BLOCKS // 8, put, 0)


def last_update(base, near, order, all0, all1, phase, derivs, time):
    return pl.pallas_call(
        last_kernel,
        out_shape=[
            jax.ShapeDtypeStruct((6, LOCAL), F32),
            jax.ShapeDtypeStruct((6, LOCAL), F32),
            jax.ShapeDtypeStruct((1, LOCAL), F32),
        ],
        in_specs=[pl.BlockSpec(memory_space=pltpu.SMEM)] + in_vmem(7),
        out_specs=in_vmem(3),
        scratch_shapes=[pltpu.VMEM((2, 64, 16, 128), F32)],
        compiler_params=params(),
        name="last_update",
    )(base, near, order, all0, all1, phase, derivs, time)


def body(phase_space, derivs, star_time, masses, active_index, active_count):
    time = star_time.reshape(1, LOCAL)
    masses = masses.reshape(1, LOCAL)
    all0, all1, near, base, order = both_steps(
        active_index, active_count.reshape(1, 2), phase_space, derivs, time, masses
    )
    phase_space, derivs, time = last_update(base, near, order, all0, all1, phase_space, derivs, time)
    return phase_space, derivs, time.reshape(LOCAL)


def solution(mesh):
    return jax.shard_map(
        body,
        mesh=mesh,
        in_specs=(
            P(None, "col"),
            P(None, "col"),
            P("col"),
            P("col"),
            P(None, "row", None),
            P(None, "row"),
        ),
        out_specs=(P(None, "col"), P(None, "col"), P("col")),
        check_vma=False,
    )
```

```python
import functools

import jax
import jax.numpy as jnp
from jax import lax
from jax.experimental import pallas as pl
from jax.experimental.pallas import tpu as pltpu
from jax.sharding import PartitionSpec as P

F32 = jnp.float32
BF16 = jnp.bfloat16
I32 = jnp.int32
softening = 0.01
block_times = (0.125, 0.25)
ROWS = 16
COLS = 8
CAP = 1024
PART = 512
HALF = 256
LOCAL = 16384
BLOCKS = LOCAL // 128
N_STARS = ROWS * PART * 16
MESH = pl.DeviceIdType.MESH
ADDED = (((1,), (1,)), ((), ()))


def rows_of(first, last, width):
    return jnp.zeros((last - first, width), F32)


def in_vmem(n):
    return [pl.BlockSpec(memory_space=pltpu.VMEM)] * n


def params(**more):
    return pltpu.CompilerParams(vmem_limit_bytes=56 * 2**20, **more)


def partners_of(axis, size, place):
    return [(k, {axis: lax.rem(place + k, size)}) for k in range(1, size)]


def exchange(axis, size, place, source, landing, send_sem, recv_sem):
    for k, partner in partners_of(axis, size, place):
        pltpu.make_async_remote_copy(
            src_ref=source,
            dst_ref=landing.at[place],
            send_sem=send_sem.at[k],
            recv_sem=recv_sem.at[place],
            device_id=partner,
            device_id_type=MESH,
        ).start()
    landing[pl.ds(place, 1)] = source[...][None]


def sent(axis, size, place, source, landing, send_sem, recv_sem):
    for k, partner in partners_of(axis, size, place):
        pltpu.make_async_remote_copy(
            src_ref=source,
            dst_ref=landing.at[place],
            send_sem=send_sem.at[k],
            recv_sem=recv_sem.at[place],
            device_id=partner,
            device_id_type=MESH,
        ).wait_send()


def arrived(axis, size, place, source, landing, send_sem, recv_sem):
    for k, partner in partners_of(axis, size, place):
        slot = lax.rem(place + k, size)
        pltpu.make_async_remote_copy(
            src_ref=source,
            dst_ref=landing.at[slot],
            send_sem=send_sem.at[k],
            recv_sem=recv_sem.at[slot],
            device_id=partner,
            device_id_type=MESH,
        ).wait_recv()


def lane_pick(table, lanes):
    return jnp.take_along_axis(table, lanes, axis=1, mode="promise_in_bounds")


def spread(row):
    return jnp.broadcast_to(row, (8, 128))


def hot(index_row, count):
    kinds = lax.broadcasted_iota(I32, (count, 128), 0).astype(F32).astype(BF16)
    return jnp.broadcast_to(index_row, (count, 128)).astype(BF16) == kinds


def scattered(entries, high_count):
    one, zero = jnp.ones((), BF16), jnp.zeros((), BF16)
    left, right = [], []
    for high, low, first, second in entries:
        left.append(jnp.where(hot(high, high_count), one, zero))
        at_low = hot(low, 128)
        a = jnp.broadcast_to(first, (128, 128)).astype(BF16)
        b = jnp.broadcast_to(second, (128, 128)).astype(BF16)
        right.append(jnp.concatenate([jnp.where(at_low, a, zero), jnp.where(at_low, b, zero)], axis=0))
    return lax.dot_general(
        jnp.concatenate(left, axis=1), jnp.concatenate(right, axis=1), ADDED, preferred_element_type=F32
    )


def place_map(lists_ref, step, offset):
    slot = lax.broadcasted_iota(I32, (8, 128), 0) * 128 + lax.broadcasted_iota(I32, (8, 128), 1)
    begin = jnp.zeros((8, 128), I32)
    entries = []
    for r in range(ROWS):
        count = spread(lists_ref[r, 16 + step : 17 + step, :])
        star = lists_ref[r, 8 * step : 8 * step + 8, :] - offset
        live = (slot < count) & (star >= 0) & (star < LOCAL)
        at = begin + slot
        high = jnp.where(live, star >> 7, 255).astype(F32)
        low = (star & 127).astype(F32)
        first, second = ((at >> 7) + 1).astype(F32), (at & 127).astype(F32)
        for k in range(8):
            cut = slice(k, k + 1)
            entries.append((high[cut], low[cut], first[cut], second[cut]))
        begin = begin + count
    return scattered(entries, 128)


def rank_map(places, near_ref, base_ref, order_ref, step):
    at_high, at_low = places[0], places[1]
    row = lax.broadcasted_iota(I32, (128, 128), 0)
    lane = lax.broadcasted_iota(I32, (128, 128), 1)
    up_to = (row <= lane).astype(F32).astype(BF16)
    before = (row < lane).astype(F32).astype(BF16)
    below = (lane < row).astype(F32).astype(BF16)
    active = (at_high > 0.0).astype(F32)
    active16 = active.astype(BF16)
    so_far = jnp.dot(active16, up_to, preferred_element_type=F32)
    total = jnp.broadcast_to(so_far[:, 127:128], (128, 128))
    first = jnp.dot(below, total.astype(BF16), preferred_element_type=F32)
    rank = (first + so_far - active).astype(I32)
    near_ref[step] = jnp.where(active > 0.0, rank - (first.astype(I32) >> 7) * 128 + 1, 0)
    ones = jnp.ones((8, 128), F32).astype(BF16)
    totals = lax.dot_general(ones, active16, ADDED, preferred_element_type=F32)
    firsts = jnp.dot(totals.astype(BF16), before, preferred_element_type=F32).astype(I32)
    base_ref[step, 0] = firsts >> 7
    base_ref[step, 1] = firsts + totals.astype(I32)
    rank_high = jnp.where(active > 0.0, rank >> 7, 255).astype(F32)
    rank_low = (rank & 127).astype(F32)
    entries = []
    for b in range(BLOCKS):
        cut = slice(b, b + 1)
        entries.append((rank_high[cut], rank_low[cut], at_high[cut], at_low[cut]))
    order_ref[step] = scattered(entries, 64)


def own_stars(lists_ref, place):
    lane = lax.broadcasted_iota(I32, (8, 128), 1)
    sub = lax.broadcasted_iota(I32, (8, 128), 0)
    position = place * PART + (sub & 3) * 128 + lane
    before = jnp.zeros((8, 128), I32)
    which = jnp.zeros((8, 128), I32)
    start = jnp.zeros((8, 128), I32)
    for r in range(ROWS):
        count = jnp.where(sub < 4, spread(lists_ref[r, 16:17, :]), spread(lists_ref[r, 17:18, :]))
        end = before + count
        passed = position >= end
        which = which + passed.astype(I32)
        start = jnp.where(passed, end, start)
        before = end
    flat = which * CAP + position - start
    high, low = flat >> 7, flat & 127
    stars = jnp.zeros((8, 128), I32)
    for r in range(ROWS):
        for k in range(8):
            row = jnp.where(
                sub < 4, spread(lists_ref[r, k : k + 1, :]), spread(lists_ref[r, 8 + k : 9 + k, :])
            )
            stars = jnp.where(high == r * 8 + k, lane_pick(row, low), stars)
    return stars


def both_halves(x, step):
    part = x[4 * step : 4 * step + 4]
    return jnp.concatenate([part, part], axis=0)


def fetch(stars, pairs):
    high, low = stars >> 7, stars & 127

    def look(g, found):
        for u in range(8):
            b = g * 8 + u
            here = high == b
            found = tuple(
                jnp.where(here, lane_pick(pair(b), low), old) for pair, old in zip(pairs, found)
            )
        return found

    return lax.fori_loop(0, BLOCKS // 8, look, tuple(jnp.zeros((8, 128), F32) for _ in pairs))


def two_rows(sub, a, b):
    return jnp.where(sub < 4, spread(a), spread(b))


def unpack(pairs, out_ref):
    for p, pair in enumerate(pairs):
        for half in range(2):
            for s in range(4):
                out_ref[2 * p + half : 2 * p + half + 1, s * 128 : s * 128 + 128] = pair[
                    4 * half + s : 4 * half + s + 1
                ]


def predict(phase, derivs, time, now):
    d = now - time
    x, v, a, j = phase[0:3], phase[3:6], derivs[0:3], derivs[3:6]
    return x + d * (v + d * (a / 2.0 + d * j / 6.0)), v + d * (a + d * j / 2.0)


def correct(x, v, old_acc, old_jerk, h, forces):
    new_acc, new_jerk = forces[0:3], forces[3:6]
    change = old_acc - new_acc
    second = (-6.0 * change - h * (4.0 * old_jerk + 2.0 * new_jerk)) / (h * h)
    third = (12.0 * change + 6.0 * h * (old_jerk + new_jerk)) / (h * h * h)
    h2 = h * h
    h3 = h2 * h
    h4 = h3 * h
    h5 = h4 * h
    x = x + h4 / 24.0 * second + h5 / 120.0 * third
    v = v + h3 / 6.0 * second + h4 / 24.0 * third
    return x, v, new_acc, new_jerk


PAIRS = ((0, 0), (0, 1), (0, 2), (1, 0), (1, 1), (2, 0))


def split3(x):
    high = x.astype(BF16).astype(F32)
    rest = x - high
    middle = rest.astype(BF16).astype(F32)
    return high, middle, rest - middle


def split2(x):
    high = x.astype(BF16)
    return high, (x - high.astype(F32)).astype(BF16)


def squares(x, v):
    xx = x * x
    xv = x * v
    return xx[0:1] + xx[1:2] + xx[2:3], xv[0:1] + xv[1:2] + xv[2:3]


def star_features(x, v):
    width = x.shape[1]
    parts = split3(jnp.concatenate([x, v, jnp.zeros((2, width), F32)], axis=0))
    xx, xv = squares(x, v)
    one = jnp.ones((3, width), F32)
    extra = jnp.concatenate(list(split3(xx)) + list(split3(xv)) + [one, one, rows_of(12, 16, width)], axis=0)
    return jnp.concatenate([parts[a] for a, _ in PAIRS] + [extra], axis=0)


def active_features(x, v):
    width = x.shape[1]
    xp, vp = split3(x), split3(v)
    xx, xv = squares(x, v)
    one, none3, none5 = jnp.ones((3, width), F32), rows_of(0, 3, width), rows_of(0, 5, width)
    dist, both = [], []
    for _, b in PAIRS:
        dist += [-2.0 * xp[b], none5]
        both += [-vp[b], -xp[b], rows_of(0, 2, width)]
    dist += [one, none3] + list(split3(xx + softening)) + [none3, rows_of(12, 16, width)]
    both += [none3, one, none3] + list(split3(xv)) + [rows_of(12, 16, width)]
    return jnp.concatenate(dist, axis=0).astype(BF16), jnp.concatenate(both, axis=0).astype(BF16)


def prepare(first, chunk, count, pred_of, weights, features):
    def one_chunk(n, _):
        x, v, mass = pred_of(n)
        at = pl.ds(pl.multiple_of(first + n * chunk, chunk), chunk)
        ones, none = jnp.ones((1, chunk), F32), jnp.zeros((1, chunk), F32)
        scaled = split3(jnp.concatenate([x, v, ones, none], axis=0) * (mass / N_STARS))
        weights[:, at] = jnp.concatenate(list(scaled) + [rows_of(24, 32, chunk)], axis=0).astype(BF16)
        features[at, :] = star_features(x, v).T.astype(BF16)
        return 0

    lax.fori_loop(0, count, one_chunk, 0)


def force_sums(deep, weights, features, dist_own, both_own, w_sum, u_sum, own, part, after):
    def quarter(t, _):
        h = t >> 1
        cut = pl.ds(pl.multiple_of(h * HALF, HALF), HALF)
        fresh = (t & 1) == 0

        def sums(n, total):
            lanes = pl.ds(pl.multiple_of(((t & 1) * 2 + n) * deep, deep), deep)
            factor = features[lanes, :]
            dist = jnp.dot(factor, dist_own[:, cut], preferred_element_type=F32)
            both = jnp.dot(factor, both_own[:, cut], preferred_element_type=F32)
            inverse = lax.rsqrt(jnp.maximum(dist, softening))
            inverse_sq = inverse * inverse
            weight = inverse * inverse_sq
            radial = (weight * inverse_sq) * both
            w_high, w_low = split2(weight)
            u_high, u_low = split2(radial)
            dot = functools.partial(jnp.dot, weights[:, lanes], preferred_element_type=F32)
            return (total[0] + (dot(w_high) + dot(w_low)), total[1] + (dot(u_high) + dot(u_low)))

        w, u = lax.fori_loop(
            0, 2, sums, (jnp.where(fresh, 0.0, w_sum[...]), jnp.where(fresh, 0.0, u_sum[...]))
        )
        w_sum[...] = w
        u_sum[...] = u

        @pl.when((t & 1) == 1)
        def _():
            w_all = w[0:8] + w[8:16] + w[16:24]
            u_all = u[0:8] + u[8:16] + u[16:24]
            mine = own[:, cut]
            x, v = mine[0:3], mine[3:6]
            acc = w_all[0:3] - x * w_all[6:7]
            jerk = w_all[3:6] - v * w_all[6:7] - 3.0 * (u_all[0:3] - x * u_all[6:7])
            part[pl.ds(h, 1)] = jnp.concatenate([acc, jerk, jnp.zeros((2, HALF), F32)], axis=0)[None]

        for number, action in after.items():
            pl.when(t == number)(action)
        return 0

    lax.fori_loop(0, 4, quarter, 0)


def sum_of(landing):
    total = landing[0]
    for c in range(1, COLS):
        total = total + landing[c]
    return total


def packed(x, v, a, j):
    rest = jnp.concatenate([a[2:3], j], axis=0)
    right = jnp.concatenate([rest[:, 0:128], rest[:, 128:256]], axis=0)
    return jnp.concatenate([jnp.concatenate([x, v, a[0:2]], axis=0), right], axis=1)


def take_moved(high, low, sub, rows_at):
    def look(r, found):
        for k in range(4):
            here = high == r * 4 + k
            found = tuple(
                jnp.where(here, lane_pick(two_rows(sub, *pair), low), was)
                for pair, was in zip(rows_at(r, k), found)
            )
        return found

    return lax.fori_loop(0, ROWS, look, tuple(jnp.zeros((8, 128), F32) for _ in range(3)))


def steps_kernel(
    index_ref, count_ref, phase_far, derivs_far, time_far, mass_far,
    all0_ref, all1_ref, near_ref, base_ref, order_ref,
    phase_ref, derivs_ref, time_ref, mass_ref, lists_own, lists_ref, places,
    picks0, picks1, land0, land1, part0, part1, landf0, landf1, lead, lead_all, mine0, mine1,
    old, fix, own, accel, weights, features, dist_own, both_own, w_sum, u_sum,
    s_in, s_list, r_list, s_pick0, r_pick0, s_pick1, r_pick1, s_for, r_for, s_lead, r_lead, s_all, r_all,
):
    row, col = lax.axis_index("row"), lax.axis_index("col")
    barrier = pltpu.get_barrier_semaphore()
    everyone = partners_of("row", ROWS, row) + partners_of("col", COLS, col)
    for _, partner in everyone:
        pl.semaphore_signal(barrier, inc=1, device_id=partner, device_id_type=MESH)
    inputs = [
        pltpu.make_async_copy(far, near, s_in.at[n])
        for n, (far, near) in enumerate(
            [(phase_far, phase_ref), (derivs_far, derivs_ref), (time_far, time_ref), (mass_far, mass_ref)]
        )
    ]
    for copy in inputs:
        copy.start()
    offset = col * LOCAL
    chunk = 2048
    sub = lax.broadcasted_iota(I32, (8, 128), 0)
    for step in range(2):
        for k in range(8):
            lists_own[8 * step + k : 8 * step + k + 1, :] = index_ref[step, 0:1, k * 128 : k * 128 + 128]
        lists_own[16 + step : 17 + step, :] = jnp.broadcast_to(count_ref[0:1, step : step + 1], (1, 128))
    lists_own[18:24, :] = jnp.zeros((6, 128), I32)
    pl.semaphore_wait(barrier, len(everyone))
    lists = ("row", ROWS, row, lists_own, lists_ref, s_list, r_list)
    exchange(*lists)
    for copy in inputs:
        copy.wait()

    def first_stars(n):
        lanes = pl.ds(pl.multiple_of(n * chunk, chunk), chunk)
        x, v = predict(phase_ref[:, lanes], derivs_ref[:, lanes], time_ref[:, lanes], block_times[0])
        return x, v, mass_ref[:, lanes]

    prepare(0, chunk, LOCAL // chunk, first_stars, weights, features)
    arrived(*lists)

    def block(b):
        return pl.ds(pl.multiple_of(b * 128, 128), 128)

    pairs = [
        lambda b, ref=ref, c=c: two_rows(sub, ref[c : c + 1, block(b)], ref[c + 1 : c + 2, block(b)])
        for ref in (phase_ref, derivs_ref)
        for c in (0, 2, 4)
    ]
    pairs.append(lambda b: two_rows(sub, time_ref[:, block(b)], mass_ref[:, block(b)]))
    local = own_stars(lists_ref, row) - offset
    for p, value in enumerate(fetch(both_halves(local, 0), pairs)):
        picks0[p] = value
    first_picks = ("col", COLS, col, picks0, land0, s_pick0, r_pick0)
    exchange(*first_picks)

    found = place_map(lists_ref, 0, offset)
    places[0, 0], places[0, 1] = found[:, 0:128], found[:, 128:256]
    pairs.append(lambda b: two_rows(sub, places[0, 0, pl.ds(b, 1), :], places[0, 1, pl.ds(b, 1), :]))
    for p, value in enumerate(fetch(both_halves(local, 1), pairs)):
        picks1[p] = value
    second_picks = ("col", COLS, col, picks1, land1, s_pick1, r_pick1)
    exchange(*second_picks)

    arrived(*first_picks)
    total = sum_of(land0)
    unpack([total[p] for p in range(7)], old)
    def force_copies(step, half):
        part, landing = (part0, landf0) if step == 0 else (part1, landf1)
        n = 2 * step + half
        return ("col", COLS, col, part.at[half], landing.at[half], s_for.at[n], r_for.at[n])

    def lead_copies(half):
        return ("row", ROWS, row, lead.at[half], lead_all.at[half], s_lead.at[half], r_lead.at[half])

    def row_copies(step, half):
        mine, landing = (mine0, all0_ref) if step == 0 else (mine1, all1_ref)
        n = 2 * step + half
        return ("row", ROWS, row, mine.at[half], landing.at[half], s_all.at[n], r_all.at[n])

    def set_own(x, v):
        own[...] = jnp.concatenate([x, v, jnp.zeros((2, PART), F32)], axis=0)
        dist_own[...], both_own[...] = active_features(x, v)

    sums = (weights, features, dist_own, both_own, w_sum, u_sum, own)
    set_own(*predict(old[0:6], old[6:12], old[12:13], block_times[0]))

    def first_corrected(half):
        arrived(*force_copies(0, half))
        cut = slice(half * HALF, half * HALF + HALF)
        x, v, a, j = correct(
            own[0:3, cut], own[3:6, cut], old[6:9, cut], old[9:12, cut],
            block_times[0] - old[12:13, cut], sum_of(landf0.at[half]),
        )
        x_next, v_next = predict(
            jnp.concatenate([x, v], axis=0), jnp.concatenate([a, j], axis=0), block_times[0], block_times[1]
        )
        lead[half] = jnp.concatenate([x_next, v_next, old[13:14, cut], jnp.zeros((1, HALF), F32)], axis=0)
        exchange(*lead_copies(half))
        mine0[half] = packed(x, v, a, j)
        exchange(*row_copies(0, half))

    force_sums(
        4096, *sums, part0,
        {1: lambda: exchange(*force_copies(0, 0)), 2: lambda: first_corrected(0)},
    )
    exchange(*force_copies(0, 1))
    found = place_map(lists_ref, 1, offset)
    places[1, 0], places[1, 1] = found[:, 0:128], found[:, 128:256]
    first_corrected(1)

    def second_stars(n):
        lanes = pl.ds(pl.multiple_of(n * chunk, chunk), chunk)
        x, v = predict(phase_ref[:, lanes], derivs_ref[:, lanes], time_ref[:, lanes], block_times[1])
        moved = jnp.concatenate([places[0, 0, pl.ds(n * 16 + k, 1), :] for k in range(16)], axis=1)
        return x, v, jnp.where(moved > 0.0, 0.0, mass_ref[:, lanes])

    prepare(0, chunk, LOCAL // chunk, second_stars, weights, features)
    rank_map(places[0], near_ref, base_ref, order_ref, 0)
    arrived(*second_picks)
    total = sum_of(land1)
    unpack([total[p] for p in range(8)], old)
    high = both_halves(total[7], 0).astype(I32) - 1
    low = both_halves(total[7], 1).astype(I32)
    for half in range(2):
        arrived(*lead_copies(half))

    def moved_stars(n):
        state = lead_all[pl.ds(n & 1, 1), pl.ds(2 * col + (n >> 1), 1)][0, 0]
        return state[0:3], state[3:6], state[6:7]

    prepare(LOCAL, HALF, 4, moved_stars, weights, features)

    def lead_rows(r, k):
        cut = slice((k % 2) * 128, (k % 2) * 128 + 128)
        return [(lead_all[k // 2, r, c : c + 1, cut], lead_all[k // 2, r, c + 1 : c + 2, cut]) for c in (0, 2, 4)]

    unpack(take_moved(high, low, sub, lead_rows), fix)
    moved = old[14:15] > 0.0
    x_own, v_own = predict(old[0:6], old[6:12], old[12:13], block_times[1])
    set_own(jnp.where(moved, fix[0:3], x_own), jnp.where(moved, fix[3:6], v_own))

    def rest_rows(r, k):
        half, at = k // 2, 4 * (k % 2)
        cut = slice((k % 2) * 128, (k % 2) * 128 + 128)
        return [
            (all0_ref[half, r, 6:7, cut], all0_ref[half, r, 7:8, cut]),
            (all0_ref[half, r, at : at + 1, 256:384], all0_ref[half, r, at + 1 : at + 2, 256:384]),
            (all0_ref[half, r, at + 2 : at + 3, 256:384], all0_ref[half, r, at + 3 : at + 4, 256:384]),
        ]

    def second_old():
        exchange(*force_copies(1, 0))
        for half in range(2):
            arrived(*row_copies(0, half))
        unpack(take_moved(high, low, sub, rest_rows), fix)
        moved = old[14:15] > 0.0
        h = block_times[1] - jnp.where(moved, block_times[0], old[12:13])
        accel[...] = jnp.concatenate(
            [jnp.where(moved, fix[0:3], old[6:9]), jnp.where(moved, fix[3:6], old[9:12]), h, h], axis=0
        )

    def second_corrected(half):
        arrived(*force_copies(1, half))
        cut = slice(half * HALF, half * HALF + HALF)
        mine1[half] = packed(
            *correct(
                own[0:3, cut], own[3:6, cut], accel[0:3, cut], accel[3:6, cut], accel[6:7, cut],
                sum_of(landf1.at[half]),
            )
        )
        exchange(*row_copies(1, half))

    force_sums(
        (LOCAL + 2 * PART) // 4, *sums, part1, {1: second_old, 2: lambda: second_corrected(0)}
    )
    exchange(*force_copies(1, 1))
    rank_map(places[1], near_ref, base_ref, order_ref, 1)
    second_corrected(1)
    for half in range(2):
        arrived(*row_copies(1, half))
    for copies in [lists, first_picks, second_picks]:
        sent(*copies)
    for half in range(2):
        sent(*lead_copies(half))
        for step in range(2):
            sent(*force_copies(step, half))
            sent(*row_copies(step, half))


def both_steps(index, count, phase, derivs, time, masses):
    stars = LOCAL + 2 * PART
    vmem = [
        ((6, LOCAL), F32),
        ((6, LOCAL), F32),
        ((1, LOCAL), F32),
        ((1, LOCAL), F32),
        ((24, 128), I32),
        ((ROWS, 24, 128), I32),
        ((2, 2, 128, 128), F32),
        ((7, 8, 128), F32),
        ((8, 8, 128), F32),
        ((COLS, 7, 8, 128), F32),
        ((COLS, 8, 8, 128), F32),
        ((2, 8, HALF), F32),
        ((2, 8, HALF), F32),
        ((2, COLS, 8, HALF), F32),
        ((2, COLS, 8, HALF), F32),
        ((2, 8, HALF), F32),
        ((2, ROWS, 8, HALF), F32),
        ((2, 8, 384), F32),
        ((2, 8, 384), F32),
        ((16, PART), F32),
        ((8, PART), F32),
        ((8, PART), F32),
        ((8, PART), F32),
        ((32, stars), BF16),
        ((stars, 64), BF16),
        ((64, PART), BF16),
        ((64, PART), BF16),
        ((32, HALF), F32),
        ((32, HALF), F32),
    ]
    sems = [(4,)] + [(ROWS,)] * 2 + [(COLS,)] * 4 + [(4, COLS)] * 2 + [(2, ROWS)] * 2 + [(4, ROWS)] * 2
    return pl.pallas_call(
        steps_kernel,
        out_shape=[
            jax.ShapeDtypeStruct((2, ROWS, 8, 384), F32),
            jax.ShapeDtypeStruct((2, ROWS, 8, 384), F32),
            jax.ShapeDtypeStruct((2, 128, 128), I32),
            jax.ShapeDtypeStruct((2, 2, 8, 128), I32),
            jax.ShapeDtypeStruct((2, 64, 256), F32),
        ],
        in_specs=in_vmem(2) + [pl.BlockSpec(memory_space=pl.ANY)] * 4,
        out_specs=in_vmem(5),
        scratch_shapes=[pltpu.VMEM(shape, kind) for shape, kind in vmem]
        + [pltpu.SemaphoreType.DMA(shape) for shape in sems],
        compiler_params=params(collective_id=0, has_side_effects=True),
        name="both_steps",
    )(index, count, phase, derivs, time, masses)


def collect(step, count, order_ref, all_ref, sorted_ref):
    def one_block(n, _):
        group = order_ref[step, pl.ds(pl.multiple_of((n >> 3) * 8, 8), 8), :]
        mask = lax.broadcasted_iota(I32, (8, 256), 0) == (n & 7)
        digits = jnp.sum(jnp.where(mask, group, 0.0), axis=0, keepdims=True)
        high = spread(digits[:, 0:128]).astype(I32) - 1
        low = spread(digits[:, 128:256]).astype(I32)
        upper = jnp.zeros((8, 128), F32)
        lower = jnp.zeros((8, 128), F32)
        shifted = high - (lax.broadcasted_iota(I32, (8, 128), 0) >> 2)
        for b in range(64):
            r, half, k = b // 4, (b % 4) // 2, b % 2
            upper = jnp.where(high == b, lane_pick(all_ref[half, r, :, k * 128 : k * 128 + 128], low), upper)
            if k == 0:
                lower = jnp.where(shifted == b, lane_pick(all_ref[half, r, :, 256:384], low), lower)
        blank = jnp.zeros((2, 128), F32)
        rest = lower[0:4] + lower[4:8]
        sorted_ref[step, n, 0:8, :] = upper
        sorted_ref[step, n, 8:16, :] = jnp.concatenate([upper[6:8], rest, blank], axis=0)
        return 0

    lax.fori_loop(0, (count + 127) // 128, one_block, 0)


def last_kernel(
    base_ref, near_ref, order_ref, all0_ref, all1_ref, phase_ref, derivs_ref, time_ref,
    phase_out, derivs_out, time_out, sorted_ref,
):
    collect(0, base_ref[0, 1, 0, 127], order_ref, all0_ref, sorted_ref)
    collect(1, base_ref[1, 1, 0, 127], order_ref, all1_ref, sorted_ref)

    def put(g, _):
        for u in range(8):
            b = g * 8 + u
            lanes = pl.ds(pl.multiple_of(b * 128, 128), 128)
            blank = jnp.zeros((2, 128), F32)
            phase = jnp.concatenate([phase_ref[:, lanes], blank], axis=0)
            derivs = jnp.concatenate([derivs_ref[:, lanes], blank], axis=0)
            time = time_ref[:, lanes]
            for step in range(2):
                n = jnp.minimum(base_ref[step, 0, 0, b], 63)
                m = jnp.minimum(n + 1, 63)
                at = spread(near_ref[step, pl.ds(b, 1), :]) - 1
                low = at & 127
                is_first = (at >= 0) & (at < 128)
                is_next = at >= 128

                def chosen(rows, was):
                    new = jnp.where(is_first, lane_pick(sorted_ref[step, n, rows, :], low), was)
                    return jnp.where(is_next, lane_pick(sorted_ref[step, m, rows, :], low), new)

                phase = chosen(slice(0, 8), phase)
                derivs = chosen(slice(8, 16), derivs)
                time = jnp.where(at[0:1] >= 0, block_times[step], time)
            phase_out[:, lanes] = phase[0:6]
            derivs_out[:, lanes] = derivs[0:6]
            time_out[:, lanes] = time
        return 0

    lax.fori_loop(0, BLOCKS // 8, put, 0)


def last_update(base, near, order, all0, all1, phase, derivs, time):
    return pl.pallas_call(
        last_kernel,
        out_shape=[
            jax.ShapeDtypeStruct((6, LOCAL), F32),
            jax.ShapeDtypeStruct((6, LOCAL), F32),
            jax.ShapeDtypeStruct((1, LOCAL), F32),
        ],
        in_specs=[pl.BlockSpec(memory_space=pltpu.SMEM)] + in_vmem(7),
        out_specs=in_vmem(3),
        scratch_shapes=[pltpu.VMEM((2, 64, 16, 128), F32)],
        compiler_params=params(),
        name="last_update",
    )(base, near, order, all0, all1, phase, derivs, time)


def body(phase_space, derivs, star_time, masses, active_index, active_count):
    time = star_time.reshape(1, LOCAL)
    masses = masses.reshape(1, LOCAL)
    all0, all1, near, base, order = both_steps(
        active_index, active_count.reshape(1, 2), phase_space, derivs, time, masses
    )
    phase_space, derivs, time = last_update(base, near, order, all0, all1, phase_space, derivs, time)
    return phase_space, derivs, time.reshape(LOCAL)


def solution(mesh):
    return jax.shard_map(
        body,
        mesh=mesh,
        in_specs=(
            P(None, "col"),
            P(None, "col"),
            P("col"),
            P("col"),
            P(None, "row", None),
            P(None, "row"),
        ),
        out_specs=(P(None, "col"), P(None, "col"), P("col")),
        check_vma=False,
    )
```

```python
import functools

import jax
import jax.numpy as jnp
from jax import lax
from jax.experimental import pallas as pl
from jax.experimental.pallas import tpu as pltpu
from jax.sharding import PartitionSpec as P

F32 = jnp.float32
BF16 = jnp.bfloat16
I32 = jnp.int32
FINE8 = jnp.float8_e4m3fn
WIDE8 = jnp.float8_e5m2
DIST_SCALE = 2.0**-4
BOTH_SCALE = 2.0**-10
WEIGHT_BACK = 2.0**-6
softening = 0.01
block_times = (0.125, 0.25)
ROWS = 16
COLS = 8
CAP = 1024
PART = 512
HALF = 256
LOCAL = 16384
BLOCKS = LOCAL // 128
N_STARS = ROWS * PART * 16
MESH = pl.DeviceIdType.MESH
ADDED = (((1,), (1,)), ((), ()))


def rows_of(first, last, width):
    return jnp.zeros((last - first, width), F32)


def in_vmem(n):
    return [pl.BlockSpec(memory_space=pltpu.VMEM)] * n


def params(**more):
    return pltpu.CompilerParams(vmem_limit_bytes=56 * 2**20, **more)


def partners_of(axis, size, place):
    return [(k, {axis: lax.rem(place + k, size)}) for k in range(1, size)]


def exchange(axis, size, place, source, landing, send_sem, recv_sem):
    for k, partner in partners_of(axis, size, place):
        pltpu.make_async_remote_copy(
            src_ref=source,
            dst_ref=landing.at[place],
            send_sem=send_sem.at[k],
            recv_sem=recv_sem.at[place],
            device_id=partner,
            device_id_type=MESH,
        ).start()
    landing[pl.ds(place, 1)] = source[...][None]


def sent(axis, size, place, source, landing, send_sem, recv_sem):
    for k, partner in partners_of(axis, size, place):
        pltpu.make_async_remote_copy(
            src_ref=source,
            dst_ref=landing.at[place],
            send_sem=send_sem.at[k],
            recv_sem=recv_sem.at[place],
            device_id=partner,
            device_id_type=MESH,
        ).wait_send()


def arrived(axis, size, place, source, landing, send_sem, recv_sem):
    for k, partner in partners_of(axis, size, place):
        slot = lax.rem(place + k, size)
        pltpu.make_async_remote_copy(
            src_ref=source,
            dst_ref=landing.at[slot],
            send_sem=send_sem.at[k],
            recv_sem=recv_sem.at[slot],
            device_id=partner,
            device_id_type=MESH,
        ).wait_recv()


def lane_pick(table, lanes):
    return jnp.take_along_axis(table, lanes, axis=1, mode="promise_in_bounds")


def spread(row):
    return jnp.broadcast_to(row, (8, 128))


def hot(index_row, count):
    kinds = lax.broadcasted_iota(I32, (count, 128), 0).astype(F32).astype(BF16)
    return jnp.broadcast_to(index_row, (count, 128)).astype(BF16) == kinds


def scattered(entries, high_count):
    one, zero = jnp.ones((), BF16), jnp.zeros((), BF16)
    left, right = [], []
    for high, low, first, second in entries:
        left.append(jnp.where(hot(high, high_count), one, zero))
        at_low = hot(low, 128)
        a = jnp.broadcast_to(first, (128, 128)).astype(BF16)
        b = jnp.broadcast_to(second, (128, 128)).astype(BF16)
        right.append(jnp.concatenate([jnp.where(at_low, a, zero), jnp.where(at_low, b, zero)], axis=0))
    return lax.dot_general(
        jnp.concatenate(left, axis=1), jnp.concatenate(right, axis=1), ADDED, preferred_element_type=F32
    )


def place_map(lists_ref, step, offset):
    slot = lax.broadcasted_iota(I32, (8, 128), 0) * 128 + lax.broadcasted_iota(I32, (8, 128), 1)
    begin = jnp.zeros((8, 128), I32)
    entries = []
    for r in range(ROWS):
        count = spread(lists_ref[r, 16 + step : 17 + step, :])
        star = lists_ref[r, 8 * step : 8 * step + 8, :] - offset
        live = (slot < count) & (star >= 0) & (star < LOCAL)
        at = begin + slot
        high = jnp.where(live, star >> 7, 255).astype(F32)
        low = (star & 127).astype(F32)
        first, second = ((at >> 7) + 1).astype(F32), (at & 127).astype(F32)
        for k in range(8):
            cut = slice(k, k + 1)
            entries.append((high[cut], low[cut], first[cut], second[cut]))
        begin = begin + count
    return scattered(entries, 128)


def rank_map(places, near_ref, base_ref, order_ref, step):
    at_high, at_low = places[0], places[1]
    row = lax.broadcasted_iota(I32, (128, 128), 0)
    lane = lax.broadcasted_iota(I32, (128, 128), 1)
    up_to = (row <= lane).astype(F32).astype(BF16)
    before = (row < lane).astype(F32).astype(BF16)
    below = (lane < row).astype(F32).astype(BF16)
    active = (at_high > 0.0).astype(F32)
    active16 = active.astype(BF16)
    so_far = jnp.dot(active16, up_to, preferred_element_type=F32)
    total = jnp.broadcast_to(so_far[:, 127:128], (128, 128))
    first = jnp.dot(below, total.astype(BF16), preferred_element_type=F32)
    rank = (first + so_far - active).astype(I32)
    near_ref[step] = jnp.where(active > 0.0, rank - (first.astype(I32) >> 7) * 128 + 1, 0)
    ones = jnp.ones((8, 128), F32).astype(BF16)
    totals = lax.dot_general(ones, active16, ADDED, preferred_element_type=F32)
    firsts = jnp.dot(totals.astype(BF16), before, preferred_element_type=F32).astype(I32)
    base_ref[step, 0] = firsts >> 7
    base_ref[step, 1] = firsts + totals.astype(I32)
    rank_high = jnp.where(active > 0.0, rank >> 7, 255).astype(F32)
    rank_low = (rank & 127).astype(F32)
    entries = []
    for b in range(BLOCKS):
        cut = slice(b, b + 1)
        entries.append((rank_high[cut], rank_low[cut], at_high[cut], at_low[cut]))
    order_ref[step] = scattered(entries, 64)


def own_stars(lists_ref, place):
    lane = lax.broadcasted_iota(I32, (8, 128), 1)
    sub = lax.broadcasted_iota(I32, (8, 128), 0)
    position = place * PART + (sub & 3) * 128 + lane
    before = jnp.zeros((8, 128), I32)
    which = jnp.zeros((8, 128), I32)
    start = jnp.zeros((8, 128), I32)
    for r in range(ROWS):
        count = jnp.where(sub < 4, spread(lists_ref[r, 16:17, :]), spread(lists_ref[r, 17:18, :]))
        end = before + count
        passed = position >= end
        which = which + passed.astype(I32)
        start = jnp.where(passed, end, start)
        before = end
    flat = which * CAP + position - start
    high, low = flat >> 7, flat & 127
    stars = jnp.zeros((8, 128), I32)
    for r in range(ROWS):
        for k in range(8):
            row = jnp.where(
                sub < 4, spread(lists_ref[r, k : k + 1, :]), spread(lists_ref[r, 8 + k : 9 + k, :])
            )
            stars = jnp.where(high == r * 8 + k, lane_pick(row, low), stars)
    return stars


def both_halves(x, step):
    part = x[4 * step : 4 * step + 4]
    return jnp.concatenate([part, part], axis=0)


def fetch(stars, pairs):
    high, low = stars >> 7, stars & 127

    def look(g, found):
        for u in range(8):
            b = g * 8 + u
            here = high == b
            found = tuple(
                jnp.where(here, lane_pick(pair(b), low), old) for pair, old in zip(pairs, found)
            )
        return found

    return lax.fori_loop(0, BLOCKS // 8, look, tuple(jnp.zeros((8, 128), F32) for _ in pairs))


def two_rows(sub, a, b):
    return jnp.where(sub < 4, spread(a), spread(b))


def unpack(pairs, out_ref):
    for p, pair in enumerate(pairs):
        for half in range(2):
            for s in range(4):
                out_ref[2 * p + half : 2 * p + half + 1, s * 128 : s * 128 + 128] = pair[
                    4 * half + s : 4 * half + s + 1
                ]


def predict(phase, derivs, time, now):
    d = now - time
    x, v, a, j = phase[0:3], phase[3:6], derivs[0:3], derivs[3:6]
    return x + d * (v + d * (a / 2.0 + d * j / 6.0)), v + d * (a + d * j / 2.0)


def correct(x, v, old_acc, old_jerk, h, forces):
    new_acc, new_jerk = forces[0:3], forces[3:6]
    change = old_acc - new_acc
    second = (-6.0 * change - h * (4.0 * old_jerk + 2.0 * new_jerk)) / (h * h)
    third = (12.0 * change + 6.0 * h * (old_jerk + new_jerk)) / (h * h * h)
    h2 = h * h
    h3 = h2 * h
    h4 = h3 * h
    h5 = h4 * h
    x = x + h4 / 24.0 * second + h5 / 120.0 * third
    v = v + h3 / 6.0 * second + h4 / 24.0 * third
    return x, v, new_acc, new_jerk


PAIRS = ((0, 0), (0, 1), (0, 2), (1, 0), (1, 1), (2, 0))


def split3(x):
    high = x.astype(BF16).astype(F32)
    rest = x - high
    middle = rest.astype(BF16).astype(F32)
    return high, middle, rest - middle


def split2(x, low_kind):
    high = x.astype(BF16)
    return high, (x - high.astype(F32)).astype(low_kind)


def split8(x):
    parts = []
    for _ in range(4):
        parts.append(x.astype(FINE8).astype(F32))
        x = x - parts[-1]
    return parts


def squares(x, v):
    xx = x * x
    xv = x * v
    return xx[0:1] + xx[1:2] + xx[2:3], xv[0:1] + xv[1:2] + xv[2:3]


def star_features(x, v):
    width = x.shape[1]
    parts = split3(jnp.concatenate([x, v, jnp.zeros((2, width), F32)], axis=0))
    xx, xv = squares(x, v)
    one = jnp.ones((3, width), F32)
    extra = jnp.concatenate(list(split3(xx)) + list(split3(xv)) + [one, one, rows_of(12, 16, width)], axis=0)
    return jnp.concatenate([parts[a] for a, _ in PAIRS] + [extra], axis=0)


def active_features(x, v):
    width = x.shape[1]
    xp, vp = split3(x), split3(v)
    xx, xv = squares(x, v)
    one, none3, none5 = jnp.ones((3, width), F32), rows_of(0, 3, width), rows_of(0, 5, width)
    dist, both = [], []
    for _, b in PAIRS:
        dist += [-2.0 * xp[b], none5]
        both += [-vp[b], -xp[b], rows_of(0, 2, width)]
    dist += [one, none3] + list(split3(xx + softening)) + [none3, rows_of(12, 16, width)]
    both += [none3, one, none3] + list(split3(xv)) + [rows_of(12, 16, width)]
    dist = jnp.concatenate(dist, axis=0) * DIST_SCALE
    both = jnp.concatenate(both, axis=0) * BOTH_SCALE
    return dist.astype(BF16), both.astype(BF16)


def prepare(first, chunk, count, pred_of, weights, weights8, features):
    def one_chunk(n, _):
        x, v, mass = pred_of(n)
        at = pl.ds(pl.multiple_of(first + n * chunk, chunk), chunk)
        ones, none = jnp.ones((1, chunk), F32), jnp.zeros((1, chunk), F32)
        scaled = jnp.concatenate([x, v, ones, none], axis=0) * mass
        parts = list(split3(scaled / N_STARS)) + [rows_of(24, 32, chunk)]
        weights[:, at] = jnp.concatenate(parts, axis=0).astype(BF16)
        weights8[:, at] = jnp.concatenate(split8(jnp.clip(scaled, -240.0, 240.0)), axis=0).astype(FINE8)
        features[at, :] = star_features(x, v).T.astype(BF16)
        return 0

    lax.fori_loop(0, count, one_chunk, 0)


def force_sums(deep, weights, weights8, features, dist_own, both_own, totals, own, part, after):
    def quarter(t, _):
        h = t >> 1
        cut = pl.ds(pl.multiple_of(h * HALF, HALF), HALF)
        fresh = (t & 1) == 0

        def sums(n, total):
            lanes = pl.ds(pl.multiple_of(((t & 1) * 2 + n) * deep, deep), deep)
            factor = features[lanes, :]
            dist = jnp.dot(factor, dist_own[:, cut], preferred_element_type=F32)
            both = jnp.dot(factor, both_own[:, cut], preferred_element_type=F32)
            inverse = lax.rsqrt(jnp.maximum(dist, softening * DIST_SCALE))
            inverse_sq = inverse * inverse
            weight = inverse * inverse_sq
            radial = (weight * inverse_sq) * both
            w_high, w_low = split2(weight, FINE8)
            u_high, u_low = split2(radial, WIDE8)
            dot = functools.partial(jnp.dot, preferred_element_type=F32)
            left, left8 = weights[:, lanes], weights8[:, lanes]
            new = dot(left, w_high), dot(left, u_high), dot(left8, w_low), dot(left8, u_low)
            return tuple(a + b for a, b in zip(total, new))

        found = lax.fori_loop(0, 2, sums, tuple(jnp.where(fresh, 0.0, totals[n]) for n in range(4)))
        for n in range(4):
            totals[n] = found[n]

        @pl.when((t & 1) == 1)
        def _():
            def whole(high, low, back):
                high = high[0:8] + high[8:16] + high[16:24]
                low = low[0:8] + low[8:16] + low[16:24] + low[24:32]
                return (high + low / N_STARS) * back

            w_all = whole(found[0], found[2], WEIGHT_BACK)
            u_all = whole(found[1], found[3], 1.0)
            mine = own[:, cut]
            x, v = mine[0:3], mine[3:6]
            acc = w_all[0:3] - x * w_all[6:7]
            jerk = w_all[3:6] - v * w_all[6:7] - 3.0 * (u_all[0:3] - x * u_all[6:7])
            part[pl.ds(h, 1)] = jnp.concatenate([acc, jerk, jnp.zeros((2, HALF), F32)], axis=0)[None]

        for number, action in after.items():
            pl.when(t == number)(action)
        return 0

    lax.fori_loop(0, 4, quarter, 0)


def sum_of(landing):
    total = landing[0]
    for c in range(1, COLS):
        total = total + landing[c]
    return total


def packed(x, v, a, j):
    rest = jnp.concatenate([a[2:3], j], axis=0)
    right = jnp.concatenate([rest[:, 0:128], rest[:, 128:256]], axis=0)
    return jnp.concatenate([jnp.concatenate([x, v, a[0:2]], axis=0), right], axis=1)


def take_moved(high, low, sub, rows_at):
    def look(r, found):
        for k in range(4):
            here = high == r * 4 + k
            found = tuple(
                jnp.where(here, lane_pick(two_rows(sub, *pair), low), was)
                for pair, was in zip(rows_at(r, k), found)
            )
        return found

    return lax.fori_loop(0, ROWS, look, tuple(jnp.zeros((8, 128), F32) for _ in range(3)))


def steps_kernel(
    index_ref, count_ref, phase_far, derivs_far, time_far, mass_far,
    all0_ref, all1_ref, near_ref, base_ref, order_ref,
    phase_ref, derivs_ref, time_ref, mass_ref, lists_own, lists_ref, places,
    picks0, picks1, land0, land1, part0, part1, landf0, landf1, lead, lead_all, mine0, mine1,
    old, fix, own, accel, weights, weights8, features, dist_own, both_own, totals,
    s_in, s_list, r_list, s_pick0, r_pick0, s_pick1, r_pick1, s_for, r_for, s_lead, r_lead, s_all, r_all,
):
    row, col = lax.axis_index("row"), lax.axis_index("col")
    barrier = pltpu.get_barrier_semaphore()
    everyone = partners_of("row", ROWS, row) + partners_of("col", COLS, col)
    for _, partner in everyone:
        pl.semaphore_signal(barrier, inc=1, device_id=partner, device_id_type=MESH)
    inputs = [
        pltpu.make_async_copy(far, near, s_in.at[n])
        for n, (far, near) in enumerate(
            [(phase_far, phase_ref), (derivs_far, derivs_ref), (time_far, time_ref), (mass_far, mass_ref)]
        )
    ]
    for copy in inputs:
        copy.start()
    offset = col * LOCAL
    chunk = 2048
    sub = lax.broadcasted_iota(I32, (8, 128), 0)
    for step in range(2):
        for k in range(8):
            lists_own[8 * step + k : 8 * step + k + 1, :] = index_ref[step, 0:1, k * 128 : k * 128 + 128]
        lists_own[16 + step : 17 + step, :] = jnp.broadcast_to(count_ref[0:1, step : step + 1], (1, 128))
    lists_own[18:24, :] = jnp.zeros((6, 128), I32)
    pl.semaphore_wait(barrier, len(everyone))
    lists = ("row", ROWS, row, lists_own, lists_ref, s_list, r_list)
    exchange(*lists)
    for copy in inputs:
        copy.wait()

    def first_stars(n):
        lanes = pl.ds(pl.multiple_of(n * chunk, chunk), chunk)
        x, v = predict(phase_ref[:, lanes], derivs_ref[:, lanes], time_ref[:, lanes], block_times[0])
        return x, v, mass_ref[:, lanes]

    prepare(0, chunk, LOCAL // chunk, first_stars, weights, weights8, features)
    arrived(*lists)

    def block(b):
        return pl.ds(pl.multiple_of(b * 128, 128), 128)

    pairs = [
        lambda b, ref=ref, c=c: two_rows(sub, ref[c : c + 1, block(b)], ref[c + 1 : c + 2, block(b)])
        for ref in (phase_ref, derivs_ref)
        for c in (0, 2, 4)
    ]
    pairs.append(lambda b: two_rows(sub, time_ref[:, block(b)], mass_ref[:, block(b)]))
    local = own_stars(lists_ref, row) - offset
    for p, value in enumerate(fetch(both_halves(local, 0), pairs)):
        picks0[p] = value
    first_picks = ("col", COLS, col, picks0, land0, s_pick0, r_pick0)
    exchange(*first_picks)

    found = place_map(lists_ref, 0, offset)
    places[0, 0], places[0, 1] = found[:, 0:128], found[:, 128:256]

    arrived(*first_picks)
    total = sum_of(land0)
    unpack([total[p] for p in range(7)], old)
    def force_copies(step, half):
        part, landing = (part0, landf0) if step == 0 else (part1, landf1)
        n = 2 * step + half
        return ("col", COLS, col, part.at[half], landing.at[half], s_for.at[n], r_for.at[n])

    def lead_copies(half):
        return ("row", ROWS, row, lead.at[half], lead_all.at[half], s_lead.at[half], r_lead.at[half])

    def row_copies(step, half):
        mine, landing = (mine0, all0_ref) if step == 0 else (mine1, all1_ref)
        n = 2 * step + half
        return ("row", ROWS, row, mine.at[half], landing.at[half], s_all.at[n], r_all.at[n])

    def set_own(x, v):
        own[...] = jnp.concatenate([x, v, jnp.zeros((2, PART), F32)], axis=0)
        dist_own[...], both_own[...] = active_features(x, v)

    sums = (weights, weights8, features, dist_own, both_own, totals, own)
    set_own(*predict(old[0:6], old[6:12], old[12:13], block_times[0]))

    def first_corrected(half):
        arrived(*force_copies(0, half))
        cut = slice(half * HALF, half * HALF + HALF)
        x, v, a, j = correct(
            own[0:3, cut], own[3:6, cut], old[6:9, cut], old[9:12, cut],
            block_times[0] - old[12:13, cut], sum_of(landf0.at[half]),
        )
        x_next, v_next = predict(
            jnp.concatenate([x, v], axis=0), jnp.concatenate([a, j], axis=0), block_times[0], block_times[1]
        )
        lead[half] = jnp.concatenate([x_next, v_next, old[13:14, cut], jnp.zeros((1, HALF), F32)], axis=0)
        exchange(*lead_copies(half))
        mine0[half] = packed(x, v, a, j)
        exchange(*row_copies(0, half))

    force_sums(
        4096, *sums, part0,
        {1: lambda: exchange(*force_copies(0, 0)), 2: lambda: first_corrected(0)},
    )
    exchange(*force_copies(0, 1))
    pairs.append(lambda b: two_rows(sub, places[0, 0, pl.ds(b, 1), :], places[0, 1, pl.ds(b, 1), :]))
    for p, value in enumerate(fetch(both_halves(local, 1), pairs)):
        picks1[p] = value
    second_picks = ("col", COLS, col, picks1, land1, s_pick1, r_pick1)
    exchange(*second_picks)
    first_corrected(1)

    def second_stars(n):
        lanes = pl.ds(pl.multiple_of(n * chunk, chunk), chunk)
        x, v = predict(phase_ref[:, lanes], derivs_ref[:, lanes], time_ref[:, lanes], block_times[1])
        moved = jnp.concatenate([places[0, 0, pl.ds(n * 16 + k, 1), :] for k in range(16)], axis=1)
        return x, v, jnp.where(moved > 0.0, 0.0, mass_ref[:, lanes])

    prepare(0, chunk, LOCAL // chunk, second_stars, weights, weights8, features)
    arrived(*second_picks)
    total = sum_of(land1)
    unpack([total[p] for p in range(8)], old)
    high = both_halves(total[7], 0).astype(I32) - 1
    low = both_halves(total[7], 1).astype(I32)
    for half in range(2):
        arrived(*lead_copies(half))

    def moved_stars(n):
        state = lead_all[pl.ds(n & 1, 1), pl.ds(2 * col + (n >> 1), 1)][0, 0]
        return state[0:3], state[3:6], state[6:7]

    prepare(LOCAL, HALF, 4, moved_stars, weights, weights8, features)

    def lead_rows(r, k):
        cut = slice((k % 2) * 128, (k % 2) * 128 + 128)
        return [(lead_all[k // 2, r, c : c + 1, cut], lead_all[k // 2, r, c + 1 : c + 2, cut]) for c in (0, 2, 4)]

    unpack(take_moved(high, low, sub, lead_rows), fix)
    moved = old[14:15] > 0.0
    x_own, v_own = predict(old[0:6], old[6:12], old[12:13], block_times[1])
    set_own(jnp.where(moved, fix[0:3], x_own), jnp.where(moved, fix[3:6], v_own))

    def rest_rows(r, k):
        half, at = k // 2, 4 * (k % 2)
        cut = slice((k % 2) * 128, (k % 2) * 128 + 128)
        return [
            (all0_ref[half, r, 6:7, cut], all0_ref[half, r, 7:8, cut]),
            (all0_ref[half, r, at : at + 1, 256:384], all0_ref[half, r, at + 1 : at + 2, 256:384]),
            (all0_ref[half, r, at + 2 : at + 3, 256:384], all0_ref[half, r, at + 3 : at + 4, 256:384]),
        ]

    def second_old():
        exchange(*force_copies(1, 0))
        for half in range(2):
            arrived(*row_copies(0, half))
        unpack(take_moved(high, low, sub, rest_rows), fix)
        moved = old[14:15] > 0.0
        h = block_times[1] - jnp.where(moved, block_times[0], old[12:13])
        accel[...] = jnp.concatenate(
            [jnp.where(moved, fix[0:3], old[6:9]), jnp.where(moved, fix[3:6], old[9:12]), h, h], axis=0
        )

    def second_corrected(half):
        arrived(*force_copies(1, half))
        cut = slice(half * HALF, half * HALF + HALF)
        mine1[half] = packed(
            *correct(
                own[0:3, cut], own[3:6, cut], accel[0:3, cut], accel[3:6, cut], accel[6:7, cut],
                sum_of(landf1.at[half]),
            )
        )
        exchange(*row_copies(1, half))

    force_sums(
        (LOCAL + 2 * PART) // 4, *sums, part1, {1: second_old, 2: lambda: second_corrected(0)}
    )
    exchange(*force_copies(1, 1))
    found = place_map(lists_ref, 1, offset)
    places[1, 0], places[1, 1] = found[:, 0:128], found[:, 128:256]
    second_corrected(1)
    rank_map(places[0], near_ref, base_ref, order_ref, 0)
    rank_map(places[1], near_ref, base_ref, order_ref, 1)
    for half in range(2):
        arrived(*row_copies(1, half))
    for copies in [lists, first_picks, second_picks]:
        sent(*copies)
    for half in range(2):
        sent(*lead_copies(half))
        for step in range(2):
            sent(*force_copies(step, half))
            sent(*row_copies(step, half))


def both_steps(index, count, phase, derivs, time, masses):
    stars = LOCAL + 2 * PART
    vmem = [
        ((6, LOCAL), F32),
        ((6, LOCAL), F32),
        ((1, LOCAL), F32),
        ((1, LOCAL), F32),
        ((24, 128), I32),
        ((ROWS, 24, 128), I32),
        ((2, 2, 128, 128), F32),
        ((7, 8, 128), F32),
        ((8, 8, 128), F32),
        ((COLS, 7, 8, 128), F32),
        ((COLS, 8, 8, 128), F32),
        ((2, 8, HALF), F32),
        ((2, 8, HALF), F32),
        ((2, COLS, 8, HALF), F32),
        ((2, COLS, 8, HALF), F32),
        ((2, 8, HALF), F32),
        ((2, ROWS, 8, HALF), F32),
        ((2, 8, 384), F32),
        ((2, 8, 384), F32),
        ((16, PART), F32),
        ((8, PART), F32),
        ((8, PART), F32),
        ((8, PART), F32),
        ((32, stars), BF16),
        ((32, stars), FINE8),
        ((stars, 64), BF16),
        ((64, PART), BF16),
        ((64, PART), BF16),
        ((4, 32, HALF), F32),
    ]
    sems = [(4,)] + [(ROWS,)] * 2 + [(COLS,)] * 4 + [(4, COLS)] * 2 + [(2, ROWS)] * 2 + [(4, ROWS)] * 2
    return pl.pallas_call(
        steps_kernel,
        out_shape=[
            jax.ShapeDtypeStruct((2, ROWS, 8, 384), F32),
            jax.ShapeDtypeStruct((2, ROWS, 8, 384), F32),
            jax.ShapeDtypeStruct((2, 128, 128), I32),
            jax.ShapeDtypeStruct((2, 2, 8, 128), I32),
            jax.ShapeDtypeStruct((2, 64, 256), F32),
        ],
        in_specs=in_vmem(2) + [pl.BlockSpec(memory_space=pl.ANY)] * 4,
        out_specs=in_vmem(5),
        scratch_shapes=[pltpu.VMEM(shape, kind) for shape, kind in vmem]
        + [pltpu.SemaphoreType.DMA(shape) for shape in sems],
        compiler_params=params(collective_id=0, has_side_effects=True),
        name="both_steps",
    )(index, count, phase, derivs, time, masses)


def collect(step, count, order_ref, all_ref, sorted_ref):
    def one_block(n, _):
        group = order_ref[step, pl.ds(pl.multiple_of((n >> 3) * 8, 8), 8), :]
        mask = lax.broadcasted_iota(I32, (8, 256), 0) == (n & 7)
        digits = jnp.sum(jnp.where(mask, group, 0.0), axis=0, keepdims=True)
        high = spread(digits[:, 0:128]).astype(I32) - 1
        low = spread(digits[:, 128:256]).astype(I32)
        upper = jnp.zeros((8, 128), F32)
        lower = jnp.zeros((8, 128), F32)
        shifted = high - (lax.broadcasted_iota(I32, (8, 128), 0) >> 2)
        for b in range(64):
            r, half, k = b // 4, (b % 4) // 2, b % 2
            upper = jnp.where(high == b, lane_pick(all_ref[half, r, :, k * 128 : k * 128 + 128], low), upper)
            if k == 0:
                lower = jnp.where(shifted == b, lane_pick(all_ref[half, r, :, 256:384], low), lower)
        blank = jnp.zeros((2, 128), F32)
        rest = lower[0:4] + lower[4:8]
        sorted_ref[step, n, 0:8, :] = upper
        sorted_ref[step, n, 8:16, :] = jnp.concatenate([upper[6:8], rest, blank], axis=0)
        return 0

    lax.fori_loop(0, (count + 127) // 128, one_block, 0)


def last_kernel(
    base_ref, near_ref, order_ref, all0_ref, all1_ref, phase_ref, derivs_ref, time_ref,
    phase_out, derivs_out, time_out, sorted_ref,
):
    collect(0, base_ref[0, 1, 0, 127], order_ref, all0_ref, sorted_ref)
    collect(1, base_ref[1, 1, 0, 127], order_ref, all1_ref, sorted_ref)

    def put(g, _):
        for u in range(8):
            b = g * 8 + u
            lanes = pl.ds(pl.multiple_of(b * 128, 128), 128)
            blank = jnp.zeros((2, 128), F32)
            phase = jnp.concatenate([phase_ref[:, lanes], blank], axis=0)
            derivs = jnp.concatenate([derivs_ref[:, lanes], blank], axis=0)
            time = time_ref[:, lanes]
            for step in range(2):
                n = jnp.minimum(base_ref[step, 0, 0, b], 63)
                m = jnp.minimum(n + 1, 63)
                at = spread(near_ref[step, pl.ds(b, 1), :]) - 1
                low = at & 127
                is_first = (at >= 0) & (at < 128)
                is_next = at >= 128

                def chosen(rows, was):
                    new = jnp.where(is_first, lane_pick(sorted_ref[step, n, rows, :], low), was)
                    return jnp.where(is_next, lane_pick(sorted_ref[step, m, rows, :], low), new)

                phase = chosen(slice(0, 8), phase)
                derivs = chosen(slice(8, 16), derivs)
                time = jnp.where(at[0:1] >= 0, block_times[step], time)
            phase_out[:, lanes] = phase[0:6]
            derivs_out[:, lanes] = derivs[0:6]
            time_out[:, lanes] = time
        return 0

    lax.fori_loop(0, BLOCKS // 8, put, 0)


def last_update(base, near, order, all0, all1, phase, derivs, time):
    return pl.pallas_call(
        last_kernel,
        out_shape=[
            jax.ShapeDtypeStruct((6, LOCAL), F32),
            jax.ShapeDtypeStruct((6, LOCAL), F32),
            jax.ShapeDtypeStruct((1, LOCAL), F32),
        ],
        in_specs=[pl.BlockSpec(memory_space=pltpu.SMEM)] + in_vmem(7),
        out_specs=in_vmem(3),
        scratch_shapes=[pltpu.VMEM((2, 64, 16, 128), F32)],
        compiler_params=params(),
        name="last_update",
    )(base, near, order, all0, all1, phase, derivs, time)


def body(phase_space, derivs, star_time, masses, active_index, active_count):
    time = star_time.reshape(1, LOCAL)
    masses = masses.reshape(1, LOCAL)
    all0, all1, near, base, order = both_steps(
        active_index, active_count.reshape(1, 2), phase_space, derivs, time, masses
    )
    phase_space, derivs, time = last_update(base, near, order, all0, all1, phase_space, derivs, time)
    return phase_space, derivs, time.reshape(LOCAL)


def solution(mesh):
    return jax.shard_map(
        body,
        mesh=mesh,
        in_specs=(
            P(None, "col"),
            P(None, "col"),
            P("col"),
            P("col"),
            P(None, "row", None),
            P(None, "row"),
        ),
        out_specs=(P(None, "col"), P(None, "col"), P("col")),
        check_vma=False,
    )
```

```python
import functools

import jax
import jax.numpy as jnp
from jax import lax
from jax.experimental import pallas as pl
from jax.experimental.pallas import tpu as pltpu
from jax.sharding import PartitionSpec as P

F32 = jnp.float32
BF16 = jnp.bfloat16
I32 = jnp.int32
FINE8 = jnp.float8_e4m3fn
WIDE8 = jnp.float8_e5m2
DIST_SCALE = 2.0**-4
BOTH_SCALE = 2.0**-10
WEIGHT_BACK = 2.0**-6
softening = 0.01
block_times = (0.125, 0.25)
ROWS = 16
COLS = 8
CAP = 1024
PART = 512
HALF = 256
LOCAL = 16384
BLOCKS = LOCAL // 128
N_STARS = ROWS * PART * 16
MESH = pl.DeviceIdType.MESH
ADDED = (((1,), (1,)), ((), ()))


def rows_of(first, last, width):
    return jnp.zeros((last - first, width), F32)


def in_vmem(n):
    return [pl.BlockSpec(memory_space=pltpu.VMEM)] * n


def in_any(n):
    return [pl.BlockSpec(memory_space=pl.ANY)] * n


def params(**more):
    return pltpu.CompilerParams(vmem_limit_bytes=56 * 2**20, **more)


def partners_of(axis, size, place):
    return [(k, {axis: lax.rem(place + k, size)}) for k in range(1, size)]


def send(axis, size, place, source, landing, send_sem, recv_sem):
    for k, partner in partners_of(axis, size, place):
        pltpu.make_async_remote_copy(
            src_ref=source,
            dst_ref=landing.at[place],
            send_sem=send_sem.at[k],
            recv_sem=recv_sem.at[place],
            device_id=partner,
            device_id_type=MESH,
        ).start()


def exchange(axis, size, place, source, landing, send_sem, recv_sem):
    send(axis, size, place, source, landing, send_sem, recv_sem)
    landing[pl.ds(place, 1)] = source[...][None]


def sent(axis, size, place, source, landing, send_sem, recv_sem):
    for k, partner in partners_of(axis, size, place):
        pltpu.make_async_remote_copy(
            src_ref=source,
            dst_ref=landing.at[place],
            send_sem=send_sem.at[k],
            recv_sem=recv_sem.at[place],
            device_id=partner,
            device_id_type=MESH,
        ).wait_send()


def arrived(axis, size, place, source, landing, send_sem, recv_sem):
    for k, partner in partners_of(axis, size, place):
        slot = lax.rem(place + k, size)
        pltpu.make_async_remote_copy(
            src_ref=source,
            dst_ref=landing.at[slot],
            send_sem=send_sem.at[k],
            recv_sem=recv_sem.at[slot],
            device_id=partner,
            device_id_type=MESH,
        ).wait_recv()


def lane_pick(table, lanes):
    return jnp.take_along_axis(table, lanes, axis=1, mode="promise_in_bounds")


def spread(row):
    return jnp.broadcast_to(row, (8, 128))


def hot(index_row, count):
    kinds = lax.broadcasted_iota(I32, (count, 128), 0).astype(F32).astype(BF16)
    return jnp.broadcast_to(index_row, (count, 128)).astype(BF16) == kinds


def scattered(entries, high_count):
    one, zero = jnp.ones((), BF16), jnp.zeros((), BF16)
    left, right = [], []
    for high, low, first, second in entries:
        left.append(jnp.where(hot(high, high_count), one, zero))
        at_low = hot(low, 128)
        a = jnp.broadcast_to(first, (128, 128)).astype(BF16)
        b = jnp.broadcast_to(second, (128, 128)).astype(BF16)
        right.append(jnp.concatenate([jnp.where(at_low, a, zero), jnp.where(at_low, b, zero)], axis=0))
    return lax.dot_general(
        jnp.concatenate(left, axis=1), jnp.concatenate(right, axis=1), ADDED, preferred_element_type=F32
    )


def place_map(lists_ref, step, offset):
    slot = lax.broadcasted_iota(I32, (8, 128), 0) * 128 + lax.broadcasted_iota(I32, (8, 128), 1)
    begin = jnp.zeros((8, 128), I32)
    entries = []
    for r in range(ROWS):
        count = spread(lists_ref[r, 16 + step : 17 + step, :])
        star = lists_ref[r, 8 * step : 8 * step + 8, :] - offset
        live = (slot < count) & (star >= 0) & (star < LOCAL)
        at = begin + slot
        high = jnp.where(live, star >> 7, 255).astype(F32)
        low = (star & 127).astype(F32)
        first, second = ((at >> 7) + 1).astype(F32), (at & 127).astype(F32)
        for k in range(8):
            cut = slice(k, k + 1)
            entries.append((high[cut], low[cut], first[cut], second[cut]))
        begin = begin + count
    return scattered(entries, 128)


def rank_map(places, near_ref, base_ref, order_ref, step):
    at_high, at_low = places[0], places[1]
    row = lax.broadcasted_iota(I32, (128, 128), 0)
    lane = lax.broadcasted_iota(I32, (128, 128), 1)
    up_to = (row <= lane).astype(F32).astype(BF16)
    before = (row < lane).astype(F32).astype(BF16)
    below = (lane < row).astype(F32).astype(BF16)
    active = (at_high > 0.0).astype(F32)
    active16 = active.astype(BF16)
    so_far = jnp.dot(active16, up_to, preferred_element_type=F32)
    total = jnp.broadcast_to(so_far[:, 127:128], (128, 128))
    first = jnp.dot(below, total.astype(BF16), preferred_element_type=F32)
    rank = (first + so_far - active).astype(I32)
    near_ref[step] = jnp.where(active > 0.0, rank - (first.astype(I32) >> 7) * 128 + 1, 0)
    ones = jnp.ones((8, 128), F32).astype(BF16)
    totals = lax.dot_general(ones, active16, ADDED, preferred_element_type=F32)
    firsts = jnp.dot(totals.astype(BF16), before, preferred_element_type=F32).astype(I32)
    base_ref[step, 0] = firsts >> 7
    base_ref[step, 1] = firsts + totals.astype(I32)
    rank_high = jnp.where(active > 0.0, rank >> 7, 255).astype(F32)
    rank_low = (rank & 127).astype(F32)
    entries = []
    for b in range(BLOCKS):
        cut = slice(b, b + 1)
        entries.append((rank_high[cut], rank_low[cut], at_high[cut], at_low[cut]))
    order_ref[step] = scattered(entries, 64)


def own_stars(lists_ref, place):
    lane = lax.broadcasted_iota(I32, (8, 128), 1)
    sub = lax.broadcasted_iota(I32, (8, 128), 0)
    position = place * PART + (sub & 3) * 128 + lane
    before = jnp.zeros((8, 128), I32)
    which = jnp.zeros((8, 128), I32)
    start = jnp.zeros((8, 128), I32)
    for r in range(ROWS):
        count = jnp.where(sub < 4, spread(lists_ref[r, 16:17, :]), spread(lists_ref[r, 17:18, :]))
        end = before + count
        passed = position >= end
        which = which + passed.astype(I32)
        start = jnp.where(passed, end, start)
        before = end
    flat = which * CAP + position - start
    high, low = flat >> 7, flat & 127
    stars = jnp.zeros((8, 128), I32)
    for r in range(ROWS):
        for k in range(8):
            row = jnp.where(
                sub < 4, spread(lists_ref[r, k : k + 1, :]), spread(lists_ref[r, 8 + k : 9 + k, :])
            )
            stars = jnp.where(high == r * 8 + k, lane_pick(row, low), stars)
    return stars


def both_halves(x, step):
    part = x[4 * step : 4 * step + 4]
    return jnp.concatenate([part, part], axis=0)


def fetch(stars, pairs):
    high, low = stars >> 7, stars & 127

    def look(g, found):
        for u in range(8):
            b = g * 8 + u
            here = high == b
            found = tuple(
                jnp.where(here, lane_pick(pair(b), low), old) for pair, old in zip(pairs, found)
            )
        return found

    return lax.fori_loop(0, BLOCKS // 8, look, tuple(jnp.zeros((8, 128), F32) for _ in pairs))


def two_rows(sub, a, b):
    return jnp.where(sub < 4, spread(a), spread(b))


def unpack(pairs, out_ref):
    for p, pair in enumerate(pairs):
        for half in range(2):
            for s in range(4):
                out_ref[2 * p + half : 2 * p + half + 1, s * 128 : s * 128 + 128] = pair[
                    4 * half + s : 4 * half + s + 1
                ]


def predict(phase, derivs, time, now):
    d = now - time
    x, v, a, j = phase[0:3], phase[3:6], derivs[0:3], derivs[3:6]
    return x + d * (v + d * (a / 2.0 + d * j / 6.0)), v + d * (a + d * j / 2.0)


def correct(x, v, old_acc, old_jerk, h, forces):
    new_acc, new_jerk = forces[0:3], forces[3:6]
    change = old_acc - new_acc
    second = (-6.0 * change - h * (4.0 * old_jerk + 2.0 * new_jerk)) / (h * h)
    third = (12.0 * change + 6.0 * h * (old_jerk + new_jerk)) / (h * h * h)
    h2 = h * h
    h3 = h2 * h
    h4 = h3 * h
    h5 = h4 * h
    x = x + h4 / 24.0 * second + h5 / 120.0 * third
    v = v + h3 / 6.0 * second + h4 / 24.0 * third
    return x, v, new_acc, new_jerk


PAIRS = ((0, 0), (0, 1), (0, 2), (1, 0), (1, 1), (2, 0))


def split3(x):
    high = x.astype(BF16).astype(F32)
    rest = x - high
    middle = rest.astype(BF16).astype(F32)
    return high, middle, rest - middle


def split2(x, low_kind):
    high = x.astype(BF16)
    return high, (x - high.astype(F32)).astype(low_kind)


def split8(x):
    parts = []
    for _ in range(4):
        parts.append(x.astype(FINE8).astype(F32))
        x = x - parts[-1]
    return parts


def squares(x, v):
    xx = x * x
    xv = x * v
    return xx[0:1] + xx[1:2] + xx[2:3], xv[0:1] + xv[1:2] + xv[2:3]


def star_features(x, v):
    width = x.shape[1]
    parts = split3(jnp.concatenate([x, v, jnp.zeros((2, width), F32)], axis=0))
    xx, xv = squares(x, v)
    one = jnp.ones((3, width), F32)
    extra = jnp.concatenate(list(split3(xx)) + list(split3(xv)) + [one, one, rows_of(12, 16, width)], axis=0)
    return jnp.concatenate([parts[a] for a, _ in PAIRS] + [extra], axis=0)


def active_features(x, v):
    width = x.shape[1]
    xp, vp = split3(x), split3(v)
    xx, xv = squares(x, v)
    one, none3, none5 = jnp.ones((3, width), F32), rows_of(0, 3, width), rows_of(0, 5, width)
    dist, both = [], []
    for _, b in PAIRS:
        dist += [-2.0 * xp[b], none5]
        both += [-vp[b], -xp[b], rows_of(0, 2, width)]
    dist += [one, none3] + list(split3(xx + softening)) + [none3, rows_of(12, 16, width)]
    both += [none3, one, none3] + list(split3(xv)) + [rows_of(12, 16, width)]
    dist = jnp.concatenate(dist, axis=0) * DIST_SCALE
    both = jnp.concatenate(both, axis=0) * BOTH_SCALE
    return dist.astype(BF16), both.astype(BF16)


def prepare(first, chunk, count, pred_of, weights, weights8, features):
    def one_chunk(n, _):
        x, v, mass = pred_of(n)
        at = pl.ds(pl.multiple_of(first + n * chunk, chunk), chunk)
        ones, none = jnp.ones((1, chunk), F32), jnp.zeros((1, chunk), F32)
        scaled = jnp.concatenate([x, v, ones, none], axis=0) * mass
        parts = list(split3(scaled / N_STARS)) + [rows_of(24, 32, chunk)]
        weights[:, at] = jnp.concatenate(parts, axis=0).astype(BF16)
        weights8[:, at] = jnp.concatenate(split8(jnp.clip(scaled, -240.0, 240.0)), axis=0).astype(FINE8)
        features[at, :] = star_features(x, v).T.astype(BF16)
        return 0

    lax.fori_loop(0, count, one_chunk, 0)


def force_sums(deep, weights, weights8, features, dist_own, both_own, totals, own, part, after):
    def quarter(t, _):
        h = t >> 1
        cut = pl.ds(pl.multiple_of(h * HALF, HALF), HALF)
        fresh = (t & 1) == 0

        def sums(n, total):
            lanes = pl.ds(pl.multiple_of(((t & 1) * 2 + n) * deep, deep), deep)
            factor = features[lanes, :]
            dist = jnp.dot(factor, dist_own[:, cut], preferred_element_type=F32)
            both = jnp.dot(factor, both_own[:, cut], preferred_element_type=F32)
            inverse = lax.rsqrt(jnp.maximum(dist, softening * DIST_SCALE))
            inverse_sq = inverse * inverse
            weight = inverse * inverse_sq
            radial = (weight * inverse_sq) * both
            w_high, w_low = split2(weight, FINE8)
            u_high, u_low = split2(radial, WIDE8)
            dot = functools.partial(jnp.dot, preferred_element_type=F32)
            left, left8 = weights[:, lanes], weights8[:, lanes]
            new = dot(left, w_high), dot(left, u_high), dot(left8, w_low), dot(left8, u_low)
            return tuple(a + b for a, b in zip(total, new))

        found = lax.fori_loop(0, 2, sums, tuple(jnp.where(fresh, 0.0, totals[n]) for n in range(4)))
        for n in range(4):
            totals[n] = found[n]

        @pl.when((t & 1) == 1)
        def _():
            def whole(high, low, back):
                high = high[0:8] + high[8:16] + high[16:24]
                low = low[0:8] + low[8:16] + low[16:24] + low[24:32]
                return (high + low / N_STARS) * back

            w_all = whole(found[0], found[2], WEIGHT_BACK)
            u_all = whole(found[1], found[3], 1.0)
            mine = own[:, cut]
            x, v = mine[0:3], mine[3:6]
            acc = w_all[0:3] - x * w_all[6:7]
            jerk = w_all[3:6] - v * w_all[6:7] - 3.0 * (u_all[0:3] - x * u_all[6:7])
            part[pl.ds(h, 1)] = jnp.concatenate([acc, jerk, jnp.zeros((2, HALF), F32)], axis=0)[None]

        for number, action in after.items():
            pl.when(t == number)(action)
        return 0

    lax.fori_loop(0, 4, quarter, 0)


def sum_of(landing):
    total = landing[0]
    for c in range(1, COLS):
        total = total + landing[c]
    return total


def packed(x, v, a, j):
    rest = jnp.concatenate([a[2:3], j], axis=0)
    right = jnp.concatenate([rest[:, 0:128], rest[:, 128:256]], axis=0)
    return jnp.concatenate([jnp.concatenate([x, v, a[0:2]], axis=0), right], axis=1)


def take_moved(high, low, sub, rows_at):
    def look(r, found):
        for k in range(4):
            here = high == r * 4 + k
            found = tuple(
                jnp.where(here, lane_pick(two_rows(sub, *pair), low), was)
                for pair, was in zip(rows_at(r, k), found)
            )
        return found

    return lax.fori_loop(0, ROWS, look, tuple(jnp.zeros((8, 128), F32) for _ in range(3)))


def steps_kernel(
    index_ref, count_ref, phase_far, derivs_far, time_far, mass_far,
    all0_far, all1_far, near_far, base_ref, order_far,
    all0_ref, near_ref, order_ref, phase_ref, derivs_ref, time_ref, mass_ref, lists_own, lists_ref, places,
    picks0, picks1, land0, land1, part0, part1, landf0, landf1, lead, lead_all, mine0, mine1,
    old, fix, own, accel, weights, weights8, features, dist_own, both_own, totals,
    s_in, s_out, s_list, r_list, s_pick0, r_pick0, s_pick1, r_pick1, s_for, r_for, s_lead, r_lead, s_all, r_all,
):
    row, col = lax.axis_index("row"), lax.axis_index("col")
    barrier = pltpu.get_barrier_semaphore()
    everyone = partners_of("row", ROWS, row) + partners_of("col", COLS, col)
    for _, partner in everyone:
        pl.semaphore_signal(barrier, inc=1, device_id=partner, device_id_type=MESH)
    inputs = [
        pltpu.make_async_copy(far, near, s_in.at[n])
        for n, (far, near) in enumerate(
            [(phase_far, phase_ref), (derivs_far, derivs_ref), (time_far, time_ref), (mass_far, mass_ref)]
        )
    ]
    for copy in inputs:
        copy.start()
    offset = col * LOCAL
    chunk = 2048
    sub = lax.broadcasted_iota(I32, (8, 128), 0)
    for step in range(2):
        for k in range(8):
            lists_own[8 * step + k : 8 * step + k + 1, :] = index_ref[step, 0:1, k * 128 : k * 128 + 128]
        lists_own[16 + step : 17 + step, :] = jnp.broadcast_to(count_ref[0:1, step : step + 1], (1, 128))
    lists_own[18:24, :] = jnp.zeros((6, 128), I32)
    pl.semaphore_wait(barrier, len(everyone))
    lists = ("row", ROWS, row, lists_own, lists_ref, s_list, r_list)
    exchange(*lists)
    for copy in inputs:
        copy.wait()

    def first_stars(n):
        lanes = pl.ds(pl.multiple_of(n * chunk, chunk), chunk)
        x, v = predict(phase_ref[:, lanes], derivs_ref[:, lanes], time_ref[:, lanes], block_times[0])
        return x, v, mass_ref[:, lanes]

    prepare(0, chunk, LOCAL // chunk, first_stars, weights, weights8, features)
    arrived(*lists)

    def block(b):
        return pl.ds(pl.multiple_of(b * 128, 128), 128)

    pairs = [
        lambda b, ref=ref, c=c: two_rows(sub, ref[c : c + 1, block(b)], ref[c + 1 : c + 2, block(b)])
        for ref in (phase_ref, derivs_ref)
        for c in (0, 2, 4)
    ]
    pairs.append(lambda b: two_rows(sub, time_ref[:, block(b)], mass_ref[:, block(b)]))
    local = own_stars(lists_ref, row) - offset
    for p, value in enumerate(fetch(both_halves(local, 0), pairs)):
        picks0[p] = value
    first_picks = ("col", COLS, col, picks0, land0, s_pick0, r_pick0)
    exchange(*first_picks)

    found = place_map(lists_ref, 0, offset)
    places[0, 0], places[0, 1] = found[:, 0:128], found[:, 128:256]

    arrived(*first_picks)
    total = sum_of(land0)
    unpack([total[p] for p in range(7)], old)
    def force_copies(step, half):
        part, landing = (part0, landf0) if step == 0 else (part1, landf1)
        n = 2 * step + half
        return ("col", COLS, col, part.at[half], landing.at[half], s_for.at[n], r_for.at[n])

    def lead_copies(half):
        return ("row", ROWS, row, lead.at[half], lead_all.at[half], s_lead.at[half], r_lead.at[half])

    def row_copies(step, half):
        mine, landing = (mine0, all0_ref) if step == 0 else (mine1, all1_far)
        n = 2 * step + half
        return ("row", ROWS, row, mine.at[half], landing.at[half], s_all.at[n], r_all.at[n])

    def set_own(x, v):
        own[...] = jnp.concatenate([x, v, jnp.zeros((2, PART), F32)], axis=0)
        dist_own[...], both_own[...] = active_features(x, v)

    sums = (weights, weights8, features, dist_own, both_own, totals, own)
    set_own(*predict(old[0:6], old[6:12], old[12:13], block_times[0]))

    def first_corrected(half):
        arrived(*force_copies(0, half))
        cut = slice(half * HALF, half * HALF + HALF)
        x, v, a, j = correct(
            own[0:3, cut], own[3:6, cut], old[6:9, cut], old[9:12, cut],
            block_times[0] - old[12:13, cut], sum_of(landf0.at[half]),
        )
        x_next, v_next = predict(
            jnp.concatenate([x, v], axis=0), jnp.concatenate([a, j], axis=0), block_times[0], block_times[1]
        )
        lead[half] = jnp.concatenate([x_next, v_next, old[13:14, cut], jnp.zeros((1, HALF), F32)], axis=0)
        exchange(*lead_copies(half))
        mine0[half] = packed(x, v, a, j)
        exchange(*row_copies(0, half))

    force_sums(
        4096, *sums, part0,
        {1: lambda: exchange(*force_copies(0, 0)), 2: lambda: first_corrected(0)},
    )
    exchange(*force_copies(0, 1))
    pairs.append(lambda b: two_rows(sub, places[0, 0, pl.ds(b, 1), :], places[0, 1, pl.ds(b, 1), :]))
    for p, value in enumerate(fetch(both_halves(local, 1), pairs)):
        picks1[p] = value
    second_picks = ("col", COLS, col, picks1, land1, s_pick1, r_pick1)
    exchange(*second_picks)
    first_corrected(1)

    def second_stars(n):
        lanes = pl.ds(pl.multiple_of(n * chunk, chunk), chunk)
        x, v = predict(phase_ref[:, lanes], derivs_ref[:, lanes], time_ref[:, lanes], block_times[1])
        moved = jnp.concatenate([places[0, 0, pl.ds(n * 16 + k, 1), :] for k in range(16)], axis=1)
        return x, v, jnp.where(moved > 0.0, 0.0, mass_ref[:, lanes])

    prepare(0, chunk, LOCAL // chunk, second_stars, weights, weights8, features)
    arrived(*second_picks)
    total = sum_of(land1)
    unpack([total[p] for p in range(8)], old)
    high = both_halves(total[7], 0).astype(I32) - 1
    low = both_halves(total[7], 1).astype(I32)
    for half in range(2):
        arrived(*lead_copies(half))

    def moved_stars(n):
        state = lead_all[pl.ds(n & 1, 1), pl.ds(2 * col + (n >> 1), 1)][0, 0]
        return state[0:3], state[3:6], state[6:7]

    prepare(LOCAL, HALF, 4, moved_stars, weights, weights8, features)

    def lead_rows(r, k):
        cut = slice((k % 2) * 128, (k % 2) * 128 + 128)
        return [(lead_all[k // 2, r, c : c + 1, cut], lead_all[k // 2, r, c + 1 : c + 2, cut]) for c in (0, 2, 4)]

    unpack(take_moved(high, low, sub, lead_rows), fix)
    moved = old[14:15] > 0.0
    x_own, v_own = predict(old[0:6], old[6:12], old[12:13], block_times[1])
    set_own(jnp.where(moved, fix[0:3], x_own), jnp.where(moved, fix[3:6], v_own))

    def rest_rows(r, k):
        half, at = k // 2, 4 * (k % 2)
        cut = slice((k % 2) * 128, (k % 2) * 128 + 128)
        return [
            (all0_ref[half, r, 6:7, cut], all0_ref[half, r, 7:8, cut]),
            (all0_ref[half, r, at : at + 1, 256:384], all0_ref[half, r, at + 1 : at + 2, 256:384]),
            (all0_ref[half, r, at + 2 : at + 3, 256:384], all0_ref[half, r, at + 3 : at + 4, 256:384]),
        ]

    outputs = [
        pltpu.make_async_copy(near, far, s_out.at[n])
        for n, (near, far) in enumerate([(all0_ref, all0_far), (near_ref, near_far), (order_ref, order_far)])
    ]

    def own_copy(half):
        return pltpu.make_async_copy(mine1.at[half], all1_far.at[half, row], s_out.at[3 + half])

    def second_old():
        exchange(*force_copies(1, 0))
        for half in range(2):
            arrived(*row_copies(0, half))
        outputs[0].start()
        unpack(take_moved(high, low, sub, rest_rows), fix)
        moved = old[14:15] > 0.0
        h = block_times[1] - jnp.where(moved, block_times[0], old[12:13])
        accel[...] = jnp.concatenate(
            [jnp.where(moved, fix[0:3], old[6:9]), jnp.where(moved, fix[3:6], old[9:12]), h, h], axis=0
        )

    def second_corrected(half):
        arrived(*force_copies(1, half))
        cut = slice(half * HALF, half * HALF + HALF)
        mine1[half] = packed(
            *correct(
                own[0:3, cut], own[3:6, cut], accel[0:3, cut], accel[3:6, cut], accel[6:7, cut],
                sum_of(landf1.at[half]),
            )
        )
        send(*row_copies(1, half))
        own_copy(half).start()

    force_sums(
        (LOCAL + 2 * PART) // 4, *sums, part1, {1: second_old, 2: lambda: second_corrected(0)}
    )
    exchange(*force_copies(1, 1))
    found = place_map(lists_ref, 1, offset)
    places[1, 0], places[1, 1] = found[:, 0:128], found[:, 128:256]
    second_corrected(1)
    rank_map(places[0], near_ref, base_ref, order_ref, 0)
    rank_map(places[1], near_ref, base_ref, order_ref, 1)
    outputs[1].start()
    outputs[2].start()
    for half in range(2):
        arrived(*row_copies(1, half))
        own_copy(half).wait()
    for copy in outputs:
        copy.wait()
    for copies in [lists, first_picks, second_picks]:
        sent(*copies)
    for half in range(2):
        sent(*lead_copies(half))
        for step in range(2):
            sent(*force_copies(step, half))
            sent(*row_copies(step, half))


def both_steps(index, count, phase, derivs, time, masses):
    stars = LOCAL + 2 * PART
    vmem = [
        ((2, ROWS, 8, 384), F32),
        ((2, 128, 128), I32),
        ((2, 64, 256), F32),
        ((6, LOCAL), F32),
        ((6, LOCAL), F32),
        ((1, LOCAL), F32),
        ((1, LOCAL), F32),
        ((24, 128), I32),
        ((ROWS, 24, 128), I32),
        ((2, 2, 128, 128), F32),
        ((7, 8, 128), F32),
        ((8, 8, 128), F32),
        ((COLS, 7, 8, 128), F32),
        ((COLS, 8, 8, 128), F32),
        ((2, 8, HALF), F32),
        ((2, 8, HALF), F32),
        ((2, COLS, 8, HALF), F32),
        ((2, COLS, 8, HALF), F32),
        ((2, 8, HALF), F32),
        ((2, ROWS, 8, HALF), F32),
        ((2, 8, 384), F32),
        ((2, 8, 384), F32),
        ((16, PART), F32),
        ((8, PART), F32),
        ((8, PART), F32),
        ((8, PART), F32),
        ((32, stars), BF16),
        ((32, stars), FINE8),
        ((stars, 64), BF16),
        ((64, PART), BF16),
        ((64, PART), BF16),
        ((4, 32, HALF), F32),
    ]
    sems = [(4,), (5,)] + [(ROWS,)] * 2 + [(COLS,)] * 4 + [(4, COLS)] * 2 + [(2, ROWS)] * 2 + [(4, ROWS)] * 2
    return pl.pallas_call(
        steps_kernel,
        out_shape=[
            jax.ShapeDtypeStruct((2, ROWS, 8, 384), F32),
            jax.ShapeDtypeStruct((2, ROWS, 8, 384), F32),
            jax.ShapeDtypeStruct((2, 128, 128), I32),
            jax.ShapeDtypeStruct((2, 2, 8, 128), I32),
            jax.ShapeDtypeStruct((2, 64, 256), F32),
        ],
        in_specs=in_vmem(2) + in_any(4),
        out_specs=in_any(3) + in_vmem(1) + in_any(1),
        scratch_shapes=[pltpu.VMEM(shape, kind) for shape, kind in vmem]
        + [pltpu.SemaphoreType.DMA(shape) for shape in sems],
        compiler_params=params(collective_id=0, has_side_effects=True),
        name="both_steps",
    )(index, count, phase, derivs, time, masses)


def collect(step, count, order_ref, all_ref, sorted_ref):
    def one_block(n, _):
        group = order_ref[step, pl.ds(pl.multiple_of((n >> 3) * 8, 8), 8), :]
        mask = lax.broadcasted_iota(I32, (8, 256), 0) == (n & 7)
        digits = jnp.sum(jnp.where(mask, group, 0.0), axis=0, keepdims=True)
        high = spread(digits[:, 0:128]).astype(I32) - 1
        low = spread(digits[:, 128:256]).astype(I32)
        upper = jnp.zeros((8, 128), F32)
        lower = jnp.zeros((8, 128), F32)
        shifted = high - (lax.broadcasted_iota(I32, (8, 128), 0) >> 2)
        for b in range(64):
            r, half, k = b // 4, (b % 4) // 2, b % 2
            upper = jnp.where(high == b, lane_pick(all_ref[half, r, :, k * 128 : k * 128 + 128], low), upper)
            if k == 0:
                lower = jnp.where(shifted == b, lane_pick(all_ref[half, r, :, 256:384], low), lower)
        blank = jnp.zeros((2, 128), F32)
        rest = lower[0:4] + lower[4:8]
        sorted_ref[step, n, 0:8, :] = upper
        sorted_ref[step, n, 8:16, :] = jnp.concatenate([upper[6:8], rest, blank], axis=0)
        return 0

    lax.fori_loop(0, (count + 127) // 128, one_block, 0)


PIECES = 4


def last_kernel(
    base_ref, near_far, order_far, all0_far, all1_far, phase_far, derivs_far, time_far,
    phase_end, derivs_end, time_end,
    near_ref, order_ref, all0_ref, all1_ref, phase_ref, derivs_ref, time_ref,
    phase_out, derivs_out, time_out, sorted_ref, s_in, s_out,
):
    fars = (order_far, all0_far, all1_far, near_far, phase_far, derivs_far, time_far)
    nears = (order_ref, all0_ref, all1_ref, near_ref, phase_ref, derivs_ref, time_ref)
    inputs = [pltpu.make_async_copy(far, near, s_in.at[n]) for n, (far, near) in enumerate(zip(fars, nears))]
    for copy in inputs:
        copy.start()
    inputs[0].wait()
    inputs[1].wait()
    collect(0, base_ref[0, 1, 0, 127], order_ref, all0_ref, sorted_ref)
    inputs[2].wait()
    collect(1, base_ref[1, 1, 0, 127], order_ref, all1_ref, sorted_ref)
    for copy in inputs[3:]:
        copy.wait()

    def put(g, _):
        for u in range(8):
            b = g * 8 + u
            lanes = pl.ds(pl.multiple_of(b * 128, 128), 128)
            blank = jnp.zeros((2, 128), F32)
            phase = jnp.concatenate([phase_ref[:, lanes], blank], axis=0)
            derivs = jnp.concatenate([derivs_ref[:, lanes], blank], axis=0)
            time = time_ref[:, lanes]
            for step in range(2):
                n = jnp.minimum(base_ref[step, 0, 0, b], 63)
                m = jnp.minimum(n + 1, 63)
                at = spread(near_ref[step, pl.ds(b, 1), :]) - 1
                low = at & 127
                is_first = (at >= 0) & (at < 128)
                is_next = at >= 128

                def chosen(rows, was):
                    new = jnp.where(is_first, lane_pick(sorted_ref[step, n, rows, :], low), was)
                    return jnp.where(is_next, lane_pick(sorted_ref[step, m, rows, :], low), new)

                phase = chosen(slice(0, 8), phase)
                derivs = chosen(slice(8, 16), derivs)
                time = jnp.where(at[0:1] >= 0, block_times[step], time)
            phase_out[:, lanes] = phase[0:6]
            derivs_out[:, lanes] = derivs[0:6]
            time_out[:, lanes] = time
        return 0

    pairs = ((phase_out, phase_end), (derivs_out, derivs_end), (time_out, time_end))
    groups = BLOCKS // 8 // PIECES
    outputs = []
    for piece in range(PIECES):
        lax.fori_loop(piece * groups, (piece + 1) * groups, put, 0)
        cut = pl.ds(piece * (LOCAL // PIECES), LOCAL // PIECES)
        for n, (near, far) in enumerate(pairs):
            outputs.append(pltpu.make_async_copy(near.at[:, cut], far.at[:, cut], s_out.at[piece, n]))
            outputs[-1].start()
    for copy in outputs:
        copy.wait()


def last_update(base, near, order, all0, all1, phase, derivs, time):
    shapes = [(x.shape, x.dtype) for x in (near, order, all0, all1, phase, derivs, time)]
    ends = [((6, LOCAL), F32), ((6, LOCAL), F32), ((1, LOCAL), F32)]
    return pl.pallas_call(
        last_kernel,
        out_shape=[jax.ShapeDtypeStruct(*end) for end in ends],
        in_specs=[pl.BlockSpec(memory_space=pltpu.SMEM)] + in_any(7),
        out_specs=in_any(3),
        scratch_shapes=[pltpu.VMEM(*shape) for shape in shapes + ends]
        + [
            pltpu.VMEM((2, 64, 16, 128), F32),
            pltpu.SemaphoreType.DMA((7,)),
            pltpu.SemaphoreType.DMA((PIECES, 3)),
        ],
        compiler_params=params(),
        name="last_update",
    )(base, near, order, all0, all1, phase, derivs, time)


def body(phase_space, derivs, star_time, masses, active_index, active_count):
    time = star_time.reshape(1, LOCAL)
    masses = masses.reshape(1, LOCAL)
    all0, all1, near, base, order = both_steps(
        active_index, active_count.reshape(1, 2), phase_space, derivs, time, masses
    )
    phase_space, derivs, time = last_update(base, near, order, all0, all1, phase_space, derivs, time)
    return phase_space, derivs, time.reshape(LOCAL)


def solution(mesh):
    return jax.shard_map(
        body,
        mesh=mesh,
        in_specs=(
            P(None, "col"),
            P(None, "col"),
            P("col"),
            P("col"),
            P(None, "row", None),
            P(None, "row"),
        ),
        out_specs=(P(None, "col"), P(None, "col"), P("col")),
        check_vma=False,
    )
```

```python
import functools

import jax
import jax.numpy as jnp
from jax import lax
from jax.experimental import pallas as pl
from jax.experimental.pallas import tpu as pltpu
from jax.sharding import PartitionSpec as P

F32 = jnp.float32
BF16 = jnp.bfloat16
I32 = jnp.int32
FINE8 = jnp.float8_e4m3fn
WIDE8 = jnp.float8_e5m2
DIST_SCALE = 2.0**-4
BOTH_SCALE = 2.0**-10
WEIGHT_BACK = 2.0**-6
softening = 0.01
block_times = (0.125, 0.25)
ROWS = 16
COLS = 8
CAP = 1024
PART = 512
HALF = 256
LOCAL = 16384
BLOCKS = LOCAL // 128
N_STARS = ROWS * PART * 16
MESH = pl.DeviceIdType.MESH
ADDED = (((1,), (1,)), ((), ()))


def rows_of(first, last, width):
    return jnp.zeros((last - first, width), F32)


def in_vmem(n):
    return [pl.BlockSpec(memory_space=pltpu.VMEM)] * n


def params(**more):
    return pltpu.CompilerParams(vmem_limit_bytes=56 * 2**20, **more)


def partners_of(axis, size, place):
    return [(k, {axis: lax.rem(place + k, size)}) for k in range(1, size)]


def exchange(axis, size, place, source, landing, send_sem, recv_sem):
    for k, partner in partners_of(axis, size, place):
        pltpu.make_async_remote_copy(
            src_ref=source,
            dst_ref=landing.at[place],
            send_sem=send_sem.at[k],
            recv_sem=recv_sem.at[place],
            device_id=partner,
            device_id_type=MESH,
        ).start()
    landing[pl.ds(place, 1)] = source[...][None]


def sent(axis, size, place, source, landing, send_sem, recv_sem):
    for k, partner in partners_of(axis, size, place):
        pltpu.make_async_remote_copy(
            src_ref=source,
            dst_ref=landing.at[place],
            send_sem=send_sem.at[k],
            recv_sem=recv_sem.at[place],
            device_id=partner,
            device_id_type=MESH,
        ).wait_send()


def arrived(axis, size, place, source, landing, send_sem, recv_sem):
    for k, partner in partners_of(axis, size, place):
        slot = lax.rem(place + k, size)
        pltpu.make_async_remote_copy(
            src_ref=source,
            dst_ref=landing.at[slot],
            send_sem=send_sem.at[k],
            recv_sem=recv_sem.at[slot],
            device_id=partner,
            device_id_type=MESH,
        ).wait_recv()


def lane_pick(table, lanes):
    return jnp.take_along_axis(table, lanes, axis=1, mode="promise_in_bounds")


def spread(row):
    return jnp.broadcast_to(row, (8, 128))


def hot(index_row, count):
    kinds = lax.broadcasted_iota(I32, (count, 128), 0).astype(F32).astype(BF16)
    return jnp.broadcast_to(index_row, (count, 128)).astype(BF16) == kinds


def scattered(entries, high_count):
    one, zero = jnp.ones((), BF16), jnp.zeros((), BF16)
    left, right = [], []
    for high, low, first, second in entries:
        left.append(jnp.where(hot(high, high_count), one, zero))
        at_low = hot(low, 128)
        a = jnp.broadcast_to(first, (128, 128)).astype(BF16)
        b = jnp.broadcast_to(second, (128, 128)).astype(BF16)
        right.append(jnp.concatenate([jnp.where(at_low, a, zero), jnp.where(at_low, b, zero)], axis=0))
    return lax.dot_general(
        jnp.concatenate(left, axis=1), jnp.concatenate(right, axis=1), ADDED, preferred_element_type=F32
    )


def place_map(lists_ref, step, offset):
    slot = lax.broadcasted_iota(I32, (8, 128), 0) * 128 + lax.broadcasted_iota(I32, (8, 128), 1)
    begin = jnp.zeros((8, 128), I32)
    entries = []
    for r in range(ROWS):
        count = spread(lists_ref[r, 16 + step : 17 + step, :])
        star = lists_ref[r, 8 * step : 8 * step + 8, :] - offset
        live = (slot < count) & (star >= 0) & (star < LOCAL)
        at = begin + slot
        high = jnp.where(live, star >> 7, 255).astype(F32)
        low = (star & 127).astype(F32)
        first, second = ((at >> 7) + 1).astype(F32), (at & 127).astype(F32)
        for k in range(8):
            cut = slice(k, k + 1)
            entries.append((high[cut], low[cut], first[cut], second[cut]))
        begin = begin + count
    return scattered(entries, 128)


def rank_map(places, near_ref, base_ref, order_ref, step):
    at_high, at_low = places[0], places[1]
    row = lax.broadcasted_iota(I32, (128, 128), 0)
    lane = lax.broadcasted_iota(I32, (128, 128), 1)
    up_to = (row <= lane).astype(F32).astype(BF16)
    before = (row < lane).astype(F32).astype(BF16)
    below = (lane < row).astype(F32).astype(BF16)
    active = (at_high > 0.0).astype(F32)
    active16 = active.astype(BF16)
    so_far = jnp.dot(active16, up_to, preferred_element_type=F32)
    total = jnp.broadcast_to(so_far[:, 127:128], (128, 128))
    first = jnp.dot(below, total.astype(BF16), preferred_element_type=F32)
    rank = (first + so_far - active).astype(I32)
    near = jnp.where(active > 0.0, rank - (first.astype(I32) >> 6) * 64 + 1, 0)
    near_ref[step] = near
    widest = jnp.max(jnp.max(near.astype(F32), axis=0, keepdims=True), axis=1, keepdims=True)
    ones = jnp.ones((8, 128), F32).astype(BF16)
    totals = lax.dot_general(ones, active16, ADDED, preferred_element_type=F32)
    firsts = jnp.dot(totals.astype(BF16), before, preferred_element_type=F32).astype(I32)
    base_ref[step, 0] = firsts >> 6
    ends = firsts + totals.astype(I32)
    sub = lax.broadcasted_iota(I32, (8, 128), 0)
    base_ref[step, 1] = jnp.where(sub == 0, ends, jnp.broadcast_to(widest, (8, 128)).astype(I32))
    rank_high = jnp.where(active > 0.0, rank >> 7, 255).astype(F32)
    rank_low = (rank & 127).astype(F32)
    entries = []
    for b in range(BLOCKS):
        cut = slice(b, b + 1)
        entries.append((rank_high[cut], rank_low[cut], at_high[cut], at_low[cut]))
    order_ref[step] = scattered(entries, 64)


def own_stars(lists_ref, place):
    lane = lax.broadcasted_iota(I32, (8, 128), 1)
    sub = lax.broadcasted_iota(I32, (8, 128), 0)
    position = place * PART + (sub & 3) * 128 + lane
    before = jnp.zeros((8, 128), I32)
    which = jnp.zeros((8, 128), I32)
    start = jnp.zeros((8, 128), I32)
    for r in range(ROWS):
        count = jnp.where(sub < 4, spread(lists_ref[r, 16:17, :]), spread(lists_ref[r, 17:18, :]))
        end = before + count
        passed = position >= end
        which = which + passed.astype(I32)
        start = jnp.where(passed, end, start)
        before = end
    flat = which * CAP + position - start
    high, low = flat >> 7, flat & 127
    stars = jnp.zeros((8, 128), I32)
    for r in range(ROWS):
        for k in range(8):
            row = jnp.where(
                sub < 4, spread(lists_ref[r, k : k + 1, :]), spread(lists_ref[r, 8 + k : 9 + k, :])
            )
            stars = jnp.where(high == r * 8 + k, lane_pick(row, low), stars)
    return stars


def both_halves(x, step):
    part = x[4 * step : 4 * step + 4]
    return jnp.concatenate([part, part], axis=0)


def fetch(stars, pairs):
    high, low = stars >> 7, stars & 127

    def look(g, found):
        for u in range(8):
            b = g * 8 + u
            here = high == b
            found = tuple(
                jnp.where(here, lane_pick(pair(b), low), old) for pair, old in zip(pairs, found)
            )
        return found

    return lax.fori_loop(0, BLOCKS // 8, look, tuple(jnp.zeros((8, 128), F32) for _ in pairs))


def two_rows(sub, a, b):
    return jnp.where(sub < 4, spread(a), spread(b))


def unpack(pairs, out_ref):
    for p, pair in enumerate(pairs):
        for half in range(2):
            for s in range(4):
                out_ref[2 * p + half : 2 * p + half + 1, s * 128 : s * 128 + 128] = pair[
                    4 * half + s : 4 * half + s + 1
                ]


def predict(phase, derivs, time, now):
    d = now - time
    x, v, a, j = phase[0:3], phase[3:6], derivs[0:3], derivs[3:6]
    return x + d * (v + d * (a / 2.0 + d * j / 6.0)), v + d * (a + d * j / 2.0)


def correct(x, v, old_acc, old_jerk, h, forces):
    new_acc, new_jerk = forces[0:3], forces[3:6]
    change = old_acc - new_acc
    second = (-6.0 * change - h * (4.0 * old_jerk + 2.0 * new_jerk)) / (h * h)
    third = (12.0 * change + 6.0 * h * (old_jerk + new_jerk)) / (h * h * h)
    h2 = h * h
    h3 = h2 * h
    h4 = h3 * h
    h5 = h4 * h
    x = x + h4 / 24.0 * second + h5 / 120.0 * third
    v = v + h3 / 6.0 * second + h4 / 24.0 * third
    return x, v, new_acc, new_jerk


PAIRS = ((0, 0), (0, 1), (0, 2), (1, 0), (1, 1), (2, 0))


def split3(x):
    high = x.astype(BF16).astype(F32)
    rest = x - high
    middle = rest.astype(BF16).astype(F32)
    return high, middle, rest - middle


def split2(x, low_kind):
    high = x.astype(BF16)
    return high, (x - high.astype(F32)).astype(low_kind)


def split8(x):
    parts = []
    for _ in range(4):
        parts.append(x.astype(FINE8).astype(F32))
        x = x - parts[-1]
    return parts


def squares(x, v):
    xx = x * x
    xv = x * v
    return xx[0:1] + xx[1:2] + xx[2:3], xv[0:1] + xv[1:2] + xv[2:3]


def star_features(x, v):
    width = x.shape[1]
    parts = split3(jnp.concatenate([x, v, jnp.zeros((2, width), F32)], axis=0))
    xx, xv = squares(x, v)
    one = jnp.ones((3, width), F32)
    extra = jnp.concatenate(list(split3(xx)) + list(split3(xv)) + [one, one, rows_of(12, 16, width)], axis=0)
    return jnp.concatenate([parts[a] for a, _ in PAIRS] + [extra], axis=0)


def active_features(x, v):
    width = x.shape[1]
    xp, vp = split3(x), split3(v)
    xx, xv = squares(x, v)
    one, none3, none5 = jnp.ones((3, width), F32), rows_of(0, 3, width), rows_of(0, 5, width)
    dist, both = [], []
    for _, b in PAIRS:
        dist += [-2.0 * xp[b], none5]
        both += [-vp[b], -xp[b], rows_of(0, 2, width)]
    dist += [one, none3] + list(split3(xx + softening)) + [none3, rows_of(12, 16, width)]
    both += [none3, one, none3] + list(split3(xv)) + [rows_of(12, 16, width)]
    dist = jnp.concatenate(dist, axis=0) * DIST_SCALE
    both = jnp.concatenate(both, axis=0) * BOTH_SCALE
    return dist.astype(BF16), both.astype(BF16)


def prepare(first, chunk, count, pred_of, weights, weights8, features):
    def one_chunk(n, _):
        x, v, mass = pred_of(n)
        at = pl.ds(pl.multiple_of(first + n * chunk, chunk), chunk)
        ones, none = jnp.ones((1, chunk), F32), jnp.zeros((1, chunk), F32)
        scaled = jnp.concatenate([x, v, ones, none], axis=0) * mass
        share = scaled / N_STARS
        high = share.astype(BF16).astype(F32)
        weights[:, at] = jnp.concatenate([high, share - high], axis=0).astype(BF16)
        weights8[:, at] = jnp.concatenate(split8(jnp.clip(scaled, -240.0, 240.0)), axis=0).astype(FINE8)
        features[at, :] = star_features(x, v).T.astype(BF16)
        return 0

    lax.fori_loop(0, count, one_chunk, 0)


def force_sums(deep, weights, weights8, features, dist_own, both_own, totals, own, part, after):
    def quarter(t, _):
        h = t >> 1
        cut = pl.ds(pl.multiple_of(h * HALF, HALF), HALF)
        fresh = (t & 1) == 0

        def sums(n, total):
            lanes = pl.ds(pl.multiple_of(((t & 1) * 2 + n) * deep, deep), deep)
            factor = features[lanes, :]
            dist = jnp.dot(factor, dist_own[:, cut], preferred_element_type=F32)
            both = jnp.dot(factor, both_own[:, cut], preferred_element_type=F32)
            inverse = lax.rsqrt(jnp.maximum(dist, softening * DIST_SCALE))
            inverse_sq = inverse * inverse
            weight = inverse * inverse_sq
            radial = (weight * inverse_sq) * both
            w_high, w_low = split2(weight, FINE8)
            u_high, u_low = split2(radial, WIDE8)
            dot = functools.partial(jnp.dot, preferred_element_type=F32)
            left, left8 = weights[:, lanes], weights8[:, lanes]
            new = dot(left, w_high), dot(left, u_high), dot(left8, w_low), dot(left8, u_low)
            return tuple(a + b for a, b in zip(total, new))

        found = lax.fori_loop(0, 2, sums, tuple(jnp.where(fresh, 0.0, held[...]) for held in totals))
        for n in range(4):
            totals[n][...] = found[n]

        @pl.when((t & 1) == 1)
        def _():
            def whole(high, low, back):
                high = high[0:8] + high[8:16]
                low = low[0:8] + low[8:16] + low[16:24] + low[24:32]
                return (high + low / N_STARS) * back

            w_all = whole(found[0], found[2], WEIGHT_BACK)
            u_all = whole(found[1], found[3], 1.0)
            mine = own[:, cut]
            x, v = mine[0:3], mine[3:6]
            acc = w_all[0:3] - x * w_all[6:7]
            jerk = w_all[3:6] - v * w_all[6:7] - 3.0 * (u_all[0:3] - x * u_all[6:7])
            part[pl.ds(h, 1)] = jnp.concatenate([acc, jerk, jnp.zeros((2, HALF), F32)], axis=0)[None]

        for number, action in after.items():
            pl.when(t == number)(action)
        return 0

    lax.fori_loop(0, 4, quarter, 0)


def sum_of(landing):
    total = landing[0]
    for c in range(1, COLS):
        total = total + landing[c]
    return total


def packed(x, v, a, j):
    rest = jnp.concatenate([a[2:3], j], axis=0)
    right = jnp.concatenate([rest[:, 0:128], rest[:, 128:256]], axis=0)
    return jnp.concatenate([jnp.concatenate([x, v, a[0:2]], axis=0), right], axis=1)


def take_moved(high, low, sub, rows_at):
    def look(r, found):
        for k in range(4):
            here = high == r * 4 + k
            found = tuple(
                jnp.where(here, lane_pick(two_rows(sub, *pair), low), was)
                for pair, was in zip(rows_at(r, k), found)
            )
        return found

    return lax.fori_loop(0, ROWS, look, tuple(jnp.zeros((8, 128), F32) for _ in range(3)))


def steps_kernel(
    index_ref, count_ref, phase_far, derivs_far, time_far, mass_far,
    all0_ref, all1_ref, near_ref, base_ref, order_ref,
    phase_ref, derivs_ref, time_ref, mass_ref, lists_own, lists_ref, places,
    pred, lead0, land_lead, picks0, picks1, land0, land1, part0, part1, landf0, landf1, lead, lead_all, mine0, mine1,
    old, fix, own, accel, weights, weights8, features, dist_own, both_own, w_high, u_high, w_low, u_low,
    s_in, s_list, r_list, s_lead0, r_lead0, s_pick0, r_pick0, s_pick1, r_pick1, s_for, r_for, s_lead, r_lead, s_all, r_all,
):
    row, col = lax.axis_index("row"), lax.axis_index("col")
    barrier = pltpu.get_barrier_semaphore()
    everyone = partners_of("row", ROWS, row) + partners_of("col", COLS, col)
    for _, partner in everyone:
        pl.semaphore_signal(barrier, inc=1, device_id=partner, device_id_type=MESH)
    inputs = [
        pltpu.make_async_copy(far, near, s_in.at[n])
        for n, (far, near) in enumerate(
            [(phase_far, phase_ref), (derivs_far, derivs_ref), (time_far, time_ref), (mass_far, mass_ref)]
        )
    ]
    for copy in inputs:
        copy.start()
    offset = col * LOCAL
    chunk = 2048
    sub = lax.broadcasted_iota(I32, (8, 128), 0)
    for step in range(2):
        for k in range(8):
            lists_own[8 * step + k : 8 * step + k + 1, :] = index_ref[step, 0:1, k * 128 : k * 128 + 128]
        lists_own[16 + step : 17 + step, :] = jnp.broadcast_to(count_ref[0:1, step : step + 1], (1, 128))
    lists_own[18:24, :] = jnp.zeros((6, 128), I32)
    pl.semaphore_wait(barrier, len(everyone))
    lists = ("row", ROWS, row, lists_own, lists_ref, s_list, r_list)
    exchange(*lists)
    for copy in inputs:
        copy.wait()

    def first_stars(n):
        lanes = pl.ds(pl.multiple_of(n * chunk, chunk), chunk)
        x, v = predict(phase_ref[:, lanes], derivs_ref[:, lanes], time_ref[:, lanes], block_times[0])
        pred[:, lanes] = jnp.concatenate([x, v], axis=0)
        return x, v, mass_ref[:, lanes]

    prepare(0, chunk, LOCAL // chunk, first_stars, weights, weights8, features)
    arrived(*lists)

    def block(b):
        return pl.ds(pl.multiple_of(b * 128, 128), 128)

    def row_pairs(ref):
        return [
            lambda b, c=c: two_rows(sub, ref[c : c + 1, block(b)], ref[c + 1 : c + 2, block(b)])
            for c in (0, 2, 4)
        ]

    rest_pairs = row_pairs(derivs_ref) + [lambda b: two_rows(sub, time_ref[:, block(b)], mass_ref[:, block(b)])]
    local = own_stars(lists_ref, row) - offset
    for p, value in enumerate(fetch(both_halves(local, 0), row_pairs(pred))):
        lead0[p] = value
    lead_picks = ("col", COLS, col, lead0, land_lead, s_lead0, r_lead0)
    exchange(*lead_picks)
    for p, value in enumerate(fetch(both_halves(local, 0), rest_pairs)):
        picks0[p] = value
    first_picks = ("col", COLS, col, picks0, land0, s_pick0, r_pick0)
    exchange(*first_picks)

    found = place_map(lists_ref, 0, offset)
    places[0, 0], places[0, 1] = found[:, 0:128], found[:, 128:256]

    arrived(*lead_picks)
    total = sum_of(land_lead)
    unpack([total[p] for p in range(3)], fix)
    def force_copies(step, half):
        part, landing = (part0, landf0) if step == 0 else (part1, landf1)
        n = 2 * step + half
        return ("col", COLS, col, part.at[half], landing.at[half], s_for.at[n], r_for.at[n])

    def lead_copies(half):
        return ("row", ROWS, row, lead.at[half], lead_all.at[half], s_lead.at[half], r_lead.at[half])

    def row_copies(step, half):
        mine, landing = (mine0, all0_ref) if step == 0 else (mine1, all1_ref)
        n = 2 * step + half
        return ("row", ROWS, row, mine.at[half], landing.at[half], s_all.at[n], r_all.at[n])

    def set_own(x, v):
        own[...] = jnp.concatenate([x, v, jnp.zeros((2, PART), F32)], axis=0)
        dist_own[...], both_own[...] = active_features(x, v)

    sums = (weights, weights8, features, dist_own, both_own, (w_high, u_high, w_low, u_low), own)
    set_own(fix[0:3], fix[3:6])

    def first_old():
        exchange(*force_copies(0, 0))
        arrived(*first_picks)
        total = sum_of(land0)
        unpack([total[p] for p in range(4)], accel)

    def first_corrected(half):
        arrived(*force_copies(0, half))
        cut = slice(half * HALF, half * HALF + HALF)
        x, v, a, j = correct(
            own[0:3, cut], own[3:6, cut], accel[0:3, cut], accel[3:6, cut],
            block_times[0] - accel[6:7, cut], sum_of(landf0.at[half]),
        )
        x_next, v_next = predict(
            jnp.concatenate([x, v], axis=0), jnp.concatenate([a, j], axis=0), block_times[0], block_times[1]
        )
        lead[half] = jnp.concatenate([x_next, v_next, accel[7:8, cut], jnp.zeros((1, HALF), F32)], axis=0)
        exchange(*lead_copies(half))
        mine0[half] = packed(x, v, a, j)
        exchange(*row_copies(0, half))

    force_sums(
        4096, *sums, part0,
        {1: first_old, 2: lambda: first_corrected(0)},
    )
    exchange(*force_copies(0, 1))
    pairs = row_pairs(phase_ref) + rest_pairs
    pairs.append(lambda b: two_rows(sub, places[0, 0, pl.ds(b, 1), :], places[0, 1, pl.ds(b, 1), :]))
    for p, value in enumerate(fetch(both_halves(local, 1), pairs)):
        picks1[p] = value
    second_picks = ("col", COLS, col, picks1, land1, s_pick1, r_pick1)
    exchange(*second_picks)
    first_corrected(1)

    def second_stars(n):
        lanes = pl.ds(pl.multiple_of(n * chunk, chunk), chunk)
        x, v = predict(phase_ref[:, lanes], derivs_ref[:, lanes], time_ref[:, lanes], block_times[1])
        moved = jnp.concatenate([places[0, 0, pl.ds(n * 16 + k, 1), :] for k in range(16)], axis=1)
        return x, v, jnp.where(moved > 0.0, 0.0, mass_ref[:, lanes])

    prepare(0, chunk, LOCAL // chunk, second_stars, weights, weights8, features)
    arrived(*second_picks)
    total = sum_of(land1)
    unpack([total[p] for p in range(8)], old)
    high = both_halves(total[7], 0).astype(I32) - 1
    low = both_halves(total[7], 1).astype(I32)
    for half in range(2):
        arrived(*lead_copies(half))

    def moved_stars(n):
        state = lead_all[pl.ds(n & 1, 1), pl.ds(2 * col + (n >> 1), 1)][0, 0]
        return state[0:3], state[3:6], state[6:7]

    prepare(LOCAL, HALF, 4, moved_stars, weights, weights8, features)

    def lead_rows(r, k):
        cut = slice((k % 2) * 128, (k % 2) * 128 + 128)
        return [(lead_all[k // 2, r, c : c + 1, cut], lead_all[k // 2, r, c + 1 : c + 2, cut]) for c in (0, 2, 4)]

    unpack(take_moved(high, low, sub, lead_rows), fix)
    moved = old[14:15] > 0.0
    x_own, v_own = predict(old[0:6], old[6:12], old[12:13], block_times[1])
    set_own(jnp.where(moved, fix[0:3], x_own), jnp.where(moved, fix[3:6], v_own))

    def rest_rows(r, k):
        half, at = k // 2, 4 * (k % 2)
        cut = slice((k % 2) * 128, (k % 2) * 128 + 128)
        return [
            (all0_ref[half, r, 6:7, cut], all0_ref[half, r, 7:8, cut]),
            (all0_ref[half, r, at : at + 1, 256:384], all0_ref[half, r, at + 1 : at + 2, 256:384]),
            (all0_ref[half, r, at + 2 : at + 3, 256:384], all0_ref[half, r, at + 3 : at + 4, 256:384]),
        ]

    def second_old():
        exchange(*force_copies(1, 0))
        for half in range(2):
            arrived(*row_copies(0, half))
        unpack(take_moved(high, low, sub, rest_rows), fix)
        moved = old[14:15] > 0.0
        h = block_times[1] - jnp.where(moved, block_times[0], old[12:13])
        accel[...] = jnp.concatenate(
            [jnp.where(moved, fix[0:3], old[6:9]), jnp.where(moved, fix[3:6], old[9:12]), h, h], axis=0
        )

    def second_corrected(half):
        arrived(*force_copies(1, half))
        cut = slice(half * HALF, half * HALF + HALF)
        mine1[half] = packed(
            *correct(
                own[0:3, cut], own[3:6, cut], accel[0:3, cut], accel[3:6, cut], accel[6:7, cut],
                sum_of(landf1.at[half]),
            )
        )
        exchange(*row_copies(1, half))

    force_sums(
        (LOCAL + 2 * PART) // 4, *sums, part1, {1: second_old, 2: lambda: second_corrected(0)}
    )
    exchange(*force_copies(1, 1))
    found = place_map(lists_ref, 1, offset)
    places[1, 0], places[1, 1] = found[:, 0:128], found[:, 128:256]
    second_corrected(1)
    rank_map(places[0], near_ref, base_ref, order_ref, 0)
    rank_map(places[1], near_ref, base_ref, order_ref, 1)
    for half in range(2):
        arrived(*row_copies(1, half))
    for copies in [lists, lead_picks, first_picks, second_picks]:
        sent(*copies)
    for half in range(2):
        sent(*lead_copies(half))
        for step in range(2):
            sent(*force_copies(step, half))
            sent(*row_copies(step, half))


def both_steps(index, count, phase, derivs, time, masses):
    stars = LOCAL + 2 * PART
    vmem = [
        ((6, LOCAL), F32),
        ((6, LOCAL), F32),
        ((1, LOCAL), F32),
        ((1, LOCAL), F32),
        ((24, 128), I32),
        ((ROWS, 24, 128), I32),
        ((2, 2, 128, 128), F32),
        ((6, LOCAL), F32),
        ((3, 8, 128), F32),
        ((COLS, 3, 8, 128), F32),
        ((4, 8, 128), F32),
        ((8, 8, 128), F32),
        ((COLS, 4, 8, 128), F32),
        ((COLS, 8, 8, 128), F32),
        ((2, 8, HALF), F32),
        ((2, 8, HALF), F32),
        ((2, COLS, 8, HALF), F32),
        ((2, COLS, 8, HALF), F32),
        ((2, 8, HALF), F32),
        ((2, ROWS, 8, HALF), F32),
        ((2, 8, 384), F32),
        ((2, 8, 384), F32),
        ((16, PART), F32),
        ((8, PART), F32),
        ((8, PART), F32),
        ((8, PART), F32),
        ((16, stars), BF16),
        ((32, stars), FINE8),
        ((stars, 64), BF16),
        ((64, PART), BF16),
        ((64, PART), BF16),
        ((16, HALF), F32),
        ((16, HALF), F32),
        ((32, HALF), F32),
        ((32, HALF), F32),
    ]
    sems = [(4,)] + [(ROWS,)] * 2 + [(COLS,)] * 6 + [(4, COLS)] * 2 + [(2, ROWS)] * 2 + [(4, ROWS)] * 2
    return pl.pallas_call(
        steps_kernel,
        out_shape=[
            jax.ShapeDtypeStruct((2, ROWS, 8, 384), F32),
            jax.ShapeDtypeStruct((2, ROWS, 8, 384), F32),
            jax.ShapeDtypeStruct((2, 128, 128), I32),
            jax.ShapeDtypeStruct((2, 2, 8, 128), I32),
            jax.ShapeDtypeStruct((2, 64, 256), F32),
        ],
        in_specs=in_vmem(2) + [pl.BlockSpec(memory_space=pl.ANY)] * 4,
        out_specs=in_vmem(5),
        scratch_shapes=[pltpu.VMEM(shape, kind) for shape, kind in vmem]
        + [pltpu.SemaphoreType.DMA(shape) for shape in sems],
        compiler_params=params(collective_id=0, has_side_effects=True),
        name="both_steps",
    )(index, count, phase, derivs, time, masses)


def collect(step, count, order_ref, all_ref, sorted_ref):
    def one_block(n, _):
        group = order_ref[step, pl.ds(pl.multiple_of((n >> 3) * 8, 8), 8), :]
        mask = lax.broadcasted_iota(I32, (8, 256), 0) == (n & 7)
        digits = jnp.sum(jnp.where(mask, group, 0.0), axis=0, keepdims=True)
        high = spread(digits[:, 0:128]).astype(I32) - 1
        low = spread(digits[:, 128:256]).astype(I32)
        upper = jnp.zeros((8, 128), F32)
        lower = jnp.zeros((8, 128), F32)
        shifted = high - (lax.broadcasted_iota(I32, (8, 128), 0) >> 2)
        for b in range(64):
            r, half, k = b // 4, (b % 4) // 2, b % 2
            upper = jnp.where(high == b, lane_pick(all_ref[half, r, :, k * 128 : k * 128 + 128], low), upper)
            if k == 0:
                lower = jnp.where(shifted == b, lane_pick(all_ref[half, r, :, 256:384], low), lower)
        blank = jnp.zeros((2, 128), F32)
        rest = lower[0:4] + lower[4:8]
        sorted_ref[step, n, 0:8, :] = upper
        sorted_ref[step, n, 8:16, :] = jnp.concatenate([upper[6:8], rest, blank], axis=0)
        return 0

    lax.fori_loop(0, (count + 127) // 128, one_block, 0)


def last_kernel(
    base_ref, near_ref, order_ref, all0_ref, all1_ref, phase_ref, derivs_ref, time_ref,
    phase_out, derivs_out, time_out, sorted_ref,
):
    collect(0, base_ref[0, 1, 0, 127], order_ref, all0_ref, sorted_ref)
    collect(1, base_ref[1, 1, 0, 127], order_ref, all1_ref, sorted_ref)

    lane = lax.broadcasted_iota(I32, (8, 128), 1)
    run = 16

    def put(g, _, wide):
        for u in range(run):
            b = g * run + u
            lanes = pl.ds(pl.multiple_of(b * 128, 128), 128)
            blank = jnp.zeros((2, 128), F32)
            phase = jnp.concatenate([phase_ref[:, lanes], blank], axis=0)
            derivs = jnp.concatenate([derivs_ref[:, lanes], blank], axis=0)
            time = time_ref[:, lanes]
            for step in range(2):
                base = base_ref[step, 0, 0, b]
                n, shift = base >> 1, (base & 1) * 64
                at = spread(near_ref[step, pl.ds(b, 1), :]) - 1
                low = (at + shift) & 127
                behind = lane >= shift

                def chosen(rows, was):
                    here, then = sorted_ref[step, n, rows, :], sorted_ref[step, n + 1, rows, :]
                    new = jnp.where(at >= 0, lane_pick(jnp.where(behind, here, then), low), was)
                    if wide:
                        last = sorted_ref[step, n + 2, rows, :]
                        new = jnp.where(at >= 128, lane_pick(jnp.where(behind, then, last), low), new)
                    return new

                phase = chosen(slice(0, 8), phase)
                derivs = chosen(slice(8, 16), derivs)
                time = jnp.where(at[0:1] >= 0, block_times[step], time)
            phase_out[:, lanes] = phase[0:6]
            derivs_out[:, lanes] = derivs[0:6]
            time_out[:, lanes] = time
        return 0

    wide = (base_ref[0, 1, 1, 0] > 128) | (base_ref[1, 1, 1, 0] > 128)

    @pl.when(wide)
    def _():
        lax.fori_loop(0, BLOCKS // run, functools.partial(put, wide=True), 0)

    @pl.when(jnp.logical_not(wide))
    def _():
        lax.fori_loop(0, BLOCKS // run, functools.partial(put, wide=False), 0)


def last_update(base, near, order, all0, all1, phase, derivs, time):
    return pl.pallas_call(
        last_kernel,
        out_shape=[
            jax.ShapeDtypeStruct((6, LOCAL), F32),
            jax.ShapeDtypeStruct((6, LOCAL), F32),
            jax.ShapeDtypeStruct((1, LOCAL), F32),
        ],
        in_specs=[pl.BlockSpec(memory_space=pltpu.SMEM)] + in_vmem(7),
        out_specs=in_vmem(3),
        scratch_shapes=[pltpu.VMEM((2, 68, 16, 128), F32)],
        compiler_params=params(),
        name="last_update",
    )(base, near, order, all0, all1, phase, derivs, time)


def body(phase_space, derivs, star_time, masses, active_index, active_count):
    time = star_time.reshape(1, LOCAL)
    masses = masses.reshape(1, LOCAL)
    all0, all1, near, base, order = both_steps(
        active_index, active_count.reshape(1, 2), phase_space, derivs, time, masses
    )
    phase_space, derivs, time = last_update(base, near, order, all0, all1, phase_space, derivs, time)
    return phase_space, derivs, time.reshape(LOCAL)


def solution(mesh):
    return jax.shard_map(
        body,
        mesh=mesh,
        in_specs=(
            P(None, "col"),
            P(None, "col"),
            P("col"),
            P("col"),
            P(None, "row", None),
            P(None, "row"),
        ),
        out_specs=(P(None, "col"), P(None, "col"), P("col")),
        check_vma=False,
    )
```

```python
import functools

import jax
import jax.numpy as jnp
from jax import lax
from jax.experimental import pallas as pl
from jax.experimental.pallas import tpu as pltpu
from jax.sharding import PartitionSpec as P

F32 = jnp.float32
BF16 = jnp.bfloat16
I32 = jnp.int32
FINE8 = jnp.float8_e4m3fn
WIDE8 = jnp.float8_e5m2
DIST_SCALE = 2.0**-4
BOTH_SCALE = 2.0**-10
WEIGHT_BACK = 2.0**-6
softening = 0.01
block_times = (0.125, 0.25)
ROWS = 16
COLS = 8
CAP = 1024
PART = 512
HALF = 256
LOCAL = 16384
BLOCKS = LOCAL // 128
N_STARS = ROWS * PART * 16
MESH = pl.DeviceIdType.MESH
ADDED = (((1,), (1,)), ((), ()))


def rows_of(first, last, width):
    return jnp.zeros((last - first, width), F32)


def in_vmem(n):
    return [pl.BlockSpec(memory_space=pltpu.VMEM)] * n


def params(**more):
    return pltpu.CompilerParams(vmem_limit_bytes=56 * 2**20, **more)


def partners_of(axis, size, place):
    return [(k, {axis: lax.rem(place + k, size)}) for k in range(1, size)]


def exchange(axis, size, place, source, landing, send_sem, recv_sem):
    for k, partner in partners_of(axis, size, place):
        pltpu.make_async_remote_copy(
            src_ref=source,
            dst_ref=landing.at[place],
            send_sem=send_sem.at[k],
            recv_sem=recv_sem.at[place],
            device_id=partner,
            device_id_type=MESH,
        ).start()
    landing[pl.ds(place, 1)] = source[...][None]


def sent(axis, size, place, source, landing, send_sem, recv_sem):
    for k, partner in partners_of(axis, size, place):
        pltpu.make_async_remote_copy(
            src_ref=source,
            dst_ref=landing.at[place],
            send_sem=send_sem.at[k],
            recv_sem=recv_sem.at[place],
            device_id=partner,
            device_id_type=MESH,
        ).wait_send()


def arrived(axis, size, place, source, landing, send_sem, recv_sem):
    for k, partner in partners_of(axis, size, place):
        slot = lax.rem(place + k, size)
        pltpu.make_async_remote_copy(
            src_ref=source,
            dst_ref=landing.at[slot],
            send_sem=send_sem.at[k],
            recv_sem=recv_sem.at[slot],
            device_id=partner,
            device_id_type=MESH,
        ).wait_recv()


def lane_pick(table, lanes):
    return jnp.take_along_axis(table, lanes, axis=1, mode="promise_in_bounds")


def spread(row):
    return jnp.broadcast_to(row, (8, 128))


def hot(index_row, count):
    kinds = lax.broadcasted_iota(I32, (count, 128), 0).astype(F32).astype(BF16)
    return jnp.broadcast_to(index_row, (count, 128)).astype(BF16) == kinds


def scattered(entries, high_count):
    one, zero = jnp.ones((), BF16), jnp.zeros((), BF16)
    left, right = [], []
    for high, low, first, second in entries:
        left.append(jnp.where(hot(high, high_count), one, zero))
        at_low = hot(low, 128)
        a = jnp.broadcast_to(first, (128, 128)).astype(BF16)
        b = jnp.broadcast_to(second, (128, 128)).astype(BF16)
        right.append(jnp.concatenate([jnp.where(at_low, a, zero), jnp.where(at_low, b, zero)], axis=0))
    return lax.dot_general(
        jnp.concatenate(left, axis=1), jnp.concatenate(right, axis=1), ADDED, preferred_element_type=F32
    )


def place_map(lists_ref, step, offset):
    slot = lax.broadcasted_iota(I32, (8, 128), 0) * 128 + lax.broadcasted_iota(I32, (8, 128), 1)
    begin = jnp.zeros((8, 128), I32)
    entries = []
    for r in range(ROWS):
        count = spread(lists_ref[r, 16 + step : 17 + step, :])
        star = lists_ref[r, 8 * step : 8 * step + 8, :] - offset
        live = (slot < count) & (star >= 0) & (star < LOCAL)
        at = begin + slot
        high = jnp.where(live, star >> 7, 255).astype(F32)
        low = (star & 127).astype(F32)
        first, second = ((at >> 7) + 1).astype(F32), (at & 127).astype(F32)
        for k in range(8):
            cut = slice(k, k + 1)
            entries.append((high[cut], low[cut], first[cut], second[cut]))
        begin = begin + count
    return scattered(entries, 128)


def rank_map(places, near_ref, base_ref, order_ref, step):
    at_high, at_low = places[0], places[1]
    row = lax.broadcasted_iota(I32, (128, 128), 0)
    lane = lax.broadcasted_iota(I32, (128, 128), 1)
    up_to = (row <= lane).astype(F32).astype(BF16)
    before = (row < lane).astype(F32).astype(BF16)
    below = (lane < row).astype(F32).astype(BF16)
    active = (at_high > 0.0).astype(F32)
    active16 = active.astype(BF16)
    so_far = jnp.dot(active16, up_to, preferred_element_type=F32)
    total = jnp.broadcast_to(so_far[:, 127:128], (128, 128))
    first = jnp.dot(below, total.astype(BF16), preferred_element_type=F32)
    rank = (first + so_far - active).astype(I32)
    near = jnp.where(active > 0.0, rank - (first.astype(I32) >> 6) * 64 + 1, 0)
    near_ref[step] = near
    widest = jnp.max(jnp.max(near.astype(F32), axis=0, keepdims=True), axis=1, keepdims=True)
    ones = jnp.ones((8, 128), F32).astype(BF16)
    totals = lax.dot_general(ones, active16, ADDED, preferred_element_type=F32)
    firsts = jnp.dot(totals.astype(BF16), before, preferred_element_type=F32).astype(I32)
    base_ref[step, 0] = firsts >> 6
    ends = firsts + totals.astype(I32)
    sub = lax.broadcasted_iota(I32, (8, 128), 0)
    base_ref[step, 1] = jnp.where(sub == 0, ends, jnp.broadcast_to(widest, (8, 128)).astype(I32))
    rank_high = jnp.where(active > 0.0, rank >> 7, 255).astype(F32)
    rank_low = (rank & 127).astype(F32)
    entries = []
    for b in range(BLOCKS):
        cut = slice(b, b + 1)
        entries.append((rank_high[cut], rank_low[cut], at_high[cut], at_low[cut]))
    order_ref[step] = scattered(entries, 64)


def own_stars(lists_ref, place):
    lane = lax.broadcasted_iota(I32, (8, 128), 1)
    sub = lax.broadcasted_iota(I32, (8, 128), 0)
    position = place * PART + (sub & 3) * 128 + lane
    before = jnp.zeros((8, 128), I32)
    which = jnp.zeros((8, 128), I32)
    start = jnp.zeros((8, 128), I32)
    for r in range(ROWS):
        count = jnp.where(sub < 4, spread(lists_ref[r, 16:17, :]), spread(lists_ref[r, 17:18, :]))
        end = before + count
        passed = position >= end
        which = which + passed.astype(I32)
        start = jnp.where(passed, end, start)
        before = end
    flat = which * CAP + position - start
    high, low = flat >> 7, flat & 127
    stars = jnp.zeros((8, 128), I32)
    for r in range(ROWS):
        for k in range(8):
            row = jnp.where(
                sub < 4, spread(lists_ref[r, k : k + 1, :]), spread(lists_ref[r, 8 + k : 9 + k, :])
            )
            stars = jnp.where(high == r * 8 + k, lane_pick(row, low), stars)
    return stars


def both_halves(x, step):
    part = x[4 * step : 4 * step + 4]
    return jnp.concatenate([part, part], axis=0)


def fetch(stars, pairs):
    high, low = stars >> 7, stars & 127

    def look(g, found):
        for u in range(8):
            b = g * 8 + u
            here = high == b
            found = tuple(
                jnp.where(here, lane_pick(pair(b), low), old) for pair, old in zip(pairs, found)
            )
        return found

    return lax.fori_loop(0, BLOCKS // 8, look, tuple(jnp.zeros((8, 128), F32) for _ in pairs))


def two_rows(sub, a, b):
    return jnp.where(sub < 4, spread(a), spread(b))


def unpack(pairs, out_ref):
    for p, pair in enumerate(pairs):
        for half in range(2):
            for s in range(4):
                out_ref[2 * p + half : 2 * p + half + 1, s * 128 : s * 128 + 128] = pair[
                    4 * half + s : 4 * half + s + 1
                ]


def predict(phase, derivs, time, now):
    d = now - time
    x, v, a, j = phase[0:3], phase[3:6], derivs[0:3], derivs[3:6]
    return x + d * (v + d * (a / 2.0 + d * j / 6.0)), v + d * (a + d * j / 2.0)


def correct(x, v, old_acc, old_jerk, h, forces):
    new_acc, new_jerk = forces[0:3], forces[3:6]
    change = old_acc - new_acc
    second = (-6.0 * change - h * (4.0 * old_jerk + 2.0 * new_jerk)) / (h * h)
    third = (12.0 * change + 6.0 * h * (old_jerk + new_jerk)) / (h * h * h)
    h2 = h * h
    h3 = h2 * h
    h4 = h3 * h
    h5 = h4 * h
    x = x + h4 / 24.0 * second + h5 / 120.0 * third
    v = v + h3 / 6.0 * second + h4 / 24.0 * third
    return x, v, new_acc, new_jerk


PAIRS = ((0, 0), (0, 1), (0, 2), (1, 0), (1, 1), (2, 0))


def split3(x):
    high = x.astype(BF16).astype(F32)
    rest = x - high
    middle = rest.astype(BF16).astype(F32)
    return high, middle, rest - middle


def split2(x, low_kind):
    high = x.astype(BF16)
    return high, (x - high.astype(F32)).astype(low_kind)


def split8(x):
    parts = []
    for _ in range(4):
        parts.append(x.astype(FINE8).astype(F32))
        x = x - parts[-1]
    return parts


def squares(x, v):
    xx = x * x
    xv = x * v
    return xx[0:1] + xx[1:2] + xx[2:3], xv[0:1] + xv[1:2] + xv[2:3]


def star_features(x, v):
    width = x.shape[1]
    parts = split3(jnp.concatenate([x, v, jnp.zeros((2, width), F32)], axis=0))
    xx, xv = squares(x, v)
    one = jnp.ones((3, width), F32)
    extra = jnp.concatenate(list(split3(xx)) + list(split3(xv)) + [one, one, rows_of(12, 16, width)], axis=0)
    return jnp.concatenate([parts[a] for a, _ in PAIRS] + [extra], axis=0)


def active_features(x, v):
    width = x.shape[1]
    xp, vp = split3(x), split3(v)
    xx, xv = squares(x, v)
    one, none3, none5 = jnp.ones((3, width), F32), rows_of(0, 3, width), rows_of(0, 5, width)
    dist, both = [], []
    for _, b in PAIRS:
        dist += [-2.0 * xp[b], none5]
        both += [-vp[b], -xp[b], rows_of(0, 2, width)]
    dist += [one, none3] + list(split3(xx + softening)) + [none3, rows_of(12, 16, width)]
    both += [none3, one, none3] + list(split3(xv)) + [rows_of(12, 16, width)]
    dist = jnp.concatenate(dist, axis=0) * DIST_SCALE
    both = jnp.concatenate(both, axis=0) * BOTH_SCALE
    return dist.astype(BF16), both.astype(BF16)


def prepare(first, chunk, count, pred_of, weights, weights8, features):
    def one_chunk(n, _):
        x, v, mass = pred_of(n)
        at = pl.ds(pl.multiple_of(first + n * chunk, chunk), chunk)
        ones, none = jnp.ones((1, chunk), F32), jnp.zeros((1, chunk), F32)
        scaled = jnp.concatenate([x, v, ones, none], axis=0) * mass
        share = scaled / N_STARS
        high = share.astype(BF16).astype(F32)
        weights[:, at] = jnp.concatenate([high, share - high], axis=0).astype(BF16)
        weights8[:, at] = jnp.concatenate(split8(jnp.clip(scaled, -240.0, 240.0)), axis=0).astype(FINE8)
        features[at, :] = star_features(x, v).T.astype(BF16)
        return 0

    lax.fori_loop(0, count, one_chunk, 0)


def force_sums(deep, weights, weights8, features, dist_own, both_own, totals, own, part, after):
    def quarter(t, _):
        h = t >> 1
        cut = pl.ds(pl.multiple_of(h * HALF, HALF), HALF)
        fresh = (t & 1) == 0

        def sums(n, total):
            lanes = pl.ds(pl.multiple_of(((t & 1) * 2 + n) * deep, deep), deep)
            factor = features[lanes, :]
            dist = jnp.dot(factor, dist_own[:, cut], preferred_element_type=F32)
            both = jnp.dot(factor, both_own[:, cut], preferred_element_type=F32)
            inverse = lax.rsqrt(jnp.maximum(dist, softening * DIST_SCALE))
            inverse_sq = inverse * inverse
            weight = inverse * inverse_sq
            radial = (weight * inverse_sq) * both
            w_high, w_low = split2(weight, FINE8)
            u_high, u_low = split2(radial, WIDE8)
            dot = functools.partial(jnp.dot, preferred_element_type=F32)
            left, left8 = weights[:, lanes], weights8[:, lanes]
            new = dot(left, w_high), dot(left, u_high), dot(left8, w_low), dot(left8, u_low)
            return tuple(a + b for a, b in zip(total, new))

        found = lax.fori_loop(0, 2, sums, tuple(jnp.where(fresh, 0.0, held[...]) for held in totals))
        for n in range(4):
            totals[n][...] = found[n]

        @pl.when((t & 1) == 1)
        def _():
            def whole(high, low, back):
                high = high[0:8] + high[8:16]
                low = low[0:8] + low[8:16] + low[16:24] + low[24:32]
                return (high + low / N_STARS) * back

            w_all = whole(found[0], found[2], WEIGHT_BACK)
            u_all = whole(found[1], found[3], 1.0)
            mine = own[:, cut]
            x, v = mine[0:3], mine[3:6]
            acc = w_all[0:3] - x * w_all[6:7]
            jerk = w_all[3:6] - v * w_all[6:7] - 3.0 * (u_all[0:3] - x * u_all[6:7])
            part[pl.ds(h, 1)] = jnp.concatenate([acc, jerk, jnp.zeros((2, HALF), F32)], axis=0)[None]

        for number, action in after.items():
            pl.when(t == number)(action)
        return 0

    lax.fori_loop(0, 4, quarter, 0)


def sum_of(landing):
    total = landing[0]
    for c in range(1, COLS):
        total = total + landing[c]
    return total


def packed(x, v, a, j):
    rest = jnp.concatenate([a[2:3], j], axis=0)
    right = jnp.concatenate([rest[:, 0:128], rest[:, 128:256]], axis=0)
    return jnp.concatenate([jnp.concatenate([x, v, a[0:2]], axis=0), right], axis=1)


def take_moved(high, low, sub, rows_at):
    def look(r, found):
        for k in range(4):
            here = high == r * 4 + k
            found = tuple(
                jnp.where(here, lane_pick(two_rows(sub, *pair), low), was)
                for pair, was in zip(rows_at(r, k), found)
            )
        return found

    return lax.fori_loop(0, ROWS, look, tuple(jnp.zeros((8, 128), F32) for _ in range(3)))


def steps_kernel(
    index_ref, count_ref, phase_far, derivs_far, time_far, mass_far,
    all0_ref, all1_ref, near_ref, base_ref, order_ref,
    phase_ref, derivs_ref, time_ref, mass_ref, lists_own, lists_ref, places,
    pred, lead0, land_lead, picks0, picks1, land0, land1, part0, part1, landf0, landf1, lead, lead_all, mine0, mine1,
    old, fix, own, accel, weights, weights8, features, dist_own, both_own, w_high, u_high, w_low, u_low,
    s_in, s_list, r_list, s_lead0, r_lead0, s_pick0, r_pick0, s_pick1, r_pick1, s_for, r_for, s_lead, r_lead, s_all, r_all,
):
    row, col = lax.axis_index("row"), lax.axis_index("col")
    barrier = pltpu.get_barrier_semaphore()
    everyone = partners_of("row", ROWS, row) + partners_of("col", COLS, col)
    for _, partner in everyone:
        pl.semaphore_signal(barrier, inc=1, device_id=partner, device_id_type=MESH)
    inputs = [
        pltpu.make_async_copy(far, near, s_in.at[n])
        for n, (far, near) in enumerate(
            [(phase_far, phase_ref), (derivs_far, derivs_ref), (time_far, time_ref), (mass_far, mass_ref)]
        )
    ]
    for copy in inputs:
        copy.start()
    offset = col * LOCAL
    chunk = 2048
    sub = lax.broadcasted_iota(I32, (8, 128), 0)
    for step in range(2):
        for k in range(8):
            lists_own[8 * step + k : 8 * step + k + 1, :] = index_ref[step, 0:1, k * 128 : k * 128 + 128]
        lists_own[16 + step : 17 + step, :] = jnp.broadcast_to(count_ref[0:1, step : step + 1], (1, 128))
    lists_own[18:24, :] = jnp.zeros((6, 128), I32)
    pl.semaphore_wait(barrier, len(everyone))
    lists = ("row", ROWS, row, lists_own, lists_ref, s_list, r_list)
    exchange(*lists)
    for copy in inputs:
        copy.wait()

    def first_stars(n):
        lanes = pl.ds(pl.multiple_of(n * chunk, chunk), chunk)
        x, v = predict(phase_ref[:, lanes], derivs_ref[:, lanes], time_ref[:, lanes], block_times[0])
        pred[:, lanes] = jnp.concatenate([x, v], axis=0)
        return x, v, mass_ref[:, lanes]

    prepare(0, chunk, LOCAL // chunk, first_stars, weights, weights8, features)
    arrived(*lists)

    def block(b):
        return pl.ds(pl.multiple_of(b * 128, 128), 128)

    def row_pairs(ref):
        return [
            lambda b, c=c: two_rows(sub, ref[c : c + 1, block(b)], ref[c + 1 : c + 2, block(b)])
            for c in (0, 2, 4)
        ]

    rest_pairs = row_pairs(derivs_ref) + [lambda b: two_rows(sub, time_ref[:, block(b)], mass_ref[:, block(b)])]
    local = own_stars(lists_ref, row) - offset
    for p, value in enumerate(fetch(both_halves(local, 0), row_pairs(pred))):
        lead0[p] = value
    lead_picks = ("col", COLS, col, lead0, land_lead, s_lead0, r_lead0)
    exchange(*lead_picks)
    for p, value in enumerate(fetch(both_halves(local, 0), rest_pairs)):
        picks0[p] = value
    first_picks = ("col", COLS, col, picks0, land0, s_pick0, r_pick0)
    exchange(*first_picks)

    found = place_map(lists_ref, 0, offset)
    places[0, 0], places[0, 1] = found[:, 0:128], found[:, 128:256]

    arrived(*lead_picks)
    total = sum_of(land_lead)
    unpack([total[p] for p in range(3)], fix)
    def force_copies(step, half):
        part, landing = (part0, landf0) if step == 0 else (part1, landf1)
        n = 2 * step + half
        return ("col", COLS, col, part.at[half], landing.at[half], s_for.at[n], r_for.at[n])

    def lead_copies(half):
        return ("row", ROWS, row, lead.at[half], lead_all.at[half], s_lead.at[half], r_lead.at[half])

    def row_copies(step, half):
        mine, landing = (mine0, all0_ref) if step == 0 else (mine1, all1_ref)
        n = 2 * step + half
        return ("row", ROWS, row, mine.at[half], landing.at[half], s_all.at[n], r_all.at[n])

    def set_own(x, v):
        own[...] = jnp.concatenate([x, v, jnp.zeros((2, PART), F32)], axis=0)
        dist_own[...], both_own[...] = active_features(x, v)

    sums = (weights, weights8, features, dist_own, both_own, (w_high, u_high, w_low, u_low), own)
    set_own(fix[0:3], fix[3:6])

    def first_old():
        exchange(*force_copies(0, 0))
        arrived(*first_picks)
        total = sum_of(land0)
        unpack([total[p] for p in range(4)], accel)

    def first_corrected(half):
        arrived(*force_copies(0, half))
        cut = slice(half * HALF, half * HALF + HALF)
        x, v, a, j = correct(
            own[0:3, cut], own[3:6, cut], accel[0:3, cut], accel[3:6, cut],
            block_times[0] - accel[6:7, cut], sum_of(landf0.at[half]),
        )
        x_next, v_next = predict(
            jnp.concatenate([x, v], axis=0), jnp.concatenate([a, j], axis=0), block_times[0], block_times[1]
        )
        lead[half] = jnp.concatenate([x_next, v_next, accel[7:8, cut], jnp.zeros((1, HALF), F32)], axis=0)
        exchange(*lead_copies(half))
        mine0[half] = packed(x, v, a, j)
        exchange(*row_copies(0, half))

    force_sums(
        4096, *sums, part0,
        {1: first_old, 2: lambda: first_corrected(0)},
    )
    exchange(*force_copies(0, 1))
    pairs = row_pairs(phase_ref) + rest_pairs
    pairs.append(lambda b: two_rows(sub, places[0, 0, pl.ds(b, 1), :], places[0, 1, pl.ds(b, 1), :]))
    for p, value in enumerate(fetch(both_halves(local, 1), pairs)):
        picks1[p] = value
    second_picks = ("col", COLS, col, picks1, land1, s_pick1, r_pick1)
    exchange(*second_picks)
    first_corrected(1)

    def second_stars(n):
        lanes = pl.ds(pl.multiple_of(n * chunk, chunk), chunk)
        x, v = predict(phase_ref[:, lanes], derivs_ref[:, lanes], time_ref[:, lanes], block_times[1])
        moved = jnp.concatenate([places[0, 0, pl.ds(n * 16 + k, 1), :] for k in range(16)], axis=1)
        return x, v, jnp.where(moved > 0.0, 0.0, mass_ref[:, lanes])

    prepare(0, chunk, LOCAL // chunk, second_stars, weights, weights8, features)
    rank_map(places[0], near_ref, base_ref, order_ref, 0)
    arrived(*second_picks)
    total = sum_of(land1)
    unpack([total[p] for p in range(8)], old)
    high = both_halves(total[7], 0).astype(I32) - 1
    low = both_halves(total[7], 1).astype(I32)
    for half in range(2):
        arrived(*lead_copies(half))

    def moved_stars(n):
        state = lead_all[pl.ds(n & 1, 1), pl.ds(2 * col + (n >> 1), 1)][0, 0]
        return state[0:3], state[3:6], state[6:7]

    prepare(LOCAL, HALF, 4, moved_stars, weights, weights8, features)

    def lead_rows(r, k):
        cut = slice((k % 2) * 128, (k % 2) * 128 + 128)
        return [(lead_all[k // 2, r, c : c + 1, cut], lead_all[k // 2, r, c + 1 : c + 2, cut]) for c in (0, 2, 4)]

    unpack(take_moved(high, low, sub, lead_rows), fix)
    moved = old[14:15] > 0.0
    x_own, v_own = predict(old[0:6], old[6:12], old[12:13], block_times[1])
    set_own(jnp.where(moved, fix[0:3], x_own), jnp.where(moved, fix[3:6], v_own))

    def rest_rows(r, k):
        half, at = k // 2, 4 * (k % 2)
        cut = slice((k % 2) * 128, (k % 2) * 128 + 128)
        return [
            (all0_ref[half, r, 6:7, cut], all0_ref[half, r, 7:8, cut]),
            (all0_ref[half, r, at : at + 1, 256:384], all0_ref[half, r, at + 1 : at + 2, 256:384]),
            (all0_ref[half, r, at + 2 : at + 3, 256:384], all0_ref[half, r, at + 3 : at + 4, 256:384]),
        ]

    def second_old():
        exchange(*force_copies(1, 0))
        for half in range(2):
            arrived(*row_copies(0, half))
        unpack(take_moved(high, low, sub, rest_rows), fix)
        moved = old[14:15] > 0.0
        h = block_times[1] - jnp.where(moved, block_times[0], old[12:13])
        accel[...] = jnp.concatenate(
            [jnp.where(moved, fix[0:3], old[6:9]), jnp.where(moved, fix[3:6], old[9:12]), h, h], axis=0
        )

    def second_corrected(half):
        arrived(*force_copies(1, half))
        cut = slice(half * HALF, half * HALF + HALF)
        mine1[half] = packed(
            *correct(
                own[0:3, cut], own[3:6, cut], accel[0:3, cut], accel[3:6, cut], accel[6:7, cut],
                sum_of(landf1.at[half]),
            )
        )
        exchange(*row_copies(1, half))

    force_sums(
        (LOCAL + 2 * PART) // 4, *sums, part1, {1: second_old, 2: lambda: second_corrected(0)}
    )
    exchange(*force_copies(1, 1))
    found = place_map(lists_ref, 1, offset)
    places[1, 0], places[1, 1] = found[:, 0:128], found[:, 128:256]
    second_corrected(1)
    rank_map(places[1], near_ref, base_ref, order_ref, 1)
    for half in range(2):
        arrived(*row_copies(1, half))
    for copies in [lists, lead_picks, first_picks, second_picks]:
        sent(*copies)
    for half in range(2):
        sent(*lead_copies(half))
        for step in range(2):
            sent(*force_copies(step, half))
            sent(*row_copies(step, half))


def both_steps(index, count, phase, derivs, time, masses):
    stars = LOCAL + 2 * PART
    vmem = [
        ((6, LOCAL), F32),
        ((6, LOCAL), F32),
        ((1, LOCAL), F32),
        ((1, LOCAL), F32),
        ((24, 128), I32),
        ((ROWS, 24, 128), I32),
        ((2, 2, 128, 128), F32),
        ((6, LOCAL), F32),
        ((3, 8, 128), F32),
        ((COLS, 3, 8, 128), F32),
        ((4, 8, 128), F32),
        ((8, 8, 128), F32),
        ((COLS, 4, 8, 128), F32),
        ((COLS, 8, 8, 128), F32),
        ((2, 8, HALF), F32),
        ((2, 8, HALF), F32),
        ((2, COLS, 8, HALF), F32),
        ((2, COLS, 8, HALF), F32),
        ((2, 8, HALF), F32),
        ((2, ROWS, 8, HALF), F32),
        ((2, 8, 384), F32),
        ((2, 8, 384), F32),
        ((16, PART), F32),
        ((8, PART), F32),
        ((8, PART), F32),
        ((8, PART), F32),
        ((16, stars), BF16),
        ((32, stars), FINE8),
        ((stars, 64), BF16),
        ((64, PART), BF16),
        ((64, PART), BF16),
        ((16, HALF), F32),
        ((16, HALF), F32),
        ((32, HALF), F32),
        ((32, HALF), F32),
    ]
    sems = [(4,)] + [(ROWS,)] * 2 + [(COLS,)] * 6 + [(4, COLS)] * 2 + [(2, ROWS)] * 2 + [(4, ROWS)] * 2
    return pl.pallas_call(
        steps_kernel,
        out_shape=[
            jax.ShapeDtypeStruct((2, ROWS, 8, 384), F32),
            jax.ShapeDtypeStruct((2, ROWS, 8, 384), F32),
            jax.ShapeDtypeStruct((2, 128, 128), I32),
            jax.ShapeDtypeStruct((2, 2, 8, 128), I32),
            jax.ShapeDtypeStruct((2, 64, 256), F32),
        ],
        in_specs=in_vmem(2) + [pl.BlockSpec(memory_space=pl.ANY)] * 4,
        out_specs=in_vmem(5),
        scratch_shapes=[pltpu.VMEM(shape, kind) for shape, kind in vmem]
        + [pltpu.SemaphoreType.DMA(shape) for shape in sems],
        compiler_params=params(collective_id=0, has_side_effects=True),
        name="both_steps",
    )(index, count, phase, derivs, time, masses)


def collect(step, count, order_ref, all_ref, sorted_ref):
    def one_block(n, _):
        group = order_ref[step, pl.ds(pl.multiple_of((n >> 3) * 8, 8), 8), :]
        mask = lax.broadcasted_iota(I32, (8, 256), 0) == (n & 7)
        digits = jnp.sum(jnp.where(mask, group, 0.0), axis=0, keepdims=True)
        high = spread(digits[:, 0:128]).astype(I32) - 1
        low = spread(digits[:, 128:256]).astype(I32)
        upper = jnp.zeros((8, 128), F32)
        lower = jnp.zeros((8, 128), F32)
        shifted = high - (lax.broadcasted_iota(I32, (8, 128), 0) >> 2)
        for b in range(64):
            r, half, k = b // 4, (b % 4) // 2, b % 2
            upper = jnp.where(high == b, lane_pick(all_ref[half, r, :, k * 128 : k * 128 + 128], low), upper)
            if k == 0:
                lower = jnp.where(shifted == b, lane_pick(all_ref[half, r, :, 256:384], low), lower)
        blank = jnp.zeros((2, 128), F32)
        rest = lower[0:4] + lower[4:8]
        sorted_ref[step, n, 0:8, :] = upper
        sorted_ref[step, n, 8:16, :] = jnp.concatenate([upper[6:8], rest, blank], axis=0)
        return 0

    lax.fori_loop(0, (count + 127) // 128, one_block, 0)


def last_kernel(
    base_ref, near_ref, order_ref, all0_ref, all1_ref, phase_ref, derivs_ref, time_ref,
    phase_out, derivs_out, time_out, sorted_ref,
):
    collect(0, base_ref[0, 1, 0, 127], order_ref, all0_ref, sorted_ref)
    collect(1, base_ref[1, 1, 0, 127], order_ref, all1_ref, sorted_ref)

    lane = lax.broadcasted_iota(I32, (8, 128), 1)
    run = 16

    def put(g, _, wide):
        for u in range(run):
            b = g * run + u
            lanes = pl.ds(pl.multiple_of(b * 128, 128), 128)
            blank = jnp.zeros((2, 128), F32)
            phase = jnp.concatenate([phase_ref[:, lanes], blank], axis=0)
            derivs = jnp.concatenate([derivs_ref[:, lanes], blank], axis=0)
            time = time_ref[:, lanes]
            for step in range(2):
                base = base_ref[step, 0, 0, b]
                n, shift = base >> 1, (base & 1) * 64
                at = spread(near_ref[step, pl.ds(b, 1), :]) - 1
                low = (at + shift) & 127
                behind = lane >= shift

                def chosen(rows, was):
                    here, then = sorted_ref[step, n, rows, :], sorted_ref[step, n + 1, rows, :]
                    new = jnp.where(at >= 0, lane_pick(jnp.where(behind, here, then), low), was)
                    if wide:
                        last = sorted_ref[step, n + 2, rows, :]
                        new = jnp.where(at >= 128, lane_pick(jnp.where(behind, then, last), low), new)
                    return new

                phase = chosen(slice(0, 8), phase)
                derivs = chosen(slice(8, 16), derivs)
                time = jnp.where(at[0:1] >= 0, block_times[step], time)
            phase_out[:, lanes] = phase[0:6]
            derivs_out[:, lanes] = derivs[0:6]
            time_out[:, lanes] = time
        return 0

    wide = (base_ref[0, 1, 1, 0] > 128) | (base_ref[1, 1, 1, 0] > 128)

    @pl.when(wide)
    def _():
        lax.fori_loop(0, BLOCKS // run, functools.partial(put, wide=True), 0)

    @pl.when(jnp.logical_not(wide))
    def _():
        lax.fori_loop(0, BLOCKS // run, functools.partial(put, wide=False), 0)


def last_update(base, near, order, all0, all1, phase, derivs, time):
    return pl.pallas_call(
        last_kernel,
        out_shape=[
            jax.ShapeDtypeStruct((6, LOCAL), F32),
            jax.ShapeDtypeStruct((6, LOCAL), F32),
            jax.ShapeDtypeStruct((1, LOCAL), F32),
        ],
        in_specs=[pl.BlockSpec(memory_space=pltpu.SMEM)] + in_vmem(7),
        out_specs=in_vmem(3),
        scratch_shapes=[pltpu.VMEM((2, 68, 16, 128), F32)],
        compiler_params=params(),
        name="last_update",
    )(base, near, order, all0, all1, phase, derivs, time)


def body(phase_space, derivs, star_time, masses, active_index, active_count):
    time = star_time.reshape(1, LOCAL)
    masses = masses.reshape(1, LOCAL)
    all0, all1, near, base, order = both_steps(
        active_index, active_count.reshape(1, 2), phase_space, derivs, time, masses
    )
    phase_space, derivs, time = last_update(base, near, order, all0, all1, phase_space, derivs, time)
    return phase_space, derivs, time.reshape(LOCAL)


def solution(mesh):
    return jax.shard_map(
        body,
        mesh=mesh,
        in_specs=(
            P(None, "col"),
            P(None, "col"),
            P("col"),
            P("col"),
            P(None, "row", None),
            P(None, "row"),
        ),
        out_specs=(P(None, "col"), P(None, "col"), P("col")),
        check_vma=False,
    )
```

```python
import functools

import jax
import jax.numpy as jnp
from jax import lax
from jax.experimental import pallas as pl
from jax.experimental.pallas import tpu as pltpu
from jax.sharding import PartitionSpec as P

F32 = jnp.float32
BF16 = jnp.bfloat16
I32 = jnp.int32
FINE8 = jnp.float8_e4m3fn
WIDE8 = jnp.float8_e5m2
DIST_SCALE = 2.0**-4
BOTH_SCALE = 2.0**-10
WEIGHT_BACK = 2.0**-6
softening = 0.01
block_times = (0.125, 0.25)
ROWS = 16
COLS = 8
CAP = 1024
PART = 512
HALF = 256
LOCAL = 16384
BLOCKS = LOCAL // 128
N_STARS = ROWS * PART * 16
MESH = pl.DeviceIdType.MESH
ADDED = (((1,), (1,)), ((), ()))


def rows_of(first, last, width):
    return jnp.zeros((last - first, width), F32)


def in_vmem(n):
    return [pl.BlockSpec(memory_space=pltpu.VMEM)] * n


def params(**more):
    return pltpu.CompilerParams(vmem_limit_bytes=56 * 2**20, **more)


def partners_of(axis, size, place):
    return [(k, {axis: lax.rem(place + k, size)}) for k in range(1, size)]


def exchange(axis, size, place, source, landing, send_sem, recv_sem):
    for k, partner in partners_of(axis, size, place):
        pltpu.make_async_remote_copy(
            src_ref=source,
            dst_ref=landing.at[place],
            send_sem=send_sem.at[k],
            recv_sem=recv_sem.at[place],
            device_id=partner,
            device_id_type=MESH,
        ).start()
    landing[pl.ds(place, 1)] = source[...][None]


def sent(axis, size, place, source, landing, send_sem, recv_sem):
    for k, partner in partners_of(axis, size, place):
        pltpu.make_async_remote_copy(
            src_ref=source,
            dst_ref=landing.at[place],
            send_sem=send_sem.at[k],
            recv_sem=recv_sem.at[place],
            device_id=partner,
            device_id_type=MESH,
        ).wait_send()


def arrived(axis, size, place, source, landing, send_sem, recv_sem):
    for k, partner in partners_of(axis, size, place):
        slot = lax.rem(place + k, size)
        pltpu.make_async_remote_copy(
            src_ref=source,
            dst_ref=landing.at[slot],
            send_sem=send_sem.at[k],
            recv_sem=recv_sem.at[slot],
            device_id=partner,
            device_id_type=MESH,
        ).wait_recv()


def lane_pick(table, lanes):
    return jnp.take_along_axis(table, lanes, axis=1, mode="promise_in_bounds")


def spread(row):
    return jnp.broadcast_to(row, (8, 128))


def hot(index_row, count):
    kinds = lax.broadcasted_iota(I32, (count, 128), 0).astype(F32).astype(BF16)
    return jnp.broadcast_to(index_row, (count, 128)).astype(BF16) == kinds


def scattered(entries, high_count):
    one, zero = jnp.ones((), BF16), jnp.zeros((), BF16)
    left, right = [], []
    for high, low, first, second in entries:
        left.append(jnp.where(hot(high, high_count), one, zero))
        at_low = hot(low, 128)
        a = jnp.broadcast_to(first, (128, 128)).astype(BF16)
        b = jnp.broadcast_to(second, (128, 128)).astype(BF16)
        right.append(jnp.concatenate([jnp.where(at_low, a, zero), jnp.where(at_low, b, zero)], axis=0))
    return lax.dot_general(
        jnp.concatenate(left, axis=1), jnp.concatenate(right, axis=1), ADDED, preferred_element_type=F32
    )


def place_map(lists_ref, step, offset):
    slot = lax.broadcasted_iota(I32, (8, 128), 0) * 128 + lax.broadcasted_iota(I32, (8, 128), 1)
    begin = jnp.zeros((8, 128), I32)
    entries = []
    for r in range(ROWS):
        count = spread(lists_ref[r, 16 + step : 17 + step, :])
        star = lists_ref[r, 8 * step : 8 * step + 8, :] - offset
        live = (slot < count) & (star >= 0) & (star < LOCAL)
        at = begin + slot
        high = jnp.where(live, star >> 7, 255).astype(F32)
        low = (star & 127).astype(F32)
        first, second = ((at >> 7) + 1).astype(F32), (at & 127).astype(F32)
        for k in range(8):
            cut = slice(k, k + 1)
            entries.append((high[cut], low[cut], first[cut], second[cut]))
        begin = begin + count
    return scattered(entries, 128)


def rank_map(places, near_ref, base_ref, order_ref, step):
    at_high, at_low = places[0], places[1]
    row = lax.broadcasted_iota(I32, (128, 128), 0)
    lane = lax.broadcasted_iota(I32, (128, 128), 1)
    up_to = (row <= lane).astype(F32).astype(BF16)
    before = (row < lane).astype(F32).astype(BF16)
    below = (lane < row).astype(F32).astype(BF16)
    active = (at_high > 0.0).astype(F32)
    active16 = active.astype(BF16)
    so_far = jnp.dot(active16, up_to, preferred_element_type=F32)
    total = jnp.broadcast_to(so_far[:, 127:128], (128, 128))
    first = jnp.dot(below, total.astype(BF16), preferred_element_type=F32)
    rank = (first + so_far - active).astype(I32)
    near = jnp.where(active > 0.0, rank - (first.astype(I32) >> 6) * 64 + 1, 0)
    near_ref[step] = near
    widest = jnp.max(jnp.max(near.astype(F32), axis=0, keepdims=True), axis=1, keepdims=True)
    ones = jnp.ones((8, 128), F32).astype(BF16)
    totals = lax.dot_general(ones, active16, ADDED, preferred_element_type=F32)
    firsts = jnp.dot(totals.astype(BF16), before, preferred_element_type=F32).astype(I32)
    base_ref[step, 0] = firsts >> 6
    ends = firsts + totals.astype(I32)
    sub = lax.broadcasted_iota(I32, (8, 128), 0)
    base_ref[step, 1] = jnp.where(sub == 0, ends, jnp.broadcast_to(widest, (8, 128)).astype(I32))
    rank_high = jnp.where(active > 0.0, rank >> 7, 255).astype(F32)
    rank_low = (rank & 127).astype(F32)
    entries = []
    for b in range(BLOCKS):
        cut = slice(b, b + 1)
        entries.append((rank_high[cut], rank_low[cut], at_high[cut], at_low[cut]))
    order_ref[step] = scattered(entries, 64)


def own_stars(lists_ref, place):
    lane = lax.broadcasted_iota(I32, (8, 128), 1)
    sub = lax.broadcasted_iota(I32, (8, 128), 0)
    position = place * PART + (sub & 3) * 128 + lane
    before = jnp.zeros((8, 128), I32)
    which = jnp.zeros((8, 128), I32)
    start = jnp.zeros((8, 128), I32)
    for r in range(ROWS):
        count = jnp.where(sub < 4, spread(lists_ref[r, 16:17, :]), spread(lists_ref[r, 17:18, :]))
        end = before + count
        passed = position >= end
        which = which + passed.astype(I32)
        start = jnp.where(passed, end, start)
        before = end
    flat = which * CAP + position - start
    high, low = flat >> 7, flat & 127
    stars = jnp.zeros((8, 128), I32)
    for r in range(ROWS):
        for k in range(8):
            row = jnp.where(
                sub < 4, spread(lists_ref[r, k : k + 1, :]), spread(lists_ref[r, 8 + k : 9 + k, :])
            )
            stars = jnp.where(high == r * 8 + k, lane_pick(row, low), stars)
    return stars


def both_halves(x, step):
    part = x[4 * step : 4 * step + 4]
    return jnp.concatenate([part, part], axis=0)


def fetch(stars, pairs):
    high, low = stars >> 7, stars & 127

    def look(g, found):
        for u in range(16):
            b = g * 16 + u
            here = high == b
            found = tuple(
                jnp.where(here, lane_pick(pair(b), low), old) for pair, old in zip(pairs, found)
            )
        return found

    return lax.fori_loop(0, BLOCKS // 16, look, tuple(jnp.zeros((8, 128), F32) for _ in pairs))


def two_rows(sub, a, b):
    return jnp.where(sub < 4, spread(a), spread(b))


def unpack(pairs, out_ref):
    for p, pair in enumerate(pairs):
        for half in range(2):
            for s in range(4):
                out_ref[2 * p + half : 2 * p + half + 1, s * 128 : s * 128 + 128] = pair[
                    4 * half + s : 4 * half + s + 1
                ]


def predict(phase, derivs, time, now):
    d = now - time
    x, v, a, j = phase[0:3], phase[3:6], derivs[0:3], derivs[3:6]
    return x + d * (v + d * (a / 2.0 + d * j / 6.0)), v + d * (a + d * j / 2.0)


def correct(x, v, old_acc, old_jerk, h, forces):
    new_acc, new_jerk = forces[0:3], forces[3:6]
    change = old_acc - new_acc
    second = (-6.0 * change - h * (4.0 * old_jerk + 2.0 * new_jerk)) / (h * h)
    third = (12.0 * change + 6.0 * h * (old_jerk + new_jerk)) / (h * h * h)
    h2 = h * h
    h3 = h2 * h
    h4 = h3 * h
    h5 = h4 * h
    x = x + h4 / 24.0 * second + h5 / 120.0 * third
    v = v + h3 / 6.0 * second + h4 / 24.0 * third
    return x, v, new_acc, new_jerk


PAIRS = ((0, 0), (0, 1), (0, 2), (1, 0), (1, 1), (2, 0))


def split3(x):
    high = x.astype(BF16).astype(F32)
    rest = x - high
    middle = rest.astype(BF16).astype(F32)
    return high, middle, rest - middle


def split2(x, low_kind):
    high = x.astype(BF16)
    return high, (x - high.astype(F32)).astype(low_kind)


def split8(x):
    parts = []
    for _ in range(4):
        parts.append(x.astype(FINE8).astype(F32))
        x = x - parts[-1]
    return parts


def squares(x, v):
    xx = x * x
    xv = x * v
    return xx[0:1] + xx[1:2] + xx[2:3], xv[0:1] + xv[1:2] + xv[2:3]


def star_features(x, v):
    width = x.shape[1]
    parts = split3(jnp.concatenate([x, v, jnp.zeros((2, width), F32)], axis=0))
    xx, xv = squares(x, v)
    one = jnp.ones((3, width), F32)
    extra = jnp.concatenate(list(split3(xx)) + list(split3(xv)) + [one, one, rows_of(12, 16, width)], axis=0)
    return jnp.concatenate([parts[a] for a, _ in PAIRS] + [extra], axis=0)


def active_features(x, v):
    width = x.shape[1]
    xp, vp = split3(x), split3(v)
    xx, xv = squares(x, v)
    one, none3, none5 = jnp.ones((3, width), F32), rows_of(0, 3, width), rows_of(0, 5, width)
    dist, both = [], []
    for _, b in PAIRS:
        dist += [-2.0 * xp[b], none5]
        both += [-vp[b], -xp[b], rows_of(0, 2, width)]
    dist += [one, none3] + list(split3(xx + softening)) + [none3, rows_of(12, 16, width)]
    both += [none3, one, none3] + list(split3(xv)) + [rows_of(12, 16, width)]
    dist = jnp.concatenate(dist, axis=0) * DIST_SCALE
    both = jnp.concatenate(both, axis=0) * BOTH_SCALE
    return dist.astype(BF16), both.astype(BF16)


def prepare(first, chunk, count, pred_of, weights, weights8, features):
    def one_chunk(n, _):
        x, v, mass = pred_of(n)
        at = pl.ds(pl.multiple_of(first + n * chunk, chunk), chunk)
        ones, none = jnp.ones((1, chunk), F32), jnp.zeros((1, chunk), F32)
        scaled = jnp.concatenate([x, v, ones, none], axis=0) * mass
        share = scaled / N_STARS
        high = share.astype(BF16).astype(F32)
        weights[:, at] = jnp.concatenate([high, share - high], axis=0).astype(BF16)
        weights8[:, at] = jnp.concatenate(split8(jnp.clip(scaled, -240.0, 240.0)), axis=0).astype(FINE8)
        features[at, :] = star_features(x, v).T.astype(BF16)
        return 0

    lax.fori_loop(0, count, one_chunk, 0)


def force_sums(deep, weights, weights8, features, dist_own, both_own, totals, own, part, after):
    def quarter(t, _):
        h = t >> 1
        cut = pl.ds(pl.multiple_of(h * HALF, HALF), HALF)
        fresh = (t & 1) == 0

        def sums(n, total):
            lanes = pl.ds(pl.multiple_of(((t & 1) * 2 + n) * deep, deep), deep)
            factor = features[lanes, :]
            dist = jnp.dot(factor, dist_own[:, cut], preferred_element_type=F32)
            both = jnp.dot(factor, both_own[:, cut], preferred_element_type=F32)
            inverse = lax.rsqrt(jnp.maximum(dist, softening * DIST_SCALE))
            inverse_sq = inverse * inverse
            weight = inverse * inverse_sq
            radial = (weight * inverse_sq) * both
            w_high, w_low = split2(weight, FINE8)
            u_high, u_low = split2(radial, WIDE8)
            dot = functools.partial(jnp.dot, preferred_element_type=F32)
            left, left8 = weights[:, lanes], weights8[:, lanes]
            new = dot(left, w_high), dot(left, u_high), dot(left8, w_low), dot(left8, u_low)
            return tuple(a + b for a, b in zip(total, new))

        found = lax.fori_loop(0, 2, sums, tuple(jnp.where(fresh, 0.0, held[...]) for held in totals))
        for n in range(4):
            totals[n][...] = found[n]

        @pl.when((t & 1) == 1)
        def _():
            def whole(high, low, back):
                high = high[0:8] + high[8:16]
                low = low[0:8] + low[8:16] + low[16:24] + low[24:32]
                return (high + low / N_STARS) * back

            w_all = whole(found[0], found[2], WEIGHT_BACK)
            u_all = whole(found[1], found[3], 1.0)
            mine = own[:, cut]
            x, v = mine[0:3], mine[3:6]
            acc = w_all[0:3] - x * w_all[6:7]
            jerk = w_all[3:6] - v * w_all[6:7] - 3.0 * (u_all[0:3] - x * u_all[6:7])
            part[pl.ds(h, 1)] = jnp.concatenate([acc, jerk, jnp.zeros((2, HALF), F32)], axis=0)[None]

        for number, action in after.items():
            pl.when(t == number)(action)
        return 0

    lax.fori_loop(0, 4, quarter, 0)


def sum_of(landing):
    total = landing[0]
    for c in range(1, COLS):
        total = total + landing[c]
    return total


def packed(x, v, a, j):
    rest = jnp.concatenate([a[2:3], j], axis=0)
    right = jnp.concatenate([rest[:, 0:128], rest[:, 128:256]], axis=0)
    return jnp.concatenate([jnp.concatenate([x, v, a[0:2]], axis=0), right], axis=1)


def take_moved(high, low, sub, rows_at):
    def look(g, found):
        for u in range(16):
            r, k = g * 4 + u // 4, u % 4
            here = high == r * 4 + k
            found = tuple(
                jnp.where(here, lane_pick(two_rows(sub, *pair), low), was)
                for pair, was in zip(rows_at(r, k), found)
            )
        return found

    return lax.fori_loop(0, ROWS // 4, look, tuple(jnp.zeros((8, 128), F32) for _ in range(3)))


def steps_kernel(
    index_ref, count_ref, phase_far, derivs_far, time_far, mass_far,
    all0_ref, all1_ref, near_ref, base_ref, order_ref,
    phase_ref, derivs_ref, time_ref, mass_ref, lists_own, lists_ref, places,
    pred, lead0, land_lead, picks0, picks1, land0, land1, part0, part1, landf0, landf1, lead, lead_all, mine0, mine1,
    old, fix, own, accel, weights, weights8, features, dist_own, both_own, w_high, u_high, w_low, u_low,
    s_in, s_list, r_list, s_lead0, r_lead0, s_pick0, r_pick0, s_pick1, r_pick1, s_for, r_for, s_lead, r_lead, s_all, r_all,
):
    row, col = lax.axis_index("row"), lax.axis_index("col")
    barrier = pltpu.get_barrier_semaphore()
    everyone = partners_of("row", ROWS, row) + partners_of("col", COLS, col)
    for _, partner in everyone:
        pl.semaphore_signal(barrier, inc=1, device_id=partner, device_id_type=MESH)
    inputs = [
        pltpu.make_async_copy(far, near, s_in.at[n])
        for n, (far, near) in enumerate(
            [(phase_far, phase_ref), (derivs_far, derivs_ref), (time_far, time_ref), (mass_far, mass_ref)]
        )
    ]
    for copy in inputs:
        copy.start()
    offset = col * LOCAL
    chunk = 2048
    sub = lax.broadcasted_iota(I32, (8, 128), 0)
    for step in range(2):
        for k in range(8):
            lists_own[8 * step + k : 8 * step + k + 1, :] = index_ref[step, 0:1, k * 128 : k * 128 + 128]
        lists_own[16 + step : 17 + step, :] = jnp.broadcast_to(count_ref[0:1, step : step + 1], (1, 128))
    lists_own[18:24, :] = jnp.zeros((6, 128), I32)
    pl.semaphore_wait(barrier, len(everyone))
    lists = ("row", ROWS, row, lists_own, lists_ref, s_list, r_list)
    exchange(*lists)
    for copy in inputs:
        copy.wait()

    def first_stars(n):
        lanes = pl.ds(pl.multiple_of(n * chunk, chunk), chunk)
        x, v = predict(phase_ref[:, lanes], derivs_ref[:, lanes], time_ref[:, lanes], block_times[0])
        pred[:, lanes] = jnp.concatenate([x, v], axis=0)
        return x, v, mass_ref[:, lanes]

    prepare(0, chunk, LOCAL // chunk, first_stars, weights, weights8, features)
    arrived(*lists)

    def block(b):
        return pl.ds(pl.multiple_of(b * 128, 128), 128)

    def row_pairs(ref):
        return [
            lambda b, c=c: two_rows(sub, ref[c : c + 1, block(b)], ref[c + 1 : c + 2, block(b)])
            for c in (0, 2, 4)
        ]

    rest_pairs = row_pairs(derivs_ref) + [lambda b: two_rows(sub, time_ref[:, block(b)], mass_ref[:, block(b)])]
    local = own_stars(lists_ref, row) - offset
    for p, value in enumerate(fetch(both_halves(local, 0), row_pairs(pred))):
        lead0[p] = value
    lead_picks = ("col", COLS, col, lead0, land_lead, s_lead0, r_lead0)
    exchange(*lead_picks)
    for p, value in enumerate(fetch(both_halves(local, 0), rest_pairs)):
        picks0[p] = value
    first_picks = ("col", COLS, col, picks0, land0, s_pick0, r_pick0)
    exchange(*first_picks)

    found = place_map(lists_ref, 0, offset)
    places[0, 0], places[0, 1] = found[:, 0:128], found[:, 128:256]

    arrived(*lead_picks)
    total = sum_of(land_lead)
    unpack([total[p] for p in range(3)], fix)
    def force_copies(step, half):
        part, landing = (part0, landf0) if step == 0 else (part1, landf1)
        n = 2 * step + half
        return ("col", COLS, col, part.at[half], landing.at[half], s_for.at[n], r_for.at[n])

    def lead_copies(half):
        return ("row", ROWS, row, lead.at[half], lead_all.at[half], s_lead.at[half], r_lead.at[half])

    def row_copies(step, half):
        mine, landing = (mine0, all0_ref) if step == 0 else (mine1, all1_ref)
        n = 2 * step + half
        return ("row", ROWS, row, mine.at[half], landing.at[half], s_all.at[n], r_all.at[n])

    def set_own(x, v):
        own[...] = jnp.concatenate([x, v, jnp.zeros((2, PART), F32)], axis=0)
        dist_own[...], both_own[...] = active_features(x, v)

    sums = (weights, weights8, features, dist_own, both_own, (w_high, u_high, w_low, u_low), own)
    set_own(fix[0:3], fix[3:6])

    def first_old():
        exchange(*force_copies(0, 0))
        arrived(*first_picks)
        total = sum_of(land0)
        unpack([total[p] for p in range(4)], accel)

    def first_corrected(half):
        arrived(*force_copies(0, half))
        cut = slice(half * HALF, half * HALF + HALF)
        x, v, a, j = correct(
            own[0:3, cut], own[3:6, cut], accel[0:3, cut], accel[3:6, cut],
            block_times[0] - accel[6:7, cut], sum_of(landf0.at[half]),
        )
        x_next, v_next = predict(
            jnp.concatenate([x, v], axis=0), jnp.concatenate([a, j], axis=0), block_times[0], block_times[1]
        )
        lead[half] = jnp.concatenate([x_next, v_next, accel[7:8, cut], jnp.zeros((1, HALF), F32)], axis=0)
        exchange(*lead_copies(half))
        mine0[half] = packed(x, v, a, j)
        exchange(*row_copies(0, half))

    force_sums(
        4096, *sums, part0,
        {1: first_old, 2: lambda: first_corrected(0)},
    )
    exchange(*force_copies(0, 1))
    pairs = row_pairs(phase_ref) + rest_pairs
    pairs.append(lambda b: two_rows(sub, places[0, 0, pl.ds(b, 1), :], places[0, 1, pl.ds(b, 1), :]))
    for p, value in enumerate(fetch(both_halves(local, 1), pairs)):
        picks1[p] = value
    second_picks = ("col", COLS, col, picks1, land1, s_pick1, r_pick1)
    exchange(*second_picks)
    first_corrected(1)

    def second_stars(n):
        lanes = pl.ds(pl.multiple_of(n * chunk, chunk), chunk)
        x, v = predict(phase_ref[:, lanes], derivs_ref[:, lanes], time_ref[:, lanes], block_times[1])
        moved = jnp.concatenate([places[0, 0, pl.ds(n * 16 + k, 1), :] for k in range(16)], axis=1)
        return x, v, jnp.where(moved > 0.0, 0.0, mass_ref[:, lanes])

    prepare(0, chunk, LOCAL // chunk, second_stars, weights, weights8, features)
    rank_map(places[0], near_ref, base_ref, order_ref, 0)
    arrived(*second_picks)
    total = sum_of(land1)
    unpack([total[p] for p in range(8)], old)
    high = both_halves(total[7], 0).astype(I32) - 1
    low = both_halves(total[7], 1).astype(I32)
    for half in range(2):
        arrived(*lead_copies(half))

    def moved_stars(n):
        state = lead_all[pl.ds(n & 1, 1), pl.ds(2 * col + (n >> 1), 1)][0, 0]
        return state[0:3], state[3:6], state[6:7]

    prepare(LOCAL, HALF, 4, moved_stars, weights, weights8, features)

    def lead_rows(r, k):
        cut = slice((k % 2) * 128, (k % 2) * 128 + 128)
        return [(lead_all[k // 2, r, c : c + 1, cut], lead_all[k // 2, r, c + 1 : c + 2, cut]) for c in (0, 2, 4)]

    unpack(take_moved(high, low, sub, lead_rows), fix)
    moved = old[14:15] > 0.0
    x_own, v_own = predict(old[0:6], old[6:12], old[12:13], block_times[1])
    set_own(jnp.where(moved, fix[0:3], x_own), jnp.where(moved, fix[3:6], v_own))

    def rest_rows(r, k):
        half, at = k // 2, 4 * (k % 2)
        cut = slice((k % 2) * 128, (k % 2) * 128 + 128)
        return [
            (all0_ref[half, r, 6:7, cut], all0_ref[half, r, 7:8, cut]),
            (all0_ref[half, r, at : at + 1, 256:384], all0_ref[half, r, at + 1 : at + 2, 256:384]),
            (all0_ref[half, r, at + 2 : at + 3, 256:384], all0_ref[half, r, at + 3 : at + 4, 256:384]),
        ]

    def second_old():
        exchange(*force_copies(1, 0))
        for half in range(2):
            arrived(*row_copies(0, half))
        unpack(take_moved(high, low, sub, rest_rows), fix)
        moved = old[14:15] > 0.0
        h = block_times[1] - jnp.where(moved, block_times[0], old[12:13])
        accel[...] = jnp.concatenate(
            [jnp.where(moved, fix[0:3], old[6:9]), jnp.where(moved, fix[3:6], old[9:12]), h, h], axis=0
        )

    def second_corrected(half):
        arrived(*force_copies(1, half))
        cut = slice(half * HALF, half * HALF + HALF)
        mine1[half] = packed(
            *correct(
                own[0:3, cut], own[3:6, cut], accel[0:3, cut], accel[3:6, cut], accel[6:7, cut],
                sum_of(landf1.at[half]),
            )
        )
        exchange(*row_copies(1, half))

    force_sums(
        (LOCAL + 2 * PART) // 4, *sums, part1, {1: second_old, 2: lambda: second_corrected(0)}
    )
    exchange(*force_copies(1, 1))
    found = place_map(lists_ref, 1, offset)
    places[1, 0], places[1, 1] = found[:, 0:128], found[:, 128:256]
    second_corrected(1)
    rank_map(places[1], near_ref, base_ref, order_ref, 1)
    for half in range(2):
        arrived(*row_copies(1, half))
    for copies in [lists, lead_picks, first_picks, second_picks]:
        sent(*copies)
    for half in range(2):
        sent(*lead_copies(half))
        for step in range(2):
            sent(*force_copies(step, half))
            sent(*row_copies(step, half))


def both_steps(index, count, phase, derivs, time, masses):
    stars = LOCAL + 2 * PART
    vmem = [
        ((6, LOCAL), F32),
        ((6, LOCAL), F32),
        ((1, LOCAL), F32),
        ((1, LOCAL), F32),
        ((24, 128), I32),
        ((ROWS, 24, 128), I32),
        ((2, 2, 128, 128), F32),
        ((6, LOCAL), F32),
        ((3, 8, 128), F32),
        ((COLS, 3, 8, 128), F32),
        ((4, 8, 128), F32),
        ((8, 8, 128), F32),
        ((COLS, 4, 8, 128), F32),
        ((COLS, 8, 8, 128), F32),
        ((2, 8, HALF), F32),
        ((2, 8, HALF), F32),
        ((2, COLS, 8, HALF), F32),
        ((2, COLS, 8, HALF), F32),
        ((2, 8, HALF), F32),
        ((2, ROWS, 8, HALF), F32),
        ((2, 8, 384), F32),
        ((2, 8, 384), F32),
        ((16, PART), F32),
        ((8, PART), F32),
        ((8, PART), F32),
        ((8, PART), F32),
        ((16, stars), BF16),
        ((32, stars), FINE8),
        ((stars, 64), BF16),
        ((64, PART), BF16),
        ((64, PART), BF16),
        ((16, HALF), F32),
        ((16, HALF), F32),
        ((32, HALF), F32),
        ((32, HALF), F32),
    ]
    sems = [(4,)] + [(ROWS,)] * 2 + [(COLS,)] * 6 + [(4, COLS)] * 2 + [(2, ROWS)] * 2 + [(4, ROWS)] * 2
    return pl.pallas_call(
        steps_kernel,
        out_shape=[
            jax.ShapeDtypeStruct((2, ROWS, 8, 384), F32),
            jax.ShapeDtypeStruct((2, ROWS, 8, 384), F32),
            jax.ShapeDtypeStruct((2, 128, 128), I32),
            jax.ShapeDtypeStruct((2, 2, 8, 128), I32),
            jax.ShapeDtypeStruct((2, 64, 256), F32),
        ],
        in_specs=in_vmem(2) + [pl.BlockSpec(memory_space=pl.ANY)] * 4,
        out_specs=in_vmem(5),
        scratch_shapes=[pltpu.VMEM(shape, kind) for shape, kind in vmem]
        + [pltpu.SemaphoreType.DMA(shape) for shape in sems],
        compiler_params=params(collective_id=0, has_side_effects=True),
        name="both_steps",
    )(index, count, phase, derivs, time, masses)


def collect(step, count, order_ref, all_ref, sorted_ref):
    def one_block(n, _):
        group = order_ref[step, pl.ds(pl.multiple_of((n >> 3) * 8, 8), 8), :]
        mask = lax.broadcasted_iota(I32, (8, 256), 0) == (n & 7)
        digits = jnp.sum(jnp.where(mask, group, 0.0), axis=0, keepdims=True)
        high = spread(digits[:, 0:128]).astype(I32) - 1
        low = spread(digits[:, 128:256]).astype(I32)
        upper = jnp.zeros((8, 128), F32)
        lower = jnp.zeros((8, 128), F32)
        shifted = high - (lax.broadcasted_iota(I32, (8, 128), 0) >> 2)
        for b in range(64):
            r, half, k = b // 4, (b % 4) // 2, b % 2
            upper = jnp.where(high == b, lane_pick(all_ref[half, r, :, k * 128 : k * 128 + 128], low), upper)
            if k == 0:
                lower = jnp.where(shifted == b, lane_pick(all_ref[half, r, :, 256:384], low), lower)
        blank = jnp.zeros((2, 128), F32)
        rest = lower[0:4] + lower[4:8]
        sorted_ref[step, n, 0:8, :] = upper
        sorted_ref[step, n, 8:16, :] = jnp.concatenate([upper[6:8], rest, blank], axis=0)
        return 0

    lax.fori_loop(0, (count + 127) // 128, one_block, 0)


def last_kernel(
    base_ref, near_ref, order_ref, all0_ref, all1_ref, phase_ref, derivs_ref, time_ref,
    phase_out, derivs_out, time_out, sorted_ref,
):
    collect(0, base_ref[0, 1, 0, 127], order_ref, all0_ref, sorted_ref)
    collect(1, base_ref[1, 1, 0, 127], order_ref, all1_ref, sorted_ref)

    lane = lax.broadcasted_iota(I32, (8, 128), 1)
    run = 16

    def put(g, _, wide):
        for u in range(run):
            b = g * run + u
            lanes = pl.ds(pl.multiple_of(b * 128, 128), 128)
            blank = jnp.zeros((2, 128), F32)
            phase = jnp.concatenate([phase_ref[:, lanes], blank], axis=0)
            derivs = jnp.concatenate([derivs_ref[:, lanes], blank], axis=0)
            time = time_ref[:, lanes]
            for step in range(2):
                base = base_ref[step, 0, 0, b]
                n, shift = base >> 1, (base & 1) * 64
                at = spread(near_ref[step, pl.ds(b, 1), :]) - 1
                low = (at + shift) & 127
                behind = lane >= shift

                def chosen(rows, was):
                    here, then = sorted_ref[step, n, rows, :], sorted_ref[step, n + 1, rows, :]
                    new = jnp.where(at >= 0, lane_pick(jnp.where(behind, here, then), low), was)
                    if wide:
                        last = sorted_ref[step, n + 2, rows, :]
                        new = jnp.where(at >= 128, lane_pick(jnp.where(behind, then, last), low), new)
                    return new

                phase = chosen(slice(0, 8), phase)
                derivs = chosen(slice(8, 16), derivs)
                time = jnp.where(at[0:1] >= 0, block_times[step], time)
            phase_out[:, lanes] = phase[0:6]
            derivs_out[:, lanes] = derivs[0:6]
            time_out[:, lanes] = time
        return 0

    wide = (base_ref[0, 1, 1, 0] > 128) | (base_ref[1, 1, 1, 0] > 128)

    @pl.when(wide)
    def _():
        lax.fori_loop(0, BLOCKS // run, functools.partial(put, wide=True), 0)

    @pl.when(jnp.logical_not(wide))
    def _():
        lax.fori_loop(0, BLOCKS // run, functools.partial(put, wide=False), 0)


def last_update(base, near, order, all0, all1, phase, derivs, time):
    return pl.pallas_call(
        last_kernel,
        out_shape=[
            jax.ShapeDtypeStruct((6, LOCAL), F32),
            jax.ShapeDtypeStruct((6, LOCAL), F32),
            jax.ShapeDtypeStruct((1, LOCAL), F32),
        ],
        in_specs=[pl.BlockSpec(memory_space=pltpu.SMEM)] + in_vmem(7),
        out_specs=in_vmem(3),
        scratch_shapes=[pltpu.VMEM((2, 68, 16, 128), F32)],
        compiler_params=params(),
        name="last_update",
    )(base, near, order, all0, all1, phase, derivs, time)


def body(phase_space, derivs, star_time, masses, active_index, active_count):
    time = star_time.reshape(1, LOCAL)
    masses = masses.reshape(1, LOCAL)
    all0, all1, near, base, order = both_steps(
        active_index, active_count.reshape(1, 2), phase_space, derivs, time, masses
    )
    phase_space, derivs, time = last_update(base, near, order, all0, all1, phase_space, derivs, time)
    return phase_space, derivs, time.reshape(LOCAL)


def solution(mesh):
    return jax.shard_map(
        body,
        mesh=mesh,
        in_specs=(
            P(None, "col"),
            P(None, "col"),
            P("col"),
            P("col"),
            P(None, "row", None),
            P(None, "row"),
        ),
        out_specs=(P(None, "col"), P(None, "col"), P("col")),
        check_vma=False,
    )
```

```python
import functools

import jax
import jax.numpy as jnp
from jax import lax
from jax.experimental import pallas as pl
from jax.experimental.pallas import tpu as pltpu
from jax.sharding import PartitionSpec as P

F32 = jnp.float32
BF16 = jnp.bfloat16
I32 = jnp.int32
FINE8 = jnp.float8_e4m3fn
WIDE8 = jnp.float8_e5m2
DIST_SCALE = 2.0**-4
BOTH_SCALE = 2.0**-10
WEIGHT_BACK = 2.0**-6
softening = 0.01
block_times = (0.125, 0.25)
ROWS = 16
COLS = 8
CAP = 1024
PART = 512
HALF = 256
LOCAL = 16384
BLOCKS = LOCAL // 128
N_STARS = ROWS * PART * 16
MESH = pl.DeviceIdType.MESH
ADDED = (((1,), (1,)), ((), ()))


def rows_of(first, last, width):
    return jnp.zeros((last - first, width), F32)


def in_vmem(n):
    return [pl.BlockSpec(memory_space=pltpu.VMEM)] * n


def params(**more):
    return pltpu.CompilerParams(vmem_limit_bytes=56 * 2**20, **more)


def partners_of(axis, size, place):
    return [(k, {axis: lax.rem(place + k, size)}) for k in range(1, size)]


def exchange(axis, size, place, source, landing, send_sem, recv_sem):
    for k, partner in partners_of(axis, size, place):
        pltpu.make_async_remote_copy(
            src_ref=source,
            dst_ref=landing.at[place],
            send_sem=send_sem.at[k],
            recv_sem=recv_sem.at[place],
            device_id=partner,
            device_id_type=MESH,
        ).start()
    landing[pl.ds(place, 1)] = source[...][None]


def sent(axis, size, place, source, landing, send_sem, recv_sem):
    for k, partner in partners_of(axis, size, place):
        pltpu.make_async_remote_copy(
            src_ref=source,
            dst_ref=landing.at[place],
            send_sem=send_sem.at[k],
            recv_sem=recv_sem.at[place],
            device_id=partner,
            device_id_type=MESH,
        ).wait_send()


def arrived(axis, size, place, source, landing, send_sem, recv_sem):
    for k, partner in partners_of(axis, size, place):
        slot = lax.rem(place + k, size)
        pltpu.make_async_remote_copy(
            src_ref=source,
            dst_ref=landing.at[slot],
            send_sem=send_sem.at[k],
            recv_sem=recv_sem.at[slot],
            device_id=partner,
            device_id_type=MESH,
        ).wait_recv()


def lane_pick(table, lanes):
    return jnp.take_along_axis(table, lanes, axis=1, mode="promise_in_bounds")


def spread(row):
    return jnp.broadcast_to(row, (8, 128))


def hot(index_row, count):
    kinds = lax.broadcasted_iota(I32, (count, 128), 0).astype(F32).astype(BF16)
    return jnp.broadcast_to(index_row, (count, 128)).astype(BF16) == kinds


def scattered(entries, high_count):
    one, zero = jnp.ones((), BF16), jnp.zeros((), BF16)
    left, right = [], []
    for high, low, first, second in entries:
        left.append(jnp.where(hot(high, high_count), one, zero))
        at_low = hot(low, 128)
        a = jnp.broadcast_to(first, (128, 128)).astype(BF16)
        b = jnp.broadcast_to(second, (128, 128)).astype(BF16)
        right.append(jnp.concatenate([jnp.where(at_low, a, zero), jnp.where(at_low, b, zero)], axis=0))
    return lax.dot_general(
        jnp.concatenate(left, axis=1), jnp.concatenate(right, axis=1), ADDED, preferred_element_type=F32
    )


def place_map(lists_ref, step, offset):
    slot = lax.broadcasted_iota(I32, (8, 128), 0) * 128 + lax.broadcasted_iota(I32, (8, 128), 1)
    begin = jnp.zeros((8, 128), I32)
    entries = []
    for r in range(ROWS):
        count = spread(lists_ref[r, 16 + step : 17 + step, :])
        star = lists_ref[r, 8 * step : 8 * step + 8, :] - offset
        live = (slot < count) & (star >= 0) & (star < LOCAL)
        at = begin + slot
        high = jnp.where(live, star >> 7, 255).astype(F32)
        low = (star & 127).astype(F32)
        first, second = ((at >> 7) + 1).astype(F32), (at & 127).astype(F32)
        for k in range(8):
            cut = slice(k, k + 1)
            entries.append((high[cut], low[cut], first[cut], second[cut]))
        begin = begin + count
    return scattered(entries, 128)


def rank_map(places, near_ref, base_ref, order_ref, step):
    at_high, at_low = places[0], places[1]
    row = lax.broadcasted_iota(I32, (128, 128), 0)
    lane = lax.broadcasted_iota(I32, (128, 128), 1)
    up_to = (row <= lane).astype(F32).astype(BF16)
    before = (row < lane).astype(F32).astype(BF16)
    below = (lane < row).astype(F32).astype(BF16)
    active = (at_high > 0.0).astype(F32)
    active16 = active.astype(BF16)
    so_far = jnp.dot(active16, up_to, preferred_element_type=F32)
    total = jnp.broadcast_to(so_far[:, 127:128], (128, 128))
    first = jnp.dot(below, total.astype(BF16), preferred_element_type=F32)
    rank = (first + so_far - active).astype(I32)
    near = jnp.where(active > 0.0, rank - (first.astype(I32) >> 6) * 64 + 1, 0)
    near_ref[step] = near
    widest = jnp.max(jnp.max(near.astype(F32), axis=0, keepdims=True), axis=1, keepdims=True)
    ones = jnp.ones((8, 128), F32).astype(BF16)
    totals = lax.dot_general(ones, active16, ADDED, preferred_element_type=F32)
    firsts = jnp.dot(totals.astype(BF16), before, preferred_element_type=F32).astype(I32)
    base_ref[step, 0] = firsts >> 6
    ends = firsts + totals.astype(I32)
    sub = lax.broadcasted_iota(I32, (8, 128), 0)
    base_ref[step, 1] = jnp.where(sub == 0, ends, jnp.broadcast_to(widest, (8, 128)).astype(I32))
    rank_high = jnp.where(active > 0.0, rank >> 7, 255).astype(F32)
    rank_low = (rank & 127).astype(F32)
    entries = []
    for b in range(BLOCKS):
        cut = slice(b, b + 1)
        entries.append((rank_high[cut], rank_low[cut], at_high[cut], at_low[cut]))
    order_ref[step] = scattered(entries, 64)


def own_stars(lists_ref, place):
    lane = lax.broadcasted_iota(I32, (8, 128), 1)
    sub = lax.broadcasted_iota(I32, (8, 128), 0)
    position = place * PART + (sub & 3) * 128 + lane
    before = jnp.zeros((8, 128), I32)
    which = jnp.zeros((8, 128), I32)
    start = jnp.zeros((8, 128), I32)
    for r in range(ROWS):
        count = jnp.where(sub < 4, spread(lists_ref[r, 16:17, :]), spread(lists_ref[r, 17:18, :]))
        end = before + count
        passed = position >= end
        which = which + passed.astype(I32)
        start = jnp.where(passed, end, start)
        before = end
    flat = which * CAP + position - start
    high, low = flat >> 7, flat & 127
    stars = jnp.zeros((8, 128), I32)
    for r in range(ROWS):
        for k in range(8):
            row = jnp.where(
                sub < 4, spread(lists_ref[r, k : k + 1, :]), spread(lists_ref[r, 8 + k : 9 + k, :])
            )
            stars = jnp.where(high == r * 8 + k, lane_pick(row, low), stars)
    return stars


def both_halves(x, step):
    part = x[4 * step : 4 * step + 4]
    return jnp.concatenate([part, part], axis=0)


def fetch(stars, pairs):
    high, low = stars >> 7, stars & 127

    def look(g, found):
        for u in range(16):
            b = g * 16 + u
            here = high == b
            found = tuple(
                jnp.where(here, lane_pick(pair(b), low), old) for pair, old in zip(pairs, found)
            )
        return found

    return lax.fori_loop(0, BLOCKS // 16, look, tuple(jnp.zeros((8, 128), F32) for _ in pairs))


def two_rows(sub, a, b):
    return jnp.where(sub < 4, spread(a), spread(b))


def unpack(pairs, out_ref):
    for p, pair in enumerate(pairs):
        for half in range(2):
            for s in range(4):
                out_ref[2 * p + half : 2 * p + half + 1, s * 128 : s * 128 + 128] = pair[
                    4 * half + s : 4 * half + s + 1
                ]


def predict(phase, derivs, time, now):
    d = now - time
    x, v, a, j = phase[0:3], phase[3:6], derivs[0:3], derivs[3:6]
    return x + d * (v + d * (a / 2.0 + d * j / 6.0)), v + d * (a + d * j / 2.0)


def correct(x, v, old_acc, old_jerk, h, forces):
    new_acc, new_jerk = forces[0:3], forces[3:6]
    change = old_acc - new_acc
    second = (-6.0 * change - h * (4.0 * old_jerk + 2.0 * new_jerk)) / (h * h)
    third = (12.0 * change + 6.0 * h * (old_jerk + new_jerk)) / (h * h * h)
    h2 = h * h
    h3 = h2 * h
    h4 = h3 * h
    h5 = h4 * h
    x = x + h4 / 24.0 * second + h5 / 120.0 * third
    v = v + h3 / 6.0 * second + h4 / 24.0 * third
    return x, v, new_acc, new_jerk


PAIRS = ((0, 0), (0, 1), (0, 2), (1, 0), (1, 1), (2, 0))


def split3(x):
    high = x.astype(BF16).astype(F32)
    rest = x - high
    middle = rest.astype(BF16).astype(F32)
    return high, middle, rest - middle


def split2(x, low_kind):
    high = x.astype(BF16)
    return high, (x - high.astype(F32)).astype(low_kind)


def split8(x):
    parts = []
    for _ in range(4):
        parts.append(x.astype(FINE8).astype(F32))
        x = x - parts[-1]
    return parts


def squares(x, v):
    xx = x * x
    xv = x * v
    return xx[0:1] + xx[1:2] + xx[2:3], xv[0:1] + xv[1:2] + xv[2:3]


def star_features(x, v):
    width = x.shape[1]
    parts = split3(jnp.concatenate([x, v, jnp.zeros((2, width), F32)], axis=0))
    xx, xv = squares(x, v)
    one = jnp.ones((3, width), F32)
    extra = jnp.concatenate(list(split3(xx)) + list(split3(xv)) + [one, one, rows_of(12, 16, width)], axis=0)
    return jnp.concatenate([parts[a] for a, _ in PAIRS] + [extra], axis=0)


def active_features(x, v):
    width = x.shape[1]
    xp, vp = split3(x), split3(v)
    xx, xv = squares(x, v)
    one, none3, none5 = jnp.ones((3, width), F32), rows_of(0, 3, width), rows_of(0, 5, width)
    dist, both = [], []
    for _, b in PAIRS:
        dist += [-2.0 * xp[b], none5]
        both += [-vp[b], -xp[b], rows_of(0, 2, width)]
    dist += [one, none3] + list(split3(xx + softening)) + [none3, rows_of(12, 16, width)]
    both += [none3, one, none3] + list(split3(xv)) + [rows_of(12, 16, width)]
    dist = jnp.concatenate(dist, axis=0) * DIST_SCALE
    both = jnp.concatenate(both, axis=0) * BOTH_SCALE
    return dist.astype(BF16), both.astype(BF16)


def prepare(first, chunk, count, pred_of, weights, weights8, features):
    def one_chunk(n, _):
        x, v, mass = pred_of(n)
        at = pl.ds(pl.multiple_of(first + n * chunk, chunk), chunk)
        ones, none = jnp.ones((1, chunk), F32), jnp.zeros((1, chunk), F32)
        scaled = jnp.concatenate([x, v, ones, none], axis=0) * mass
        share = scaled / N_STARS
        high = share.astype(BF16).astype(F32)
        weights[:, at] = jnp.concatenate([high, share - high], axis=0).astype(BF16)
        weights8[:, at] = jnp.concatenate(split8(jnp.clip(scaled, -240.0, 240.0)), axis=0).astype(FINE8)
        features[at, :] = star_features(x, v).T.astype(BF16)
        return 0

    lax.fori_loop(0, count, one_chunk, 0, unroll=count <= 4)


def force_sums(deep, weights, weights8, features, dist_own, both_own, totals, own, part, after):
    def quarter(t, _):
        h = t >> 1
        cut = pl.ds(pl.multiple_of(h * HALF, HALF), HALF)
        fresh = (t & 1) == 0

        def sums(n, total):
            lanes = pl.ds(pl.multiple_of(((t & 1) * 2 + n) * deep, deep), deep)
            factor = features[lanes, :]
            dist = jnp.dot(factor, dist_own[:, cut], preferred_element_type=F32)
            both = jnp.dot(factor, both_own[:, cut], preferred_element_type=F32)
            inverse = lax.rsqrt(jnp.maximum(dist, softening * DIST_SCALE))
            inverse_sq = inverse * inverse
            weight = inverse * inverse_sq
            radial = (weight * inverse_sq) * both
            w_high, w_low = split2(weight, FINE8)
            u_high, u_low = split2(radial, WIDE8)
            dot = functools.partial(jnp.dot, preferred_element_type=F32)
            left, left8 = weights[:, lanes], weights8[:, lanes]
            new = dot(left, w_high), dot(left, u_high), dot(left8, w_low), dot(left8, u_low)
            return tuple(a + b for a, b in zip(total, new))

        found = lax.fori_loop(0, 2, sums, tuple(jnp.where(fresh, 0.0, held[...]) for held in totals))
        for n in range(4):
            totals[n][...] = found[n]

        @pl.when((t & 1) == 1)
        def _():
            def whole(high, low, back):
                high = high[0:8] + high[8:16]
                low = low[0:8] + low[8:16] + low[16:24] + low[24:32]
                return (high + low / N_STARS) * back

            w_all = whole(found[0], found[2], WEIGHT_BACK)
            u_all = whole(found[1], found[3], 1.0)
            mine = own[:, cut]
            x, v = mine[0:3], mine[3:6]
            acc = w_all[0:3] - x * w_all[6:7]
            jerk = w_all[3:6] - v * w_all[6:7] - 3.0 * (u_all[0:3] - x * u_all[6:7])
            part[pl.ds(h, 1)] = jnp.concatenate([acc, jerk, jnp.zeros((2, HALF), F32)], axis=0)[None]

        for number, action in after.items():
            pl.when(t == number)(action)
        return 0

    lax.fori_loop(0, 4, quarter, 0)


def sum_of(landing):
    total = landing[0]
    for c in range(1, COLS):
        total = total + landing[c]
    return total


def packed(x, v, a, j):
    rest = jnp.concatenate([a[2:3], j], axis=0)
    right = jnp.concatenate([rest[:, 0:128], rest[:, 128:256]], axis=0)
    return jnp.concatenate([jnp.concatenate([x, v, a[0:2]], axis=0), right], axis=1)


def take_moved(high, low, sub, rows_at):
    def look(g, found):
        for u in range(16):
            r, k = g * 4 + u // 4, u % 4
            here = high == r * 4 + k
            found = tuple(
                jnp.where(here, lane_pick(two_rows(sub, *pair), low), was)
                for pair, was in zip(rows_at(r, k), found)
            )
        return found

    return lax.fori_loop(0, ROWS // 4, look, tuple(jnp.zeros((8, 128), F32) for _ in range(3)))


def steps_kernel(
    index_ref, count_ref, phase_far, derivs_far, time_far, mass_far,
    all0_ref, all1_ref, near_ref, base_ref, order_ref,
    phase_ref, derivs_ref, time_ref, mass_ref, lists_own, lists_ref, places,
    pred, lead0, land_lead, picks0, picks1, land0, land1, part0, part1, landf0, landf1, lead, lead_all, mine0, mine1,
    old, fix, own, accel, weights, weights8, features, dist_own, both_own, w_high, u_high, w_low, u_low,
    s_in, s_list, r_list, s_lead0, r_lead0, s_pick0, r_pick0, s_pick1, r_pick1, s_for, r_for, s_lead, r_lead, s_all, r_all,
):
    row, col = lax.axis_index("row"), lax.axis_index("col")
    barrier = pltpu.get_barrier_semaphore()
    everyone = partners_of("row", ROWS, row) + partners_of("col", COLS, col)
    for _, partner in everyone:
        pl.semaphore_signal(barrier, inc=1, device_id=partner, device_id_type=MESH)
    inputs = [
        pltpu.make_async_copy(far, near, s_in.at[n])
        for n, (far, near) in enumerate(
            [(phase_far, phase_ref), (derivs_far, derivs_ref), (time_far, time_ref), (mass_far, mass_ref)]
        )
    ]
    for copy in inputs:
        copy.start()
    offset = col * LOCAL
    chunk = 2048
    sub = lax.broadcasted_iota(I32, (8, 128), 0)
    for step in range(2):
        for k in range(8):
            lists_own[8 * step + k : 8 * step + k + 1, :] = index_ref[step, 0:1, k * 128 : k * 128 + 128]
        lists_own[16 + step : 17 + step, :] = jnp.broadcast_to(count_ref[0:1, step : step + 1], (1, 128))
    lists_own[18:24, :] = jnp.zeros((6, 128), I32)
    pl.semaphore_wait(barrier, len(everyone))
    lists = ("row", ROWS, row, lists_own, lists_ref, s_list, r_list)
    exchange(*lists)
    for copy in inputs:
        copy.wait()

    def first_stars(n):
        lanes = pl.ds(pl.multiple_of(n * chunk, chunk), chunk)
        x, v = predict(phase_ref[:, lanes], derivs_ref[:, lanes], time_ref[:, lanes], block_times[0])
        pred[:, lanes] = jnp.concatenate([x, v], axis=0)
        return x, v, mass_ref[:, lanes]

    prepare(0, chunk, LOCAL // chunk, first_stars, weights, weights8, features)
    arrived(*lists)

    def block(b):
        return pl.ds(pl.multiple_of(b * 128, 128), 128)

    def row_pairs(ref):
        return [
            lambda b, c=c: two_rows(sub, ref[c : c + 1, block(b)], ref[c + 1 : c + 2, block(b)])
            for c in (0, 2, 4)
        ]

    rest_pairs = row_pairs(derivs_ref) + [lambda b: two_rows(sub, time_ref[:, block(b)], mass_ref[:, block(b)])]
    local = own_stars(lists_ref, row) - offset
    for p, value in enumerate(fetch(both_halves(local, 0), row_pairs(pred))):
        lead0[p] = value
    lead_picks = ("col", COLS, col, lead0, land_lead, s_lead0, r_lead0)
    exchange(*lead_picks)
    for p, value in enumerate(fetch(both_halves(local, 0), rest_pairs)):
        picks0[p] = value
    first_picks = ("col", COLS, col, picks0, land0, s_pick0, r_pick0)
    exchange(*first_picks)

    found = place_map(lists_ref, 0, offset)
    places[0, 0], places[0, 1] = found[:, 0:128], found[:, 128:256]

    arrived(*lead_picks)
    total = sum_of(land_lead)
    unpack([total[p] for p in range(3)], fix)
    def force_copies(step, half):
        part, landing = (part0, landf0) if step == 0 else (part1, landf1)
        n = 2 * step + half
        return ("col", COLS, col, part.at[half], landing.at[half], s_for.at[n], r_for.at[n])

    def lead_copies(half):
        return ("row", ROWS, row, lead.at[half], lead_all.at[half], s_lead.at[half], r_lead.at[half])

    def row_copies(step, half):
        mine, landing = (mine0, all0_ref) if step == 0 else (mine1, all1_ref)
        n = 2 * step + half
        return ("row", ROWS, row, mine.at[half], landing.at[half], s_all.at[n], r_all.at[n])

    def set_own(x, v):
        own[...] = jnp.concatenate([x, v, jnp.zeros((2, PART), F32)], axis=0)
        dist_own[...], both_own[...] = active_features(x, v)

    sums = (weights, weights8, features, dist_own, both_own, (w_high, u_high, w_low, u_low), own)
    set_own(fix[0:3], fix[3:6])

    def first_old():
        exchange(*force_copies(0, 0))
        arrived(*first_picks)
        total = sum_of(land0)
        unpack([total[p] for p in range(4)], accel)

    def first_corrected(half):
        arrived(*force_copies(0, half))
        cut = slice(half * HALF, half * HALF + HALF)
        x, v, a, j = correct(
            own[0:3, cut], own[3:6, cut], accel[0:3, cut], accel[3:6, cut],
            block_times[0] - accel[6:7, cut], sum_of(landf0.at[half]),
        )
        x_next, v_next = predict(
            jnp.concatenate([x, v], axis=0), jnp.concatenate([a, j], axis=0), block_times[0], block_times[1]
        )
        lead[half] = jnp.concatenate([x_next, v_next, accel[7:8, cut], jnp.zeros((1, HALF), F32)], axis=0)
        exchange(*lead_copies(half))
        mine0[half] = packed(x, v, a, j)
        exchange(*row_copies(0, half))

    force_sums(
        4096, *sums, part0,
        {1: first_old, 2: lambda: first_corrected(0)},
    )
    exchange(*force_copies(0, 1))
    pairs = row_pairs(phase_ref) + rest_pairs
    pairs.append(lambda b: two_rows(sub, places[0, 0, pl.ds(b, 1), :], places[0, 1, pl.ds(b, 1), :]))
    for p, value in enumerate(fetch(both_halves(local, 1), pairs)):
        picks1[p] = value
    second_picks = ("col", COLS, col, picks1, land1, s_pick1, r_pick1)
    exchange(*second_picks)
    first_corrected(1)

    def second_stars(n):
        lanes = pl.ds(pl.multiple_of(n * chunk, chunk), chunk)
        x, v = predict(phase_ref[:, lanes], derivs_ref[:, lanes], time_ref[:, lanes], block_times[1])
        moved = jnp.concatenate([places[0, 0, pl.ds(n * 16 + k, 1), :] for k in range(16)], axis=1)
        return x, v, jnp.where(moved > 0.0, 0.0, mass_ref[:, lanes])

    prepare(0, chunk, LOCAL // chunk, second_stars, weights, weights8, features)
    rank_map(places[0], near_ref, base_ref, order_ref, 0)
    arrived(*second_picks)
    total = sum_of(land1)
    unpack([total[p] for p in range(8)], old)
    high = both_halves(total[7], 0).astype(I32) - 1
    low = both_halves(total[7], 1).astype(I32)
    for half in range(2):
        arrived(*lead_copies(half))

    def moved_stars(n):
        state = lead_all[pl.ds(n & 1, 1), pl.ds(2 * col + (n >> 1), 1)][0, 0]
        return state[0:3], state[3:6], state[6:7]

    prepare(LOCAL, HALF, 4, moved_stars, weights, weights8, features)

    def lead_rows(r, k):
        cut = slice((k % 2) * 128, (k % 2) * 128 + 128)
        return [(lead_all[k // 2, r, c : c + 1, cut], lead_all[k // 2, r, c + 1 : c + 2, cut]) for c in (0, 2, 4)]

    unpack(take_moved(high, low, sub, lead_rows), fix)
    moved = old[14:15] > 0.0
    x_own, v_own = predict(old[0:6], old[6:12], old[12:13], block_times[1])
    set_own(jnp.where(moved, fix[0:3], x_own), jnp.where(moved, fix[3:6], v_own))

    def rest_rows(r, k):
        half, at = k // 2, 4 * (k % 2)
        cut = slice((k % 2) * 128, (k % 2) * 128 + 128)
        return [
            (all0_ref[half, r, 6:7, cut], all0_ref[half, r, 7:8, cut]),
            (all0_ref[half, r, at : at + 1, 256:384], all0_ref[half, r, at + 1 : at + 2, 256:384]),
            (all0_ref[half, r, at + 2 : at + 3, 256:384], all0_ref[half, r, at + 3 : at + 4, 256:384]),
        ]

    def second_old():
        exchange(*force_copies(1, 0))
        for half in range(2):
            arrived(*row_copies(0, half))
        unpack(take_moved(high, low, sub, rest_rows), fix)
        moved = old[14:15] > 0.0
        h = block_times[1] - jnp.where(moved, block_times[0], old[12:13])
        accel[...] = jnp.concatenate(
            [jnp.where(moved, fix[0:3], old[6:9]), jnp.where(moved, fix[3:6], old[9:12]), h, h], axis=0
        )

    def second_corrected(half):
        arrived(*force_copies(1, half))
        cut = slice(half * HALF, half * HALF + HALF)
        mine1[half] = packed(
            *correct(
                own[0:3, cut], own[3:6, cut], accel[0:3, cut], accel[3:6, cut], accel[6:7, cut],
                sum_of(landf1.at[half]),
            )
        )
        exchange(*row_copies(1, half))

    force_sums(
        (LOCAL + 2 * PART) // 4, *sums, part1, {1: second_old, 2: lambda: second_corrected(0)}
    )
    exchange(*force_copies(1, 1))
    found = place_map(lists_ref, 1, offset)
    places[1, 0], places[1, 1] = found[:, 0:128], found[:, 128:256]
    second_corrected(1)
    rank_map(places[1], near_ref, base_ref, order_ref, 1)
    for half in range(2):
        arrived(*row_copies(1, half))
    for copies in [lists, lead_picks, first_picks, second_picks]:
        sent(*copies)
    for half in range(2):
        sent(*lead_copies(half))
        for step in range(2):
            sent(*force_copies(step, half))
            sent(*row_copies(step, half))


def both_steps(index, count, phase, derivs, time, masses):
    stars = LOCAL + 2 * PART
    vmem = [
        ((6, LOCAL), F32),
        ((6, LOCAL), F32),
        ((1, LOCAL), F32),
        ((1, LOCAL), F32),
        ((24, 128), I32),
        ((ROWS, 24, 128), I32),
        ((2, 2, 128, 128), F32),
        ((6, LOCAL), F32),
        ((3, 8, 128), F32),
        ((COLS, 3, 8, 128), F32),
        ((4, 8, 128), F32),
        ((8, 8, 128), F32),
        ((COLS, 4, 8, 128), F32),
        ((COLS, 8, 8, 128), F32),
        ((2, 8, HALF), F32),
        ((2, 8, HALF), F32),
        ((2, COLS, 8, HALF), F32),
        ((2, COLS, 8, HALF), F32),
        ((2, 8, HALF), F32),
        ((2, ROWS, 8, HALF), F32),
        ((2, 8, 384), F32),
        ((2, 8, 384), F32),
        ((16, PART), F32),
        ((8, PART), F32),
        ((8, PART), F32),
        ((8, PART), F32),
        ((16, stars), BF16),
        ((32, stars), FINE8),
        ((stars, 64), BF16),
        ((64, PART), BF16),
        ((64, PART), BF16),
        ((16, HALF), F32),
        ((16, HALF), F32),
        ((32, HALF), F32),
        ((32, HALF), F32),
    ]
    sems = [(4,)] + [(ROWS,)] * 2 + [(COLS,)] * 6 + [(4, COLS)] * 2 + [(2, ROWS)] * 2 + [(4, ROWS)] * 2
    return pl.pallas_call(
        steps_kernel,
        out_shape=[
            jax.ShapeDtypeStruct((2, ROWS, 8, 384), F32),
            jax.ShapeDtypeStruct((2, ROWS, 8, 384), F32),
            jax.ShapeDtypeStruct((2, 128, 128), I32),
            jax.ShapeDtypeStruct((2, 2, 8, 128), I32),
            jax.ShapeDtypeStruct((2, 64, 256), F32),
        ],
        in_specs=in_vmem(2) + [pl.BlockSpec(memory_space=pl.ANY)] * 4,
        out_specs=in_vmem(5),
        scratch_shapes=[pltpu.VMEM(shape, kind) for shape, kind in vmem]
        + [pltpu.SemaphoreType.DMA(shape) for shape in sems],
        compiler_params=params(collective_id=0, has_side_effects=True),
        name="both_steps",
    )(index, count, phase, derivs, time, masses)


def collect(step, count, order_ref, all_ref, sorted_ref):
    def one_block(n, _):
        group = order_ref[step, pl.ds(pl.multiple_of((n >> 3) * 8, 8), 8), :]
        mask = lax.broadcasted_iota(I32, (8, 256), 0) == (n & 7)
        digits = jnp.sum(jnp.where(mask, group, 0.0), axis=0, keepdims=True)
        high = spread(digits[:, 0:128]).astype(I32) - 1
        low = spread(digits[:, 128:256]).astype(I32)
        upper = jnp.zeros((8, 128), F32)
        lower = jnp.zeros((8, 128), F32)
        shifted = high - (lax.broadcasted_iota(I32, (8, 128), 0) >> 2)
        for b in range(64):
            r, half, k = b // 4, (b % 4) // 2, b % 2
            upper = jnp.where(high == b, lane_pick(all_ref[half, r, :, k * 128 : k * 128 + 128], low), upper)
            if k == 0:
                lower = jnp.where(shifted == b, lane_pick(all_ref[half, r, :, 256:384], low), lower)
        blank = jnp.zeros((2, 128), F32)
        rest = lower[0:4] + lower[4:8]
        sorted_ref[step, n, 0:8, :] = upper
        sorted_ref[step, n, 8:16, :] = jnp.concatenate([upper[6:8], rest, blank], axis=0)
        return 0

    def two_blocks(n, _):
        one_block(2 * n, 0)
        return one_block(2 * n + 1, 0)

    lax.fori_loop(0, (count + 255) // 256, two_blocks, 0)


def last_kernel(
    base_ref, near_ref, order_ref, all0_ref, all1_ref, phase_ref, derivs_ref, time_ref,
    phase_out, derivs_out, time_out, sorted_ref,
):
    collect(0, base_ref[0, 1, 0, 127], order_ref, all0_ref, sorted_ref)
    collect(1, base_ref[1, 1, 0, 127], order_ref, all1_ref, sorted_ref)

    lane = lax.broadcasted_iota(I32, (8, 128), 1)
    run = 32

    def put(g, _, wide):
        for u in range(run):
            b = g * run + u
            lanes = pl.ds(pl.multiple_of(b * 128, 128), 128)
            blank = jnp.zeros((2, 128), F32)
            phase = jnp.concatenate([phase_ref[:, lanes], blank], axis=0)
            derivs = jnp.concatenate([derivs_ref[:, lanes], blank], axis=0)
            time = time_ref[:, lanes]
            for step in range(2):
                base = base_ref[step, 0, 0, b]
                n, shift = base >> 1, (base & 1) * 64
                at = spread(near_ref[step, pl.ds(b, 1), :]) - 1
                low = (at + shift) & 127
                behind = lane >= shift

                def chosen(rows, was):
                    here, then = sorted_ref[step, n, rows, :], sorted_ref[step, n + 1, rows, :]
                    new = jnp.where(at >= 0, lane_pick(jnp.where(behind, here, then), low), was)
                    if wide:
                        last = sorted_ref[step, n + 2, rows, :]
                        new = jnp.where(at >= 128, lane_pick(jnp.where(behind, then, last), low), new)
                    return new

                phase = chosen(slice(0, 8), phase)
                derivs = chosen(slice(8, 16), derivs)
                time = jnp.where(at[0:1] >= 0, block_times[step], time)
            phase_out[:, lanes] = phase[0:6]
            derivs_out[:, lanes] = derivs[0:6]
            time_out[:, lanes] = time
        return 0

    wide = (base_ref[0, 1, 1, 0] > 128) | (base_ref[1, 1, 1, 0] > 128)

    @pl.when(wide)
    def _():
        lax.fori_loop(0, BLOCKS // run, functools.partial(put, wide=True), 0)

    @pl.when(jnp.logical_not(wide))
    def _():
        lax.fori_loop(0, BLOCKS // run, functools.partial(put, wide=False), 0)


def last_update(base, near, order, all0, all1, phase, derivs, time):
    return pl.pallas_call(
        last_kernel,
        out_shape=[
            jax.ShapeDtypeStruct((6, LOCAL), F32),
            jax.ShapeDtypeStruct((6, LOCAL), F32),
            jax.ShapeDtypeStruct((1, LOCAL), F32),
        ],
        in_specs=[pl.BlockSpec(memory_space=pltpu.SMEM)] + in_vmem(7),
        out_specs=in_vmem(3),
        scratch_shapes=[pltpu.VMEM((2, 68, 16, 128), F32)],
        compiler_params=params(),
        name="last_update",
    )(base, near, order, all0, all1, phase, derivs, time)


def body(phase_space, derivs, star_time, masses, active_index, active_count):
    time = star_time.reshape(1, LOCAL)
    masses = masses.reshape(1, LOCAL)
    all0, all1, near, base, order = both_steps(
        active_index, active_count.reshape(1, 2), phase_space, derivs, time, masses
    )
    phase_space, derivs, time = last_update(base, near, order, all0, all1, phase_space, derivs, time)
    return phase_space, derivs, time.reshape(LOCAL)


def solution(mesh):
    return jax.shard_map(
        body,
        mesh=mesh,
        in_specs=(
            P(None, "col"),
            P(None, "col"),
            P("col"),
            P("col"),
            P(None, "row", None),
            P(None, "row"),
        ),
        out_specs=(P(None, "col"), P(None, "col"), P("col")),
        check_vma=False,
    )
```
